128 devices in a mesh: replica: 32 (over y, z, core), tensor: 4 (over x).
Axes of the slice: x: 4, y: 4, z: 4, core: 2. Of those that a mesh axis runs over, the one named last changes fastest.
Arguments:
- hidden_in: bfloat16 [4, 1024, 5120], P(None, 'replica'), may hold values from -600 to 600
- norm_gain: float32 [5120], replicated, may hold values from 0.1 to 1.9
- w_query: bfloat16 [5120, 2560], P(None, 'tensor'), may hold values from -0.078125 to 0.078125
- w_key: bfloat16 [5120, 512], P(None, 'tensor'), may hold values from -0.078125 to 0.078125
- w_value: bfloat16 [5120, 512], P(None, 'tensor'), may hold values from -0.078125 to 0.078125
- w_out: bfloat16 [2560, 5120], P('tensor'), may hold values from -0.25 to 0.25
- kv_pages: bfloat16 [4096, 2, 128, 512], P('replica', None, None, 'tensor'), may hold values from -210 to 210
- lengths: int32 [1024], P('replica'), may hold values from 1 to 512, as said below
- page_table: int32 [1024, 4], P('replica'), may hold values from 0 to 127, as said below
- destination: int32 [1024], P('replica'), may hold values from 0 to 31, as said below
Outputs:
- attended: bfloat16 [4, 1024, 5120], P(None, 'replica')
The draws below stay inside these ranges and needn't reach their ends.
Inputs may be any that keep to these rules, and one draw needn't show every extreme that they name: `lengths`: some trajectory has exactly 512 cached tokens. `page_table`: the 4 entries of a row are distinct local page numbers of its replica's pool of 128 pages; no two rows of a replica share a page. `destination`: each replica sends exactly one of its rows to each replica (itself included), and each replica receives exactly one row for each slot b % 32.
All inputs are finite; a program needn't handle non-finite values.
Results may differ from the reference program's by a relative error of at most 0.01.
The reference program's roundings to bfloat16 on the way (of `normed`, `queries`, `fresh_values` and `heads`) count: a program that leaves them out, or rounds other values in their place, can miss the bound.
Values may be sent and summed in bfloat16 or wider, within the bound.
A program may use at most 128 MiB of HBM per device.

```python
import math
import jax
import jax.numpy as jnp
from jax import lax

D = 5120
QH = 20
KVH = 4
HD = 128
PAGE = 128
MAXP = 4
STEPS = 4
ROWS_DEV = 32
ROWS = 1024
POOL = 128
N_REPLICA = 32


def draw_hidden_in(key, part):
    key = jax.random.fold_in(key, 11)
    base_key, row_key, column_key = jax.random.split(key, 3)
    shape = (STEPS, ROWS, D)
    base = jnp.clip(jax.random.normal(base_key, shape, jnp.float32), -6.0, 6.0)
    row_scale = jnp.exp(jax.random.uniform(row_key, (STEPS, ROWS, 1), jnp.float32, 0.0, math.log(10.0)))
    column_scale = jnp.exp(jax.random.uniform(column_key, (1, 1, D), jnp.float32, 0.0, math.log(10.0)))
    return (base * row_scale * column_scale).astype(jnp.bfloat16)


def draw_kv_pages(key, part):
    key = jax.random.fold_in(key, 23)
    base_key = jax.random.fold_in(key, 0)
    page_count = N_REPLICA * POOL
    shape = (page_count, 2, PAGE, KVH * HD)
    base = jnp.clip(jax.random.normal(base_key, shape, jnp.float32), -6.0, 6.0)
    return jnp.concatenate([base[:, 0:1] * 2.0, base[:, 1:2]], 1).astype(jnp.bfloat16)


def draw_lengths(key, part):
    key = jax.random.fold_in(key, 31)
    load_key, length_key, peak_key = jax.random.split(key, 3)
    load = jax.random.randint(load_key, (N_REPLICA, 1), 1, MAXP + 1)
    raw = jax.random.randint(length_key, (N_REPLICA, ROWS_DEV), 0, 1048576)
    spans = 1 + raw % (load * PAGE)
    flat_spans = spans.reshape(ROWS)
    chosen = jax.random.randint(peak_key, (), 0, ROWS)
    return flat_spans.at[chosen].set(MAXP * PAGE).astype(jnp.int32)


def draw_page_table(key, part):
    key = jax.random.fold_in(key, 41)
    replica_keys = jax.random.split(key, N_REPLICA)
    orders = jax.vmap(lambda each_key: jax.random.permutation(each_key, POOL))(replica_keys)
    return orders.reshape(ROWS, MAXP).astype(jnp.int32)


def draw_destination(key, part):
    key = jax.random.fold_in(key, 53)
    home_key, slot_key = jax.random.split(key, 2)
    home_shift = jax.random.permutation(home_key, N_REPLICA)
    slot_shift = jax.random.permutation(slot_key, N_REPLICA)
    row_ids = jnp.arange(ROWS, dtype=jnp.int32)
    return ((home_shift[row_ids // ROWS_DEV] + slot_shift[row_ids % ROWS_DEV]) % N_REPLICA).astype(jnp.int32)


def shard_levels(stream_key, extent, shards, least, largest):
    gain = 1.0
    for axis_at, blocks in shards:
        draws = jax.random.uniform(jax.random.fold_in(jax.random.fold_in(stream_key, 6), axis_at), (blocks,), jnp.float32, least / len(shards), largest / len(shards))
        gain = gain * jnp.repeat(jnp.exp(draws), extent[axis_at] // blocks).reshape((-1,) + (1,) * (len(extent) - 1 - axis_at))
    return gain


def bell_draw(own_key, extent, spread, most, cuts=(), kind=jnp.bfloat16):
    factor_of = shard_levels(own_key, extent, cuts, -0.22, 0.18) if cuts else 1.0
    values = jax.random.normal(own_key, extent, jnp.float32) * spread * factor_of
    return jnp.minimum(jnp.maximum(values, -most), most).astype(kind)


def setup_inputs(seed: int = 0) -> dict:
    streams_of = jax.random.split(jax.random.key(seed), 11)
    hidden_in = draw_hidden_in(jax.random.fold_in(streams_of[10], 71), 0)
    norm_gain = jnp.clip(1.0 + 0.18 * jax.random.normal(streams_of[1], (D,), jnp.float32), 0.1, 1.9)
    w_query = bell_draw(streams_of[2], (D, QH * HD), D ** -0.5, 0.078125, ((1, 4),))
    w_key = bell_draw(streams_of[3], (D, KVH * HD), D ** -0.5, 0.078125, ((1, 4),))
    w_value = bell_draw(streams_of[4], (D, KVH * HD), D ** -0.5, 0.078125, ((1, 4),))
    w_out = bell_draw(streams_of[5], (QH * HD, D), (QH * HD // 4) ** -0.5, 0.25, ((0, 4),))
    kv_pages = draw_kv_pages(jax.random.fold_in(streams_of[10], 71), 0)
    lengths = draw_lengths(jax.random.fold_in(streams_of[10], 71), 0)
    page_table = draw_page_table(jax.random.fold_in(streams_of[10], 71), 0)
    destination = draw_destination(jax.random.fold_in(streams_of[10], 71), 0)
    return {"hidden_in": hidden_in, "norm_gain": norm_gain, "w_query": w_query, "w_key": w_key, "w_value": w_value, "w_out": w_out, "kv_pages": kv_pages, "lengths": lengths, "page_table": page_table, "destination": destination}


ROPE_BASE = 1000000.0
EPSILON = 1e-06

def rotate(vectors, positions):
    half_dim = vectors.shape[-1] // 2
    inv_freq = ROPE_BASE ** (-(jnp.arange(half_dim, dtype=jnp.float32) * (2.0 / vectors.shape[-1])))
    angles = positions.astype(jnp.float32)[..., None] * inv_freq
    cosine = jnp.cos(angles)
    sine = jnp.sin(angles)
    first_half = vectors[..., :half_dim]
    second_half = vectors[..., half_dim:]
    return jnp.concatenate([first_half * cosine - second_half * sine, second_half * cosine + first_half * sine], -1)

def softmax_part(scores, inside):
    scores = jnp.where(inside, scores, -jnp.inf)
    peak = lax.optimization_barrier(jnp.max(scores, -1))
    weights = jnp.exp(scores - peak[..., None]).astype(jnp.bfloat16)
    weight_sum = lax.optimization_barrier(jnp.sum(weights.astype(jnp.float32), -1))
    return (weights, peak, weight_sum)

def reference(hidden_in, norm_gain, w_query, w_key, w_value, w_out, kv_pages, lengths, page_table, destination):
    group_size = QH // KVH
    row_ids = jnp.arange(ROWS, dtype=jnp.int32)
    new_index = destination * ROWS_DEV + row_ids % ROWS_DEV
    anchor = jnp.zeros((ROWS,), jnp.int32).at[new_index].set(row_ids)
    row_len = lengths[anchor]
    row_pages = (anchor // ROWS_DEV)[:, None] * POOL + page_table[anchor]
    widened = hidden_in.astype(jnp.float32)
    scale = lax.rsqrt(lax.optimization_barrier(jnp.mean(widened * widened, -1, keepdims=True)) + EPSILON)
    normed = (widened * scale * norm_gain).astype(jnp.bfloat16).reshape(STEPS * ROWS, D)
    positions = row_len[None, :, None] + jnp.arange(STEPS, dtype=jnp.int32)[:, None, None]
    queries = rotate(jnp.dot(normed, w_query, preferred_element_type=jnp.float32).reshape(STEPS, ROWS, QH, HD), positions).astype(jnp.bfloat16)
    fresh_keys = rotate(jnp.dot(normed, w_key, preferred_element_type=jnp.float32).reshape(STEPS, ROWS, KVH, HD), positions).astype(jnp.bfloat16)
    fresh_values = jnp.dot(normed, w_value, preferred_element_type=jnp.float32).reshape(STEPS, ROWS, KVH, HD).astype(jnp.bfloat16)
    causal = jnp.arange(STEPS)[:, None] >= jnp.arange(STEPS)[None, :]

    def row_attention(pieces):
        query_row, key_row, value_row, pages, length = pieces
        cache = kv_pages[pages].astype(jnp.float32)
        cache_keys = cache[:, 0].reshape(MAXP * PAGE, KVH, HD)
        cache_values = cache[:, 1].reshape(MAXP * PAGE, KVH, HD)
        grouped = query_row.astype(jnp.float32).reshape(STEPS, KVH, group_size, HD)
        scores = jnp.einsum('sghd,tgd->sght', grouped, cache_keys) / math.sqrt(HD)
        inside = (jnp.arange(MAXP * PAGE) < length)[None, None, None, :]
        weights, peak_c, sum_c = softmax_part(scores, inside)
        out_c = jnp.einsum('sght,tgd->sghd', weights.astype(jnp.float32), cache_values)
        scores = jnp.einsum('sghd,jgd->sghj', grouped, key_row.astype(jnp.float32)) / math.sqrt(HD)
        weights, peak_f, sum_f = softmax_part(scores, causal[:, None, None, :])
        out_f = jnp.einsum('sghj,jgd->sghd', weights.astype(jnp.float32), value_row.astype(jnp.float32))
        highest = jnp.maximum(peak_c, peak_f)
        factor_c = jnp.exp(peak_c - highest)
        factor_f = jnp.exp(peak_f - highest)
        blended = (out_c * factor_c[..., None] + out_f * factor_f[..., None]) / (sum_c * factor_c + sum_f * factor_f)[..., None]
        return blended.reshape(STEPS, QH * HD).astype(jnp.bfloat16)
    heads = lax.map(row_attention, (queries.transpose(1, 0, 2, 3), fresh_keys.transpose(1, 0, 2, 3), fresh_values.transpose(1, 0, 2, 3), row_pages, row_len))
    flat_heads = heads.transpose(1, 0, 2).reshape(STEPS * ROWS, QH * HD)
    return jnp.dot(flat_heads, w_out, preferred_element_type=jnp.float32).astype(jnp.bfloat16).reshape(STEPS, ROWS, D)
```

```python
import math

import jax
import jax.numpy as jnp
from jax import lax
from jax.sharding import PartitionSpec as P

HD = 128


ROPE_BASE = 1000000.0
EPSILON = 1e-06


def rotate(vectors, positions):
    half_dim = vectors.shape[-1] // 2
    inv_freq = ROPE_BASE ** (-(jnp.arange(half_dim, dtype=jnp.float32) * (2.0 / vectors.shape[-1])))
    angles = positions.astype(jnp.float32)[..., None] * inv_freq
    cosine = jnp.cos(angles)
    sine = jnp.sin(angles)
    first_half = vectors[..., :half_dim]
    second_half = vectors[..., half_dim:]
    return jnp.concatenate(
        [first_half * cosine - second_half * sine, second_half * cosine + first_half * sine], -1
    )


def softmax_part(scores, inside):
    scores = jnp.where(inside, scores, -jnp.inf)
    peak = jnp.max(scores, -1)
    weights = jnp.exp(scores - peak[..., None]).astype(jnp.bfloat16)
    weight_sum = jnp.sum(weights, -1, dtype=jnp.float32)
    return (weights, peak, weight_sum)


def cached_part(asked, cache, row_lengths, kv_heads):
    row_count, step_count, columns = asked.shape
    head_dim = cache.shape[-1] // kv_heads
    group_size = columns // (kv_heads * head_dim)
    span = cache.shape[1] * cache.shape[3]
    cache_keys = cache[:, :, 0].reshape(row_count, span, kv_heads, head_dim)
    cache_values = cache[:, :, 1].reshape(row_count, span, kv_heads, head_dim)
    grouped = asked.reshape(row_count, step_count, kv_heads, group_size, head_dim)
    scores = jnp.einsum(
        "nsghd,ntgd->nsght", grouped, cache_keys, preferred_element_type=jnp.float32
    ) / math.sqrt(head_dim)
    inside = jnp.arange(span)[None, :] < row_lengths[:, None]
    weights, peak, weight_sum = softmax_part(scores, inside[:, None, None, None, :])
    blended = jnp.einsum(
        "nsght,ntgd->nsghd", weights, cache_values, preferred_element_type=jnp.float32
    )
    head_total = kv_heads * group_size
    return (
        blended.reshape(row_count, step_count, columns),
        peak.reshape(row_count, step_count, head_total),
        weight_sum.reshape(row_count, step_count, head_total),
    )


def shards(
    hidden_in, norm_gain, w_query, w_key, w_value, w_out, kv_pages, lengths, page_table, destination
):
    step_count, rows_here, model_width = hidden_in.shape
    replicas = lax.axis_size("replica")
    kv_heads = w_key.shape[1] // HD
    q_heads = w_query.shape[1] // HD
    group_size = q_heads // kv_heads
    widened = hidden_in.astype(jnp.float32)
    scale = lax.rsqrt(jnp.mean(widened * widened, -1, keepdims=True) + EPSILON)
    normed = (
        (widened * scale * norm_gain)
        .astype(jnp.bfloat16)
        .reshape(step_count * rows_here, model_width)
    )
    query_raw = (
        jnp.dot(normed, w_query, preferred_element_type=jnp.float32)
        .reshape(step_count, rows_here, q_heads, HD)
        .transpose(1, 0, 2, 3)
    )
    key_raw = (
        jnp.dot(normed, w_key, preferred_element_type=jnp.float32)
        .reshape(step_count, rows_here, kv_heads, HD)
        .transpose(1, 0, 2, 3)
    )
    value_raw = (
        jnp.dot(normed, w_value, preferred_element_type=jnp.float32)
        .reshape(step_count, rows_here, kv_heads, HD)
        .transpose(1, 0, 2, 3)
    )
    own_rows = jnp.arange(rows_here, dtype=jnp.int32)
    picked = destination[None, :] == jnp.arange(replicas, dtype=jnp.int32)[:, None]
    slot_of_dst = jnp.sum(jnp.where(picked, own_rows[None, :], 0), 1)
    own_lengths = jnp.sum(jnp.where(picked, lengths[None, :], 0), 1)
    outgoing = jnp.stack([slot_of_dst, own_lengths], -1)
    arrived = lax.all_to_all(outgoing, "replica", split_axis=0, concat_axis=0, tiled=True)
    source_slot = arrived[:, 0]
    slot_match = source_slot[:, None] == own_rows[None, :]
    source_of_slot = jnp.sum(jnp.where(slot_match, own_rows[:, None], 0), 0)
    slot_length = jnp.sum(jnp.where(slot_match, arrived[:, 1:2], 0), 0)
    positions = slot_length[:, None, None] + jnp.arange(step_count, dtype=jnp.int32)[None, :, None]
    queries = rotate(query_raw, positions).astype(jnp.bfloat16)
    fresh_keys = rotate(key_raw, positions).astype(jnp.bfloat16)
    fresh_values = value_raw.astype(jnp.bfloat16)
    package = jnp.concatenate([queries, fresh_keys, fresh_values], 2)[source_slot]
    package = lax.all_to_all(package, "replica", split_axis=0, concat_axis=0, tiled=True)
    queries = package[:, :, :q_heads]
    fresh_keys = package[:, :, q_heads : q_heads + kv_heads]
    fresh_values = package[:, :, q_heads + kv_heads :]
    cache = kv_pages[page_table[slot_of_dst]]
    cache_out, cache_peak, cache_sum = cached_part(
        queries.reshape(rows_here, step_count, q_heads * HD), cache, own_lengths, kv_heads
    )
    cache_out = cache_out.reshape(rows_here, step_count, q_heads, HD)
    grouped = queries.reshape(rows_here, step_count, kv_heads, group_size, HD)
    scores = jnp.einsum(
        "rsghd,rjgd->rsghj", grouped, fresh_keys, preferred_element_type=jnp.float32
    ) / math.sqrt(HD)
    causal = jnp.arange(step_count)[:, None] >= jnp.arange(step_count)[None, :]
    weights, fresh_peak, fresh_sum = softmax_part(scores, causal[None, :, None, None, :])
    fresh_out = jnp.einsum(
        "rsghj,rjgd->rsghd", weights, fresh_values, preferred_element_type=jnp.float32
    )
    fresh_out = fresh_out.reshape(rows_here, step_count, q_heads, HD)
    fresh_peak = fresh_peak.reshape(rows_here, step_count, q_heads)
    fresh_sum = fresh_sum.reshape(rows_here, step_count, q_heads)
    highest = jnp.maximum(cache_peak, fresh_peak)
    factor_c = jnp.exp(cache_peak - highest)
    factor_f = jnp.exp(fresh_peak - highest)
    blended = (cache_out * factor_c[..., None] + fresh_out * factor_f[..., None]) / (
        cache_sum * factor_c + fresh_sum * factor_f
    )[..., None]
    heads = blended.reshape(rows_here, step_count, q_heads * HD).astype(jnp.bfloat16)
    heads = lax.all_to_all(heads, "replica", split_axis=0, concat_axis=0, tiled=True)
    heads = heads[source_of_slot]
    flat_heads = heads.transpose(1, 0, 2).reshape(step_count * rows_here, q_heads * HD)
    partial_out = jnp.dot(flat_heads, w_out, preferred_element_type=jnp.float32)
    summed = lax.psum(partial_out, "tensor").astype(jnp.bfloat16)
    return summed.reshape(step_count, rows_here, model_width)


def solution(mesh):
    in_specs = (
        P(None, "replica", None),
        P(),
        P(None, "tensor"),
        P(None, "tensor"),
        P(None, "tensor"),
        P("tensor", None),
        P("replica", None, None, "tensor"),
        P("replica"),
        P("replica", None),
        P("replica"),
    )
    out_specs = P(None, "replica", None)
    return jax.shard_map(shards, mesh=mesh, in_specs=in_specs, out_specs=out_specs, check_vma=False)
```

```python
import functools
import math

import jax
import jax.numpy as jnp
from jax import lax
from jax.experimental import pallas as pl
from jax.experimental.pallas import tpu as pltpu
from jax.sharding import PartitionSpec as P

HD = 128
MSG = 32
ROPE_BASE = 1000000.0
EPSILON = 1e-06
MESH = pl.DeviceIdType.MESH
F32 = jnp.float32
BF16 = jnp.bfloat16


def mod(value, size):
    return lax.rem(value + 2 * size, size)


def kernel(
    sizes,
    dest_sm, len_sm, table_sm, gain_ref, hid_hbm, wq_hbm, wk_hbm, wv_hbm, wo_hbm, kv_hbm,
    out_hbm,
    hid, wall, kv, wo, acc, code, code_sm, meta_out, meta_in, pick, unpick, stack,
    q_out, q_in, h_out, h_in, heads, part, far, near_r, near_l, got, final,
    hid_sem, w_sem, kv_sem, wo_sem, code_sem,
    meta_send, meta_recv, q_send, q_recv, h_send, h_recv, x_send, x_recv, out_sem,
):
    R, T, S, NQ, D, KC = sizes
    M = S * R
    NH = NQ + 2
    me = lax.axis_index("replica")
    tx = lax.axis_index("tensor")
    chunks = D // KC
    DC = D // T
    half = M // 2
    pages = kv.shape[0]
    max_pages = pages // R
    page = kv.shape[2]

    def weight_copies(c):
        rows = pl.ds(pl.multiple_of(c * KC, KC), KC)
        return (
            pltpu.make_async_copy(wq_hbm.at[rows], wall.at[rows, 0 : NQ * HD], w_sem.at[c, 0]),
            pltpu.make_async_copy(wk_hbm.at[rows], wall.at[rows, NQ * HD : (NQ + 1) * HD], w_sem.at[c, 1]),
            pltpu.make_async_copy(wv_hbm.at[rows], wall.at[rows, (NQ + 1) * HD :], w_sem.at[c, 2]),
        )

    hid_copy = pltpu.make_async_copy(hid_hbm, hid, hid_sem)
    hid_copy.start()
    for c in range(chunks):
        for copy in weight_copies(c):
            copy.start()

    barrier = pltpu.get_barrier_semaphore()

    def greet(k, carry):
        pl.semaphore_signal(barrier, inc=1, device_id={"replica": mod(me + k, R)}, device_id_type=MESH)
        return carry

    lax.fori_loop(1, R, greet, 0)
    right = mod(tx + 1, T)
    left = mod(tx - 1, T)
    for other in (right, left):
        pl.semaphore_signal(barrier, inc=1, device_id={"tensor": other}, device_id_type=MESH)

    numbers = lax.broadcasted_iota(jnp.int32, (R, 128), 0)
    codes = jnp.zeros((R, 128), jnp.int32)
    for b in range(R):
        codes = jnp.where(numbers == dest_sm[b], len_sm[b] * R + b, codes)
    code[...] = codes
    code_copy = pltpu.make_async_copy(code, code_sm, code_sem)
    code_copy.start()
    for n in range(R):
        meta_out[n] = jnp.broadcast_to(codes[n : n + 1], (8, 128))

    pl.semaphore_wait(barrier, R - 1 + 2)

    def send_meta(k, carry):
        n = mod(me + k, R)
        pltpu.make_async_remote_copy(
            src_ref=meta_out.at[n], dst_ref=meta_in.at[me], send_sem=meta_send, recv_sem=meta_recv,
            device_id={"replica": n}, device_id_type=MESH,
        ).start()
        return carry

    lax.fori_loop(1, R, send_meta, 0)

    hid_copy.wait()
    squares = jnp.zeros((M, 128), F32)
    for c in range(D // 128):
        wide = hid[:, c * 128 : (c + 1) * 128].astype(F32)
        squares = squares + wide * wide
    scale = lax.rsqrt(jnp.sum(squares, 1, keepdims=True) * (1.0 / D) + EPSILON)

    acc[...] = jnp.zeros_like(acc)

    def project(c, carry):
        for copy in weight_copies(c):
            copy.wait()
        cols = pl.ds(pl.multiple_of(c * KC, KC), KC)
        normed = (hid[:, cols].astype(F32) * scale * gain_ref[:, cols]).astype(BF16)
        acc[...] += jnp.dot(normed, wall[cols, :], preferred_element_type=F32)
        return carry

    early = chunks // 2
    lax.fori_loop(0, early, project, 0)

    kv_copies = []
    step = pages // 4
    for c in range(4):
        rows = pl.ds(c * step, step)
        kv_copies.append(pltpu.make_async_copy(kv_hbm.at[rows], kv.at[rows], kv_sem.at[c]))
        kv_copies[-1].start()

    meta_all = pltpu.make_async_copy(meta_in.at[pl.ds(0, R - 1)], meta_in.at[pl.ds(0, R - 1)], meta_recv)
    meta_all.wait()
    meta_in[me] = meta_out[me]

    slot_rows = lax.broadcasted_iota(jnp.int32, (R, 128), 0)
    lens = jnp.zeros((R, 128), jnp.int32)
    msg_row = lax.broadcasted_iota(jnp.int32, (MSG, 128), 0)
    lane = lax.broadcasted_iota(jnp.int32, (MSG, 128), 1)
    for o in range(R):
        tile = meta_in[o]
        slot = tile & (R - 1)
        slot_wide = jnp.concatenate([slot] * (R // 8), 0)
        len_wide = jnp.concatenate([lax.shift_right_logical(tile, int(math.log2(R)))] * (R // 8), 0)
        lens = jnp.where(slot_rows == slot_wide, len_wide, lens)
        target = R * msg_row + jnp.concatenate([slot] * (MSG // 8), 0)
        for c in range(0, NH * M, 128):
            width = min(128, NH * M - c)
            hit = jnp.where(target == lane + c, 1.0, 0.0).astype(BF16)
            pick[pl.ds(o * MSG, MSG), c : c + width] = hit[:, :width]
    per = 128 // MSG
    group_of_lane = lax.broadcasted_iota(jnp.int32, (8, 128), 1) // MSG
    row_of_lane = lax.broadcasted_iota(jnp.int32, (8, 128), 1) % MSG
    wide_row = lax.broadcasted_iota(jnp.int32, (NQ * M, 128), 0)
    for g in range(R // per):
        slots = jnp.zeros((8, 128), jnp.int32)
        for i in range(per):
            slots = jnp.where(group_of_lane == i, meta_in[g * per + i] & (R - 1), slots)
        target = jnp.concatenate([R * row_of_lane + slots] * (NQ * M // 8), 0)
        unpick[:, g * 128 : (g + 1) * 128] = jnp.where(target == wide_row, 1.0, 0.0).astype(BF16)

    freq_lane = lax.broadcasted_iota(jnp.int32, (8, 128), 1) % (HD // 2)
    freq = jnp.exp(freq_lane.astype(F32) * (-2.0 / HD * math.log(ROPE_BASE)))
    angle = lens.astype(F32) * jnp.concatenate([freq] * (R // 8), 0)
    cos_len, sin_len = jnp.cos(angle), jnp.sin(angle)
    sign = jnp.where(lax.broadcasted_iota(jnp.int32, (R, 128), 1) < HD // 2, -1.0, 1.0)
    cosines, sines = [], []
    for s in range(S):
        if s == 0:
            cosines.append(cos_len)
            sines.append(sin_len * sign)
            continue
        cos_s = jnp.concatenate([jnp.cos(freq * float(s))] * (R // 8), 0)
        sin_s = jnp.concatenate([jnp.sin(freq * float(s))] * (R // 8), 0)
        cosines.append(cos_len * cos_s - sin_len * sin_s)
        sines.append((sin_len * cos_s + cos_len * sin_s) * sign)
    cosine = jnp.concatenate(cosines, 0)
    sine = jnp.concatenate(sines, 0)

    lax.fori_loop(early, chunks, project, 0)

    wo_copy = pltpu.make_async_copy(wo_hbm, wo, wo_sem)
    wo_copy.start()

    for h in range(NH):
        vec = acc[:, h * HD : (h + 1) * HD]
        if h <= NQ:
            vec = vec * cosine + pltpu.roll(vec, HD // 2, 1) * sine
        stack[h * M : (h + 1) * M, :] = vec.astype(BF16)
    q_out[...] = jnp.dot(pick[...], stack[...], preferred_element_type=F32).astype(BF16).reshape(R, MSG, HD)

    def send_q(k, carry):
        o = mod(me + k, R)
        pltpu.make_async_remote_copy(
            src_ref=q_out.at[o], dst_ref=q_in.at[me], send_sem=q_send, recv_sem=q_recv.at[me],
            device_id={"replica": o}, device_id_type=MESH,
        ).start()
        return carry

    lax.fori_loop(1, R, send_q, 0)
    q_in[me] = q_out[me]

    code_copy.wait()
    for copy in kv_copies:
        copy.wait()

    tok = lax.broadcasted_iota(jnp.int32, (MSG, page), 1)
    f_row = lax.broadcasted_iota(jnp.int32, (MSG, MSG), 0) % S
    f_col = lax.broadcasted_iota(jnp.int32, (MSG, MSG), 1) - NQ * S
    fresh_ok = (f_col >= 0) & (f_col <= f_row)
    factor = 1.0 / math.sqrt(HD)
    dims = (((1,), (1,)), ((), ()))

    def attend(n):
        word = code_sm[n, 0]
        slot = word & (R - 1)
        length = lax.shift_right_logical(word, int(math.log2(R)))
        where = [table_sm[p, slot] for p in range(max_pages)]
        q = q_in[n]
        scores = []
        for p in range(max_pages):
            sc = lax.dot_general(q, kv[where[p], 0], dims, preferred_element_type=F32) * factor
            scores.append(jnp.where(tok < length - p * page, sc, -jnp.inf))
        fresh = lax.dot_general(q, q, dims, preferred_element_type=F32) * factor
        fresh = jnp.where(fresh_ok, fresh, -jnp.inf)
        top = functools.reduce(jnp.maximum, scores)
        peak = jnp.maximum(jnp.max(top, 1, keepdims=True), jnp.max(fresh, 1, keepdims=True))
        w_fresh = jnp.exp(fresh - peak).astype(BF16)
        values = pltpu.roll(q.astype(F32), MSG - S, 0).astype(BF16)
        total = jnp.dot(w_fresh, values, preferred_element_type=F32)
        weight = jnp.zeros((MSG, page), F32)
        for p in range(max_pages):
            w = jnp.exp(scores[p] - peak).astype(BF16)
            weight = weight + w.astype(F32)
            total = total + jnp.dot(w, kv[where[p], 1], preferred_element_type=F32)
        denom = jnp.sum(weight, 1, keepdims=True) + jnp.sum(w_fresh.astype(F32), 1, keepdims=True)
        h_out[n] = (total / denom).astype(BF16)

    def wait_q(n):
        pltpu.make_async_copy(q_in.at[n], q_in.at[n], q_recv.at[n]).wait()

    def send_heads(n):
        pltpu.make_async_remote_copy(
            src_ref=h_out.at[n], dst_ref=h_in.at[me], send_sem=h_send, recv_sem=h_recv,
            device_id={"replica": n}, device_id_type=MESH,
        ).start()

    unroll = 4

    def attend_group(i, carry):
        them = [mod(me - (unroll * i + u + 1), R) for u in range(unroll)]
        for n in them:
            wait_q(n)
        for n in them:
            attend(n)
        for n in them:
            send_heads(n)
        return carry

    lax.fori_loop(0, R // unroll - 1, attend_group, 0)
    last = [mod(me - (R - unroll + u + 1), R) for u in range(unroll - 1)]
    for n in last:
        wait_q(n)
    for n in last:
        attend(n)
    for n in last:
        send_heads(n)
    attend(me)
    h_in[me] = h_out[me]

    wo_copy.wait()
    pltpu.make_async_copy(h_in.at[pl.ds(0, R - 1)], h_in.at[pl.ds(0, R - 1)], h_recv).wait()
    flat = h_in[...].reshape(R * MSG, HD)
    by_head = jnp.dot(unpick[...], flat, preferred_element_type=F32).astype(BF16)
    for h in range(NQ):
        heads[:, h * HD : (h + 1) * HD] = by_head[h * M : (h + 1) * M]

    def cols_of(c):
        return pl.ds(pl.multiple_of(c * DC, DC), DC)

    def partial(c):
        return jnp.dot(heads[...], wo[:, cols_of(c)], preferred_element_type=F32)

    def push(src, dst, i, other):
        copy = pltpu.make_async_remote_copy(
            src_ref=src, dst_ref=dst, send_sem=x_send.at[i], recv_sem=x_recv.at[i],
            device_id={"tensor": other}, device_id_type=MESH,
        )
        copy.start()
        return copy

    low, high = slice(0, half), slice(half, M)
    far[...] = partial(mod(tx + 2, T)).astype(BF16)
    c0 = push(far.at[low], got.at[0], 0, right)
    c1 = push(far.at[high], got.at[1], 1, left)
    sum_r = partial(right)
    near_r[high] = sum_r[half:].astype(BF16)
    c2 = push(near_r.at[high], got.at[2], 2, right)
    sum_l = partial(left)
    near_l[low] = sum_l[:half].astype(BF16)
    c3 = push(near_l.at[low], got.at[3], 3, left)
    part[...] = partial(tx)
    c0.wait_recv()
    near_r[low] = (sum_r[:half] + got[0].astype(F32)).astype(BF16)
    c4 = push(near_r.at[low], got.at[4], 4, right)
    c1.wait_recv()
    near_l[high] = (sum_l[half:] + got[1].astype(F32)).astype(BF16)
    c5 = push(near_l.at[high], got.at[5], 5, left)
    c3.wait_recv()
    c4.wait_recv()
    final[low] = (part[low] + got[3].astype(F32) + got[4].astype(F32)).astype(BF16)
    mine = out_hbm.at[:, cols_of(tx)]
    c6 = push(final.at[low], mine.at[low], 6, right)
    c2.wait_recv()
    c5.wait_recv()
    final[high] = (part[high] + got[2].astype(F32) + got[5].astype(F32)).astype(BF16)
    c7 = push(final.at[high], mine.at[high], 7, left)
    c8 = push(final.at[high], mine.at[high], 8, right)
    c9 = push(final.at[low], mine.at[low], 9, left)
    own = pltpu.make_async_copy(final, mine, out_sem)
    own.start()
    from_left = out_hbm.at[low, cols_of(left)]
    from_right = out_hbm.at[high, cols_of(right)]
    c6.wait_recv()
    c10 = push(from_left, from_left, 10, right)
    c7.wait_recv()
    c11 = push(from_right, from_right, 11, left)
    for copy in (c8, c9, c10, c11):
        copy.wait_recv()
    for copy in (c0, c1, c2, c3, c4, c5, c6, c7, c8, c9, c10, c11):
        copy.wait_send()
    own.wait()
    some = pl.ds(0, R - 1)
    pltpu.make_async_copy(meta_out.at[some], meta_out.at[some], meta_send).wait()
    pltpu.make_async_copy(q_out.at[some], q_out.at[some], q_send).wait()
    pltpu.make_async_copy(h_out.at[some], h_out.at[some], h_send).wait()


def shards(
    replicas, tensors, hidden_in, norm_gain, w_query, w_key, w_value, w_out, kv_pages, lengths, page_table, destination
):
    S, R, D = hidden_in.shape
    T = tensors
    NQ = w_query.shape[1] // HD
    NH = NQ + 2
    M = S * R
    KC = min(512, D // 2)
    DC = D // T
    pages, _, page, _ = kv_pages.shape
    any_spec = pl.BlockSpec(memory_space=pl.ANY)
    smem = pl.BlockSpec(memory_space=pltpu.SMEM)
    dma = pltpu.SemaphoreType.DMA
    out = pl.pallas_call(
        functools.partial(kernel, (R, T, S, NQ, D, KC)),
        out_shape=jax.ShapeDtypeStruct((M, D), BF16),
        in_specs=[smem, smem, smem, pl.BlockSpec(memory_space=pltpu.VMEM)] + [any_spec] * 6,
        out_specs=any_spec,
        scratch_shapes=[
            pltpu.VMEM((M, D), BF16),
            pltpu.VMEM((D, NH * HD), BF16),
            pltpu.VMEM(kv_pages.shape, BF16),
            pltpu.VMEM(w_out.shape, BF16),
            pltpu.VMEM((M, NH * HD), F32),
            pltpu.VMEM((R, 128), jnp.int32),
            pltpu.SMEM((R, 128), jnp.int32),
            pltpu.VMEM((R, 8, 128), jnp.int32),
            pltpu.VMEM((R, 8, 128), jnp.int32),
            pltpu.VMEM((R * MSG, NH * M), BF16),
            pltpu.VMEM((NQ * M, R * MSG), BF16),
            pltpu.VMEM((NH * M, HD), BF16),
            pltpu.VMEM((R, MSG, HD), BF16),
            pltpu.VMEM((R, MSG, HD), BF16),
            pltpu.VMEM((R, MSG, HD), BF16),
            pltpu.VMEM((R, MSG, HD), BF16),
            pltpu.VMEM((M, NQ * HD), BF16),
            pltpu.VMEM((M, DC), F32),
            pltpu.VMEM((M, DC), BF16),
            pltpu.VMEM((M, DC), BF16),
            pltpu.VMEM((M, DC), BF16),
            pltpu.VMEM((6, M // 2, DC), BF16),
            pltpu.VMEM((M, DC), BF16),
            dma, dma((D // KC, 3)), dma((4,)), dma, dma,
            dma, dma, dma, dma((R,)), dma, dma, dma((12,)), dma((12,)), dma,
        ],
        compiler_params=pltpu.CompilerParams(
            collective_id=0, has_side_effects=True, vmem_limit_bytes=58 * 1024 * 1024
        ),
        name="decode_attention",
    )(
        destination, lengths, page_table.T, norm_gain.reshape(1, D), hidden_in.reshape(M, D),
        w_query, w_key, w_value, w_out, kv_pages,
    )
    return out.reshape(S, R, D)


def solution(mesh):
    in_specs = (
        P(None, "replica", None),
        P(),
        P(None, "tensor"),
        P(None, "tensor"),
        P(None, "tensor"),
        P("tensor", None),
        P("replica", None, None, "tensor"),
        P("replica"),
        P("replica", None),
        P("replica"),
    )
    body = functools.partial(shards, mesh.shape["replica"], mesh.shape["tensor"])
    return jax.shard_map(
        body, mesh=mesh, in_specs=in_specs, out_specs=P(None, "replica", None), check_vma=False
    )
```

```python
import functools
import math

import jax
import jax.numpy as jnp
from jax import lax
from jax.experimental import pallas as pl
from jax.experimental.pallas import tpu as pltpu
from jax.sharding import PartitionSpec as P

HD = 128
GROUP = 4
MSG = 32
ROPE_BASE = 1000000.0
EPSILON = 1e-06
SUBS = 2
MESH = pl.DeviceIdType.MESH
F32 = jnp.float32
BF16 = jnp.bfloat16


def mod(value, size):
    return lax.rem(value + 2 * size, size)


def settle(ref, sem):
    pltpu.make_async_copy(ref, ref, sem).wait()


def kernel(
    sizes,
    dest_sm, len_sm, table_sm, gain_ref, hid_hbm, wq_hbm, wk_hbm, wv_hbm, wo_hbm, kv_hbm,
    out_hbm,
    hid, wall, kv, wo, acc, code, code_sm, meta_out, meta_in, pick, unpick, stack,
    q_out, q_in, h_out, h_in, heads, part, sums_r, sums_l, far, near_r, near_l, got, final,
    hid_sem, w_sem, kv_sem, wo_sem, code_sem,
    meta_send, meta_recv, q_send, q_recv, h_send, h_recv, x_send, x_recv, out_sem,
):
    R, T, S, NQ, D, KC = sizes
    M = S * R
    NH = NQ + 2
    me = lax.axis_index("replica")
    tx = lax.axis_index("tensor")
    chunks = D // KC
    group = me // GROUP
    groups = R // GROUP
    DC = D // T
    half = M // 2
    pages = kv.shape[0]
    max_pages = pages // R
    page = kv.shape[2]

    def weight_copies(c):
        rows = pl.ds(pl.multiple_of(c * KC, KC), KC)
        return (
            pltpu.make_async_copy(wq_hbm.at[rows], wall.at[rows, 0 : NQ * HD], w_sem.at[c, 0]),
            pltpu.make_async_copy(wk_hbm.at[rows], wall.at[rows, NQ * HD : (NQ + 1) * HD], w_sem.at[c, 1]),
            pltpu.make_async_copy(wv_hbm.at[rows], wall.at[rows, (NQ + 1) * HD :], w_sem.at[c, 2]),
        )

    hid_copy = pltpu.make_async_copy(hid_hbm, hid, hid_sem)
    hid_copy.start()
    ahead = 2
    for c in range(ahead):
        for copy in weight_copies(c):
            copy.start()

    barrier = pltpu.get_barrier_semaphore()

    def greet(k, carry):
        pl.semaphore_signal(barrier, inc=1, device_id={"replica": mod(me + k, R)}, device_id_type=MESH)
        return carry

    lax.fori_loop(1, R, greet, 0)
    right = mod(tx + 1, T)
    left = mod(tx - 1, T)
    for other in (right, left):
        pl.semaphore_signal(barrier, inc=1, device_id={"tensor": other}, device_id_type=MESH)

    numbers = lax.broadcasted_iota(jnp.int32, (R, 128), 0)
    codes = jnp.zeros((R, 128), jnp.int32)
    for b in range(R):
        codes = jnp.where(numbers == dest_sm[b], len_sm[b] * R + b, codes)
    code[...] = codes
    code_copy = pltpu.make_async_copy(code, code_sm, code_sem)
    code_copy.start()
    for n in range(R):
        meta_out[n] = jnp.broadcast_to(codes[n : n + 1], (8, 128))

    pl.semaphore_wait(barrier, R - 1 + 2)

    def to_all(make):
        def send(k, carry):
            n = mod(group * GROUP + GROUP + k, R)

            @pl.when(n != me)
            def _():
                make(n).start()

            return carry

        lax.fori_loop(0, R, send, 0)

    def meta_copy(n):
        return pltpu.make_async_remote_copy(
            src_ref=meta_out.at[n], dst_ref=meta_in.at[me], send_sem=meta_send, recv_sem=meta_recv,
            device_id={"replica": n}, device_id_type=MESH,
        )

    to_all(meta_copy)

    hid_copy.wait()
    squares = jnp.zeros((M, 128), F32)
    for c in range(D // 128):
        wide = hid[:, c * 128 : (c + 1) * 128].astype(F32)
        squares = squares + wide * wide
    scale = lax.rsqrt(jnp.sum(squares, 1, keepdims=True) * (1.0 / D) + EPSILON)

    for c in range(0, D, 512):
        cols = slice(c, c + 512)
        hid[:, cols] = (hid[:, cols].astype(F32) * scale * gain_ref[:, cols]).astype(BF16)

    kv_copies = []
    step = pages // 4
    for c in range(4):
        rows = pl.ds(c * step, step)
        kv_copies.append(pltpu.make_async_copy(kv_hbm.at[rows], kv.at[rows], kv_sem.at[c]))

    def project(c):
        for copy in weight_copies(c):
            copy.wait()
        if c + ahead < chunks:
            for copy in weight_copies(c + ahead):
                copy.start()
        elif c + ahead == chunks:
            kv_copies[0].start()
            kv_copies[1].start()
        cols = slice(c * KC, (c + 1) * KC)
        term = jnp.dot(hid[:, cols], wall[cols, :], preferred_element_type=F32)
        acc[...] = term if c == 0 else acc[...] + term

    early = chunks // 2
    for c in range(early):
        project(c)

    settle(meta_in.at[pl.ds(0, R - 1)], meta_recv)
    meta_in[me] = meta_out[me]

    slot_rows = lax.broadcasted_iota(jnp.int32, (R, 128), 0)
    lens = jnp.zeros((R, 128), jnp.int32)
    msg_row = lax.broadcasted_iota(jnp.int32, (MSG, 128), 0)
    lane = lax.broadcasted_iota(jnp.int32, (MSG, 128), 1)
    for o in range(R):
        tile = meta_in[o]
        slot = tile & (R - 1)
        slot_wide = jnp.concatenate([slot] * (R // 8), 0)
        len_wide = jnp.concatenate([lax.shift_right_logical(tile, int(math.log2(R)))] * (R // 8), 0)
        lens = jnp.where(slot_rows == slot_wide, len_wide, lens)
        target = R * msg_row + jnp.concatenate([slot] * (MSG // 8), 0)
        for c in range(0, NH * M, 128):
            width = min(128, NH * M - c)
            hit = jnp.where(target == lane + c, 1.0, 0.0).astype(BF16)
            pick[pl.ds(o * MSG, MSG), c : c + width] = hit[:, :width]
    freq_lane = lax.broadcasted_iota(jnp.int32, (8, 128), 1) % (HD // 2)
    freq = jnp.exp(freq_lane.astype(F32) * (-2.0 / HD * math.log(ROPE_BASE)))
    angle = lens.astype(F32) * jnp.concatenate([freq] * (R // 8), 0)
    cos_len, sin_len = jnp.cos(angle), jnp.sin(angle)
    sign = jnp.where(lax.broadcasted_iota(jnp.int32, (R, 128), 1) < HD // 2, -1.0, 1.0)
    cosines, sines = [], []
    for s in range(S):
        if s == 0:
            cosines.append(cos_len)
            sines.append(sin_len * sign)
            continue
        cos_s = jnp.concatenate([jnp.cos(freq * float(s))] * (R // 8), 0)
        sin_s = jnp.concatenate([jnp.sin(freq * float(s))] * (R // 8), 0)
        cosines.append(cos_len * cos_s - sin_len * sin_s)
        sines.append((sin_len * cos_s + cos_len * sin_s) * sign)
    cosine = jnp.concatenate(cosines, 0)
    sine = jnp.concatenate(sines, 0)

    for c in range(early, chunks):
        project(c)
    kv_copies[2].start()
    kv_copies[3].start()

    for h in range(NH):
        vec = acc[:, h * HD : (h + 1) * HD]
        if h <= NQ:
            vec = vec * cosine + pltpu.roll(vec, HD // 2, 1) * sine
        stack[h * M : (h + 1) * M, :] = vec.astype(BF16)
    q_out[...] = jnp.dot(pick[...], stack[...], preferred_element_type=F32).astype(BF16).reshape(R, MSG, HD)

    def q_copy(o):
        return pltpu.make_async_remote_copy(
            src_ref=q_out.at[o], dst_ref=q_in.at[me], send_sem=q_send, recv_sem=q_recv.at[me],
            device_id={"replica": o}, device_id_type=MESH,
        )

    to_all(q_copy)
    q_in[me] = q_out[me]
    wo_copy = pltpu.make_async_copy(wo_hbm, wo, wo_sem)
    wo_copy.start()

    per = 128 // MSG
    group_of_lane = lax.broadcasted_iota(jnp.int32, (8, 128), 1) // MSG
    row_of_lane = lax.broadcasted_iota(jnp.int32, (8, 128), 1) % MSG
    wide_row = lax.broadcasted_iota(jnp.int32, (NQ * M, 128), 0)
    for g in range(R // per):
        slots = jnp.zeros((8, 128), jnp.int32)
        for i in range(per):
            slots = jnp.where(group_of_lane == i, meta_in[g * per + i] & (R - 1), slots)
        target = jnp.concatenate([R * row_of_lane + slots] * (NQ * M // 8), 0)
        unpick[:, g * 128 : (g + 1) * 128] = jnp.where(target == wide_row, 1.0, 0.0).astype(BF16)

    code_copy.wait()
    for copy in kv_copies:
        copy.wait()

    span = max_pages * page
    rows = GROUP * MSG
    tok = lax.broadcasted_iota(jnp.int32, (MSG, span), 1)
    f_row = lax.broadcasted_iota(jnp.int32, (rows, rows), 0)
    f_col = lax.broadcasted_iota(jnp.int32, (rows, rows), 1)
    f_key = f_col % MSG - NQ * S
    fresh_ok = (f_row // MSG == f_col // MSG) & (f_key >= 0) & (f_key <= f_row % S)
    factor = math.log2(math.e) / math.sqrt(HD)
    dims = (((1,), (1,)), ((), ()))

    def attend(g):
        first = g * GROUP
        q = q_in[pl.ds(first, GROUP)].reshape(rows, HD)
        fresh = lax.dot_general(q, q, dims, preferred_element_type=F32)
        fresh = jnp.where(fresh_ok, fresh, -jnp.inf)
        places, scores = [], []
        for u in range(GROUP):
            word = code_sm[first + u, 0]
            slot = word & (R - 1)
            length = lax.shift_right_logical(word, int(math.log2(R)))
            places.append([table_sm[p, slot] for p in range(max_pages)])
            keys = jnp.concatenate([kv[at, 0] for at in places[u]], 0)
            sc = lax.dot_general(q[u * MSG : (u + 1) * MSG], keys, dims, preferred_element_type=F32)
            scores.append(jnp.where(tok < length, sc, -jnp.inf))
        values = pltpu.roll(q.astype(F32), rows - S, 0).astype(BF16)
        for u in range(GROUP):
            mine = slice(u * MSG, (u + 1) * MSG)
            peak = jnp.maximum(
                jnp.max(scores[u], 1, keepdims=True), jnp.max(fresh[mine], 1, keepdims=True)
            )
            w_fresh = jnp.exp2((fresh[mine] - peak) * factor).astype(BF16)
            w = jnp.exp2((scores[u] - peak) * factor).astype(BF16)
            total = jnp.dot(w_fresh, values, preferred_element_type=F32)
            cached = jnp.concatenate([kv[at, 1] for at in places[u]], 0)
            total = total + jnp.dot(w, cached, preferred_element_type=F32)
            denom = jnp.sum(w.astype(F32), 1, keepdims=True) + jnp.sum(
                w_fresh.astype(F32), 1, keepdims=True
            )
            h_out[first + u] = (total / denom).astype(BF16)

    def wait_q(n):
        settle(q_in.at[n], q_recv.at[n])

    def heads_copy(n):
        return pltpu.make_async_remote_copy(
            src_ref=h_out.at[n], dst_ref=h_in.at[me], send_sem=h_send, recv_sem=h_recv,
            device_id={"replica": n}, device_id_type=MESH,
        )

    def attend_group(i, carry):
        g = mod(group - 1 - i, groups)
        for u in range(GROUP):
            n = g * GROUP + u

            @pl.when(n != me)
            def _():
                wait_q(n)

        attend(g)
        for u in range(GROUP):
            n = g * GROUP + u

            @pl.when(n != me)
            def _():
                heads_copy(n).start()

        return carry

    lax.fori_loop(0, groups, attend_group, 0)
    h_in[me] = h_out[me]

    wo_copy.wait()
    settle(h_in.at[pl.ds(0, R - 1)], h_recv)
    flat = h_in[...].reshape(R * MSG, HD)
    by_head = jnp.dot(unpick[...], flat, preferred_element_type=F32).astype(BF16)
    for h in range(NQ):
        heads[:, h * HD : (h + 1) * HD] = by_head[h * M : (h + 1) * M]

    wide = DC // SUBS

    def cols_of(c, b):
        return pl.ds(pl.multiple_of(c * DC + b * wide, 128), wide)

    def partial(c, b):
        return jnp.dot(heads[...], wo[:, cols_of(c, b)], preferred_element_type=F32)

    copies = []

    def push(src, dst, b, i, other):
        copy = pltpu.make_async_remote_copy(
            src_ref=src, dst_ref=dst, send_sem=x_send.at[b, i], recv_sem=x_recv.at[b, i],
            device_id={"tensor": other}, device_id_type=MESH,
        )
        copy.start()
        copies.append(copy)
        return copy

    low, high = slice(0, half), slice(half, M)
    subs = range(SUBS)
    c0, c1, c2, c3, c4, c5, c6, c7, c8, c9 = ([] for _ in range(10))
    for b in subs:
        far[b] = partial(mod(tx + 2, T), b).astype(BF16)
        c0.append(push(far.at[b, low], got.at[b, 0], b, 0, right))
        c1.append(push(far.at[b, high], got.at[b, 1], b, 1, left))
    for b in subs:
        sums_r[b] = partial(right, b)
        near_r[b, high] = sums_r[b, high].astype(BF16)
        c2.append(push(near_r.at[b, high], got.at[b, 2], b, 2, right))
        sums_l[b] = partial(left, b)
        near_l[b, low] = sums_l[b, low].astype(BF16)
        c3.append(push(near_l.at[b, low], got.at[b, 3], b, 3, left))
    for b in subs:
        part[b] = partial(tx, b)
    for b in subs:
        c0[b].wait_recv()
        near_r[b, low] = (sums_r[b, low] + got[b, 0].astype(F32)).astype(BF16)
        c4.append(push(near_r.at[b, low], got.at[b, 4], b, 4, right))
        c1[b].wait_recv()
        near_l[b, high] = (sums_l[b, high] + got[b, 1].astype(F32)).astype(BF16)
        c5.append(push(near_l.at[b, high], got.at[b, 5], b, 5, left))
    own = []
    for b in subs:
        mine = out_hbm.at[:, cols_of(tx, b)]
        c3[b].wait_recv()
        c4[b].wait_recv()
        final[b, low] = (part[b, low] + got[b, 3].astype(F32) + got[b, 4].astype(F32)).astype(BF16)
        c6.append(push(final.at[b, low], mine.at[low], b, 6, right))
        c2[b].wait_recv()
        c5[b].wait_recv()
        final[b, high] = (part[b, high] + got[b, 2].astype(F32) + got[b, 5].astype(F32)).astype(BF16)
        c7.append(push(final.at[b, high], mine.at[high], b, 7, left))
        c8.append(push(final.at[b, high], mine.at[high], b, 8, right))
        c9.append(push(final.at[b, low], mine.at[low], b, 9, left))
        own.append(pltpu.make_async_copy(final.at[b], mine, out_sem.at[b]))
        own[b].start()
    last = []
    for b in subs:
        from_left = out_hbm.at[low, cols_of(left, b)]
        from_right = out_hbm.at[high, cols_of(right, b)]
        c6[b].wait_recv()
        last.append(push(from_left, from_left, b, 10, right))
        c7[b].wait_recv()
        last.append(push(from_right, from_right, b, 11, left))
    for copy in c8 + c9 + last:
        copy.wait_recv()
    for copy in copies:
        copy.wait_send()
    for copy in own:
        copy.wait()
    some = pl.ds(0, R - 1)
    settle(meta_out.at[some], meta_send)
    settle(q_out.at[some], q_send)
    settle(h_out.at[some], h_send)


def shards(
    replicas, tensors, hidden_in, norm_gain, w_query, w_key, w_value, w_out, kv_pages, lengths, page_table, destination
):
    S, R, D = hidden_in.shape
    T = tensors
    NQ = w_query.shape[1] // HD
    NH = NQ + 2
    M = S * R
    KC = min(1024, D // 2)
    DC = D // T
    pages, _, page, _ = kv_pages.shape
    any_spec = pl.BlockSpec(memory_space=pl.ANY)
    smem = pl.BlockSpec(memory_space=pltpu.SMEM)
    dma = pltpu.SemaphoreType.DMA
    out = pl.pallas_call(
        functools.partial(kernel, (R, T, S, NQ, D, KC)),
        out_shape=jax.ShapeDtypeStruct((M, D), BF16),
        in_specs=[smem, smem, smem, pl.BlockSpec(memory_space=pltpu.VMEM)] + [any_spec] * 6,
        out_specs=any_spec,
        scratch_shapes=[
            pltpu.VMEM((M, D), BF16),
            pltpu.VMEM((D, NH * HD), BF16),
            pltpu.VMEM(kv_pages.shape, BF16),
            pltpu.VMEM(w_out.shape, BF16),
            pltpu.VMEM((M, NH * HD), F32),
            pltpu.VMEM((R, 128), jnp.int32),
            pltpu.SMEM((R, 128), jnp.int32),
            pltpu.VMEM((R, 8, 128), jnp.int32),
            pltpu.VMEM((R, 8, 128), jnp.int32),
            pltpu.VMEM((R * MSG, NH * M), BF16),
            pltpu.VMEM((NQ * M, R * MSG), BF16),
            pltpu.VMEM((NH * M, HD), BF16),
            pltpu.VMEM((R, MSG, HD), BF16),
            pltpu.VMEM((R, MSG, HD), BF16),
            pltpu.VMEM((R, MSG, HD), BF16),
            pltpu.VMEM((R, MSG, HD), BF16),
            pltpu.VMEM((M, NQ * HD), BF16),
            pltpu.VMEM((SUBS, M, DC // SUBS), F32),
            pltpu.VMEM((SUBS, M, DC // SUBS), F32),
            pltpu.VMEM((SUBS, M, DC // SUBS), F32),
            pltpu.VMEM((SUBS, M, DC // SUBS), BF16),
            pltpu.VMEM((SUBS, M, DC // SUBS), BF16),
            pltpu.VMEM((SUBS, M, DC // SUBS), BF16),
            pltpu.VMEM((SUBS, 6, M // 2, DC // SUBS), BF16),
            pltpu.VMEM((SUBS, M, DC // SUBS), BF16),
            dma, dma((D // KC, 3)), dma((4,)), dma, dma,
            dma, dma, dma, dma((R,)), dma, dma, dma((SUBS, 12)), dma((SUBS, 12)), dma((SUBS,)),
        ],
        compiler_params=pltpu.CompilerParams(
            collective_id=0, has_side_effects=True, vmem_limit_bytes=58 * 1024 * 1024
        ),
        name="decode_attention",
    )(
        destination, lengths, page_table.T, norm_gain.reshape(1, D), hidden_in.reshape(M, D),
        w_query, w_key, w_value, w_out, kv_pages,
    )
    return out.reshape(S, R, D)


def solution(mesh):
    in_specs = (
        P(None, "replica", None),
        P(),
        P(None, "tensor"),
        P(None, "tensor"),
        P(None, "tensor"),
        P("tensor", None),
        P("replica", None, None, "tensor"),
        P("replica"),
        P("replica", None),
        P("replica"),
    )
    body = functools.partial(shards, mesh.shape["replica"], mesh.shape["tensor"])
    return jax.shard_map(
        body, mesh=mesh, in_specs=in_specs, out_specs=P(None, "replica", None), check_vma=False
    )
```

```python
import functools
import math

import jax
import jax.numpy as jnp
from jax import lax
from jax.experimental import pallas as pl
from jax.experimental.pallas import tpu as pltpu
from jax.sharding import PartitionSpec as P

HD = 128
GROUP = 4
MSG = 32
ROPE_BASE = 1000000.0
EPSILON = 1e-06
SUBS = 2
MESH = pl.DeviceIdType.MESH
F32 = jnp.float32
BF16 = jnp.bfloat16


def mod(value, size):
    return lax.rem(value + 2 * size, size)


def settle(ref, sem):
    pltpu.make_async_copy(ref, ref, sem).wait()


def kernel(
    sizes,
    dest_sm, len_sm, table_sm, gain_ref, hid_hbm, wq_hbm, wk_hbm, wv_hbm, wo_hbm, kv_hbm,
    out_hbm,
    hid, wq, wk, wv, kv, wo, acc, code, code_sm, meta_out, meta_in, pick, unpick, stack,
    q_out, q_in, h_out, h_in, heads, part, sums_r, sums_l, far, near_r, near_l, got, final,
    hid_sem, w_sem, kv_sem, wo_sem, code_sem,
    meta_send, meta_recv, q_send, q_recv, h_send, h_recv, x_send, x_recv, out_sem,
):
    R, T, S, NQ, D, KC = sizes
    M = S * R
    NH = NQ + 2
    me = lax.axis_index("replica")
    tx = lax.axis_index("tensor")
    chunks = D // KC
    group = me // GROUP
    groups = R // GROUP
    DC = D // T
    half = M // 2
    pages = kv.shape[0]
    max_pages = pages // R
    page = kv.shape[2]

    def weight_copies(c):
        rows = pl.ds(pl.multiple_of(c * KC, KC), KC)
        return (
            pltpu.make_async_copy(wq_hbm.at[rows], wq.at[rows], w_sem.at[c, 0]),
            pltpu.make_async_copy(wk_hbm.at[rows], wk.at[rows], w_sem.at[c, 1]),
            pltpu.make_async_copy(wv_hbm.at[rows], wv.at[rows], w_sem.at[c, 2]),
        )

    hid_copy = pltpu.make_async_copy(hid_hbm, hid, hid_sem)
    hid_copy.start()
    def load(c):
        if c < chunks:
            for copy in weight_copies(c):
                copy.start()

    load(0)
    load(1)

    barrier = pltpu.get_barrier_semaphore()

    def greet(k, carry):
        pl.semaphore_signal(barrier, inc=1, device_id={"replica": mod(me + k, R)}, device_id_type=MESH)
        return carry

    lax.fori_loop(1, R, greet, 0)
    right = mod(tx + 1, T)
    left = mod(tx - 1, T)
    for other in (right, left):
        pl.semaphore_signal(barrier, inc=1, device_id={"tensor": other}, device_id_type=MESH)

    numbers = lax.broadcasted_iota(jnp.int32, (R, 128), 0)
    codes = jnp.zeros((R, 128), jnp.int32)
    for b in range(R):
        codes = jnp.where(numbers == dest_sm[b], len_sm[b] * R + b, codes)
    code[...] = codes
    code_copy = pltpu.make_async_copy(code, code_sm, code_sem)
    code_copy.start()
    for n in range(R):
        meta_out[n] = jnp.broadcast_to(codes[n : n + 1], (8, 128))

    pl.semaphore_wait(barrier, R - 1 + 2)

    def to_all(make):
        def send(k, carry):
            n = mod(group * GROUP + GROUP + k, R)

            @pl.when(n != me)
            def _():
                make(n).start()

            return carry

        lax.fori_loop(0, R, send, 0)

    def meta_copy(n):
        return pltpu.make_async_remote_copy(
            src_ref=meta_out.at[n], dst_ref=meta_in.at[me], send_sem=meta_send, recv_sem=meta_recv,
            device_id={"replica": n}, device_id_type=MESH,
        )

    to_all(meta_copy)

    hid_copy.wait()
    load(2)
    squares = jnp.zeros((M, 128), F32)
    for c in range(D // 128):
        wide = hid[:, c * 128 : (c + 1) * 128].astype(F32)
        squares = squares + wide * wide
    load(3)
    scale = lax.rsqrt(jnp.sum(squares, 1, keepdims=True) * (1.0 / D) + EPSILON)

    for c in range(0, D, 512):
        cols = slice(c, c + 512)
        hid[:, cols] = (hid[:, cols].astype(F32) * scale * gain_ref[:, cols]).astype(BF16)

    for c in range(4, chunks):
        load(c)
    kv_copies = []
    step = pages // 4
    for c in range(4):
        rows = pl.ds(c * step, step)
        kv_copies.append(pltpu.make_async_copy(kv_hbm.at[rows], kv.at[rows], kv_sem.at[c]))

    def project(c):
        for copy in weight_copies(c):
            copy.wait()
        if c + 1 == chunks:
            for copy in kv_copies:
                copy.start()
        cols = slice(c * KC, (c + 1) * KC)
        weights = jnp.concatenate([wq[cols], wk[cols], wv[cols]], 1)
        term = jnp.dot(hid[:, cols], weights, preferred_element_type=F32)
        acc[...] = term if c == 0 else acc[...] + term

    early = chunks // 2
    for c in range(early):
        project(c)

    settle(meta_in.at[pl.ds(0, R - 1)], meta_recv)
    meta_in[me] = meta_out[me]

    slot_rows = lax.broadcasted_iota(jnp.int32, (R, 128), 0)
    lens = jnp.zeros((R, 128), jnp.int32)
    msg_row = lax.broadcasted_iota(jnp.int32, (MSG, 128), 0)
    lane = lax.broadcasted_iota(jnp.int32, (MSG, 128), 1)
    for o in range(R):
        tile = meta_in[o]
        slot = tile & (R - 1)
        slot_wide = jnp.concatenate([slot] * (R // 8), 0)
        len_wide = jnp.concatenate([lax.shift_right_logical(tile, int(math.log2(R)))] * (R // 8), 0)
        lens = jnp.where(slot_rows == slot_wide, len_wide, lens)
        target = R * msg_row + jnp.concatenate([slot] * (MSG // 8), 0)
        for c in range(0, NH * M, 128):
            width = min(128, NH * M - c)
            hit = jnp.where(target == lane + c, 1.0, 0.0).astype(BF16)
            pick[pl.ds(o * MSG, MSG), c : c + width] = hit[:, :width]
    freq_lane = lax.broadcasted_iota(jnp.int32, (8, 128), 1) % (HD // 2)
    freq = jnp.exp(freq_lane.astype(F32) * (-2.0 / HD * math.log(ROPE_BASE)))
    angle = lens.astype(F32) * jnp.concatenate([freq] * (R // 8), 0)
    cos_len, sin_len = jnp.cos(angle), jnp.sin(angle)
    sign = jnp.where(lax.broadcasted_iota(jnp.int32, (R, 128), 1) < HD // 2, -1.0, 1.0)
    cosines, sines = [], []
    for s in range(S):
        if s == 0:
            cosines.append(cos_len)
            sines.append(sin_len * sign)
            continue
        cos_s = jnp.concatenate([jnp.cos(freq * float(s))] * (R // 8), 0)
        sin_s = jnp.concatenate([jnp.sin(freq * float(s))] * (R // 8), 0)
        cosines.append(cos_len * cos_s - sin_len * sin_s)
        sines.append((sin_len * cos_s + cos_len * sin_s) * sign)
    cosine = jnp.concatenate(cosines, 0)
    sine = jnp.concatenate(sines, 0)

    for c in range(early, chunks):
        project(c)

    for h in range(NH):
        vec = acc[:, h * HD : (h + 1) * HD]
        if h <= NQ:
            vec = vec * cosine + pltpu.roll(vec, HD // 2, 1) * sine
        stack[h * M : (h + 1) * M, :] = vec.astype(BF16)
    q_out[...] = jnp.dot(pick[...], stack[...], preferred_element_type=F32).astype(BF16).reshape(R, MSG, HD)

    def q_copy(o):
        return pltpu.make_async_remote_copy(
            src_ref=q_out.at[o], dst_ref=q_in.at[me], send_sem=q_send, recv_sem=q_recv.at[me],
            device_id={"replica": o}, device_id_type=MESH,
        )

    to_all(q_copy)
    q_in[me] = q_out[me]
    wo_copy = pltpu.make_async_copy(wo_hbm, wo, wo_sem)
    wo_copy.start()

    per = 128 // MSG
    group_of_lane = lax.broadcasted_iota(jnp.int32, (8, 128), 1) // MSG
    row_of_lane = lax.broadcasted_iota(jnp.int32, (8, 128), 1) % MSG
    wide_row = lax.broadcasted_iota(jnp.int32, (NQ * M, 128), 0)
    for g in range(R // per):
        slots = jnp.zeros((8, 128), jnp.int32)
        for i in range(per):
            slots = jnp.where(group_of_lane == i, meta_in[g * per + i] & (R - 1), slots)
        target = jnp.concatenate([R * row_of_lane + slots] * (NQ * M // 8), 0)
        unpick[:, g * 128 : (g + 1) * 128] = jnp.where(target == wide_row, 1.0, 0.0).astype(BF16)

    code_copy.wait()
    for copy in kv_copies:
        copy.wait()

    span = max_pages * page
    rows = GROUP * MSG
    tok = lax.broadcasted_iota(jnp.int32, (MSG, span), 1)
    f_row = lax.broadcasted_iota(jnp.int32, (rows, rows), 0)
    f_col = lax.broadcasted_iota(jnp.int32, (rows, rows), 1)
    f_key = f_col % MSG - NQ * S
    fresh_ok = (f_row // MSG == f_col // MSG) & (f_key >= 0) & (f_key <= f_row % S)
    factor = math.log2(math.e) / math.sqrt(HD)
    dims = (((1,), (1,)), ((), ()))

    def attend(g):
        first = g * GROUP
        q = q_in[pl.ds(first, GROUP)].reshape(rows, HD)
        fresh = lax.dot_general(q, q, dims, preferred_element_type=F32)
        fresh = jnp.where(fresh_ok, fresh, -jnp.inf)
        places, scores = [], []
        for u in range(GROUP):
            word = code_sm[first + u, 0]
            slot = word & (R - 1)
            length = lax.shift_right_logical(word, int(math.log2(R)))
            places.append([table_sm[p, slot] for p in range(max_pages)])
            keys = jnp.concatenate([kv[at, 0] for at in places[u]], 0)
            sc = lax.dot_general(q[u * MSG : (u + 1) * MSG], keys, dims, preferred_element_type=F32)
            scores.append(jnp.where(tok < length, sc, -jnp.inf))
        values = pltpu.roll(q.astype(F32), rows - S, 0).astype(BF16)
        for u in range(GROUP):
            mine = slice(u * MSG, (u + 1) * MSG)
            peak = jnp.maximum(
                jnp.max(scores[u], 1, keepdims=True), jnp.max(fresh[mine], 1, keepdims=True)
            )
            w_fresh = jnp.exp2((fresh[mine] - peak) * factor).astype(BF16)
            w = jnp.exp2((scores[u] - peak) * factor).astype(BF16)
            total = jnp.dot(w_fresh, values, preferred_element_type=F32)
            cached = jnp.concatenate([kv[at, 1] for at in places[u]], 0)
            total = total + jnp.dot(w, cached, preferred_element_type=F32)
            denom = jnp.sum(w.astype(F32), 1, keepdims=True) + jnp.sum(
                w_fresh.astype(F32), 1, keepdims=True
            )
            h_out[first + u] = (total / denom).astype(BF16)

    def wait_q(n):
        settle(q_in.at[n], q_recv.at[n])

    def heads_copy(n):
        return pltpu.make_async_remote_copy(
            src_ref=h_out.at[n], dst_ref=h_in.at[me], send_sem=h_send, recv_sem=h_recv,
            device_id={"replica": n}, device_id_type=MESH,
        )

    def attend_group(i, carry):
        g = mod(group - 1 - i, groups)
        for u in range(GROUP):
            n = g * GROUP + u

            @pl.when(n != me)
            def _():
                wait_q(n)

        attend(g)
        for u in range(GROUP):
            n = g * GROUP + u

            @pl.when(n != me)
            def _():
                heads_copy(n).start()

        return carry

    lax.fori_loop(0, groups, attend_group, 0, unroll=2)
    h_in[me] = h_out[me]

    wo_copy.wait()
    settle(h_in.at[pl.ds(0, R - 1)], h_recv)
    flat = h_in[...].reshape(R * MSG, HD)
    by_head = jnp.dot(unpick[...], flat, preferred_element_type=F32).astype(BF16)
    for h in range(NQ):
        heads[:, h * HD : (h + 1) * HD] = by_head[h * M : (h + 1) * M]

    wide = DC // SUBS

    def cols_of(c, b):
        return pl.ds(pl.multiple_of(c * DC + b * wide, 128), wide)

    def partial(c, b):
        return jnp.dot(heads[...], wo[:, cols_of(c, b)], preferred_element_type=F32)

    def push(src, dst, b, i, other):
        copy = pltpu.make_async_remote_copy(
            src_ref=src, dst_ref=dst, send_sem=x_send.at[b, i], recv_sem=x_recv.at[b, i],
            device_id={"tensor": other}, device_id_type=MESH,
        )
        copy.start()
        return copy

    low, high = slice(0, half), slice(half, M)
    subs = range(SUBS)
    c0, c1, c2, c3, c4, c5, c6, c7, c8, c9 = ([] for _ in range(10))
    for b in subs:
        far[b] = partial(mod(tx + 2, T), b).astype(BF16)
        c0.append(push(far.at[b, low], got.at[b, 0], b, 0, right))
        c1.append(push(far.at[b, high], got.at[b, 1], b, 1, left))
    for b in subs:
        sums_r[b] = partial(right, b)
        near_r[b, high] = sums_r[b, high].astype(BF16)
        sums_l[b] = partial(left, b)
        near_l[b, low] = sums_l[b, low].astype(BF16)
    for b in subs:
        part[b] = partial(tx, b)
    for b in subs:
        c0[b].wait_send()
        c2.append(push(near_r.at[b, high], got.at[b, 2], b, 2, right))
        c1[b].wait_send()
        c3.append(push(near_l.at[b, low], got.at[b, 3], b, 3, left))
    for b in subs:
        c0[b].wait_recv()
        near_r[b, low] = (sums_r[b, low] + got[b, 0].astype(F32)).astype(BF16)
        c2[b].wait_send()
        c4.append(push(near_r.at[b, low], got.at[b, 4], b, 4, right))
        c1[b].wait_recv()
        near_l[b, high] = (sums_l[b, high] + got[b, 1].astype(F32)).astype(BF16)
        c3[b].wait_send()
        c5.append(push(near_l.at[b, high], got.at[b, 5], b, 5, left))
    own = []
    for b in subs:
        mine = out_hbm.at[:, cols_of(tx, b)]
        c3[b].wait_recv()
        c4[b].wait_recv()
        final[b, low] = (part[b, low] + got[b, 3].astype(F32) + got[b, 4].astype(F32)).astype(BF16)
        c6.append(push(final.at[b, low], mine.at[low], b, 6, right))
        c2[b].wait_recv()
        c5[b].wait_recv()
        final[b, high] = (part[b, high] + got[b, 2].astype(F32) + got[b, 5].astype(F32)).astype(BF16)
        c7.append(push(final.at[b, high], mine.at[high], b, 7, left))
        c8.append(push(final.at[b, high], mine.at[high], b, 8, right))
        c9.append(push(final.at[b, low], mine.at[low], b, 9, left))
        own.append(pltpu.make_async_copy(final.at[b], mine, out_sem.at[b]))
        own[b].start()
    last = []
    for b in subs:
        from_left = out_hbm.at[low, cols_of(left, b)]
        from_right = out_hbm.at[high, cols_of(right, b)]
        c6[b].wait_recv()
        last.append(push(from_left, from_left, b, 10, right))
        c7[b].wait_recv()
        last.append(push(from_right, from_right, b, 11, left))
    for copy in c8 + c9 + last:
        copy.wait_recv()
    for copy in c4 + c5 + c6 + c7 + c8 + c9 + last:
        copy.wait_send()
    for copy in own:
        copy.wait()
    some = pl.ds(0, R - 1)
    settle(meta_out.at[some], meta_send)
    settle(q_out.at[some], q_send)
    settle(h_out.at[some], h_send)


def shards(
    replicas, tensors, hidden_in, norm_gain, w_query, w_key, w_value, w_out, kv_pages, lengths, page_table, destination
):
    S, R, D = hidden_in.shape
    T = tensors
    NQ = w_query.shape[1] // HD
    NH = NQ + 2
    M = S * R
    KC = min(1024, D // 2)
    DC = D // T
    pages, _, page, _ = kv_pages.shape
    any_spec = pl.BlockSpec(memory_space=pl.ANY)
    smem = pl.BlockSpec(memory_space=pltpu.SMEM)
    dma = pltpu.SemaphoreType.DMA
    out = pl.pallas_call(
        functools.partial(kernel, (R, T, S, NQ, D, KC)),
        out_shape=jax.ShapeDtypeStruct((M, D), BF16),
        in_specs=[smem, smem, smem, pl.BlockSpec(memory_space=pltpu.VMEM)] + [any_spec] * 6,
        out_specs=any_spec,
        scratch_shapes=[
            pltpu.VMEM((M, D), BF16),
            pltpu.VMEM((D, NQ * HD), BF16),
            pltpu.VMEM((D, HD), BF16),
            pltpu.VMEM((D, HD), BF16),
            pltpu.VMEM(kv_pages.shape, BF16),
            pltpu.VMEM(w_out.shape, BF16),
            pltpu.VMEM((M, NH * HD), F32),
            pltpu.VMEM((R, 128), jnp.int32),
            pltpu.SMEM((R, 128), jnp.int32),
            pltpu.VMEM((R, 8, 128), jnp.int32),
            pltpu.VMEM((R, 8, 128), jnp.int32),
            pltpu.VMEM((R * MSG, NH * M), BF16),
            pltpu.VMEM((NQ * M, R * MSG), BF16),
            pltpu.VMEM((NH * M, HD), BF16),
            pltpu.VMEM((R, MSG, HD), BF16),
            pltpu.VMEM((R, MSG, HD), BF16),
            pltpu.VMEM((R, MSG, HD), BF16),
            pltpu.VMEM((R, MSG, HD), BF16),
            pltpu.VMEM((M, NQ * HD), BF16),
            pltpu.VMEM((SUBS, M, DC // SUBS), F32),
            pltpu.VMEM((SUBS, M, DC // SUBS), F32),
            pltpu.VMEM((SUBS, M, DC // SUBS), F32),
            pltpu.VMEM((SUBS, M, DC // SUBS), BF16),
            pltpu.VMEM((SUBS, M, DC // SUBS), BF16),
            pltpu.VMEM((SUBS, M, DC // SUBS), BF16),
            pltpu.VMEM((SUBS, 6, M // 2, DC // SUBS), BF16),
            pltpu.VMEM((SUBS, M, DC // SUBS), BF16),
            dma, dma((D // KC, 3)), dma((4,)), dma, dma,
            dma, dma, dma, dma((R,)), dma, dma, dma((SUBS, 12)), dma((SUBS, 12)), dma((SUBS,)),
        ],
        compiler_params=pltpu.CompilerParams(
            collective_id=0, has_side_effects=True, vmem_limit_bytes=58 * 1024 * 1024
        ),
        name="decode_attention",
    )(
        destination, lengths, page_table.T, norm_gain.reshape(1, D), hidden_in.reshape(M, D),
        w_query, w_key, w_value, w_out, kv_pages,
    )
    return out.reshape(S, R, D)


def solution(mesh):
    in_specs = (
        P(None, "replica", None),
        P(),
        P(None, "tensor"),
        P(None, "tensor"),
        P(None, "tensor"),
        P("tensor", None),
        P("replica", None, None, "tensor"),
        P("replica"),
        P("replica", None),
        P("replica"),
    )
    body = functools.partial(shards, mesh.shape["replica"], mesh.shape["tensor"])
    return jax.shard_map(
        body, mesh=mesh, in_specs=in_specs, out_specs=P(None, "replica", None), check_vma=False
    )
```

```python
import functools
import math

import jax
import jax.numpy as jnp
from jax import lax
from jax.experimental import pallas as pl
from jax.experimental.pallas import tpu as pltpu
from jax.sharding import PartitionSpec as P

HD = 128
GROUP = 4
MSG = 32
ROPE_BASE = 1000000.0
EPSILON = 1e-06
SUBS = 2
CHIPS_Z = 4
MESH = pl.DeviceIdType.MESH
F32 = jnp.float32
BF16 = jnp.bfloat16


def mod(value, size):
    return lax.rem(value + 2 * size, size)


def settle(ref, sem):
    pltpu.make_async_copy(ref, ref, sem).wait()


def kernel(
    sizes,
    dest_sm, len_sm, table_sm, gain_ref, hid_hbm, wq_hbm, wk_hbm, wv_hbm, wo_hbm, kv_hbm,
    out_ref,
    hid, wq, wk, wv, kv, wf, relay, acc, code, code_sm, meta_out, meta_in, pick, unpick, stack,
    q_out, q_in, h_out, h_in, heads, total,
    hid_sem, w_sem, kv_sem, wo_sem, code_sem,
    meta_send, meta_recv, q_send, q_recv, h_send, h_recv, x_send, x_recv, f_send, f_recv,
):
    R, T, S, NQ, D, KC = sizes
    M = S * R
    NH = NQ + 2
    me = lax.axis_index("replica")
    tx = lax.axis_index("tensor")
    chunks = D // KC
    group = me // GROUP
    groups = R // GROUP
    DC = D // T
    half = M // 2
    pages = kv.shape[0]
    max_pages = pages // R
    page = kv.shape[2]
    KR = wo_hbm.shape[0]
    HB, QB = KR // 2, KR // 8
    HC = DC // 2
    core = me % 2
    mate = me + 1 - 2 * core
    chip = me // 2
    z, y = chip % CHIPS_Z, chip // CHIPS_Z
    chips_y = R // (2 * CHIPS_Z)
    parity = (y + z) % 2
    opposite = mod(tx + 2, T)

    def at(yy, zz):
        return (mod(yy, chips_y) * CHIPS_Z + mod(zz, CHIPS_Z)) * 2 + core

    around = (at(y + 1, z), at(y - 1, z), at(y, z + 1), at(y, z - 1))

    def rows_at(owner, first, size):
        return pl.ds(pl.multiple_of(owner * KR + first, 16), size)

    half_cols = pl.ds(pl.multiple_of(core * HC, 128), HC)

    def own_rows(target, first, size):
        cols = pl.ds(pl.multiple_of(target * DC + core * HC, 128), HC)
        return wo_hbm.at[pl.ds(pl.multiple_of(first, 16), size), cols]

    def weight_piece(src, dst, i, other):
        return pltpu.make_async_remote_copy(
            src_ref=src, dst_ref=dst, send_sem=f_send.at[i], recv_sem=f_recv.at[i],
            device_id=other, device_id_type=MESH,
        )

    def held(owner, first, size):
        return wf.at[rows_at(owner, first, size), half_cols]

    def same_place(owner, first, size, i, other):
        return weight_piece(held(owner, first, size), held(owner, first, size), i, {"replica": other})

    right = mod(tx + 1, T)
    left = mod(tx - 1, T)
    fetched, missing = parity * HB, (1 - parity) * HB
    QH2 = HB // 2
    far_a = weight_piece(own_rows(opposite, fetched, QH2), relay.at[0], 0, {"tensor": right})
    far_b = weight_piece(own_rows(opposite, fetched + QH2, QH2), relay.at[1], 1, {"tensor": left})
    near_a = weight_piece(own_rows(right, fetched, HB), held(tx, fetched, HB), 2, {"tensor": right})
    near_b = weight_piece(own_rows(left, fetched, HB), held(tx, fetched, HB), 3, {"tensor": left})
    pass_a = weight_piece(relay.at[0], held(left, fetched, QH2), 4, {"tensor": right})
    pass_b = weight_piece(relay.at[1], held(right, fetched + QH2, QH2), 5, {"tensor": left})
    owners = (left, right, opposite)
    spread = [
        [same_place(owner, fetched + e * QB, QB, 6 + 4 * j + e, around[e]) for e in range(4)]
        for j, owner in enumerate(owners)
    ]
    to_mate = [same_place(owner, fetched, HB, 18 + j, mate) for j, owner in enumerate(owners)]
    rest_to_mate = [same_place(owner, missing, HB, 21 + j, mate) for j, owner in enumerate(owners)]

    def weight_copies(c):
        rows = pl.ds(pl.multiple_of(c * KC, KC), KC)
        return (
            pltpu.make_async_copy(wq_hbm.at[rows], wq.at[rows], w_sem.at[c, 0]),
            pltpu.make_async_copy(wk_hbm.at[rows], wk.at[rows], w_sem.at[c, 1]),
            pltpu.make_async_copy(wv_hbm.at[rows], wv.at[rows], w_sem.at[c, 2]),
        )

    hid_copy = pltpu.make_async_copy(hid_hbm, hid, hid_sem)
    hid_copy.start()
    def load(c):
        if c < chunks:
            for copy in weight_copies(c):
                copy.start()

    load(0)
    load(1)

    barrier = pltpu.get_barrier_semaphore()

    def greet(k, carry):
        pl.semaphore_signal(barrier, inc=1, device_id={"replica": mod(me + k, R)}, device_id_type=MESH)
        return carry

    lax.fori_loop(1, R, greet, 0)
    for other in (right, left):
        pl.semaphore_signal(barrier, inc=1, device_id={"tensor": other}, device_id_type=MESH)

    numbers = lax.broadcasted_iota(jnp.int32, (R, 128), 0)
    codes = jnp.zeros((R, 128), jnp.int32)
    for b in range(R):
        codes = jnp.where(numbers == dest_sm[b], len_sm[b] * R + b, codes)
    code[...] = codes
    code_copy = pltpu.make_async_copy(code, code_sm, code_sem)
    code_copy.start()
    for n in range(R):
        meta_out[n] = jnp.broadcast_to(codes[n : n + 1], (8, 128))

    pl.semaphore_wait(barrier, R - 1 + 2)
    far_a.start()
    far_b.start()

    def to_all(make):
        def send(k, carry):
            n = mod(group * GROUP + GROUP + k, R)

            @pl.when(n != me)
            def _():
                make(n).start()

            return carry

        lax.fori_loop(0, R, send, 0)

    def meta_copy(n):
        return pltpu.make_async_remote_copy(
            src_ref=meta_out.at[n], dst_ref=meta_in.at[me], send_sem=meta_send, recv_sem=meta_recv,
            device_id={"replica": n}, device_id_type=MESH,
        )

    to_all(meta_copy)

    hid_copy.wait()
    load(2)
    squares = jnp.zeros((M, 128), F32)
    for c in range(D // 128):
        wide = hid[:, c * 128 : (c + 1) * 128].astype(F32)
        squares = squares + wide * wide
    load(3)
    scale = lax.rsqrt(jnp.sum(squares, 1, keepdims=True) * (1.0 / D) + EPSILON)

    for c in range(0, D, 512):
        cols = slice(c, c + 512)
        hid[:, cols] = (hid[:, cols].astype(F32) * scale * gain_ref[:, cols]).astype(BF16)

    for c in range(4, chunks):
        load(c)
    kv_copies = []
    step = pages // 4
    for c in range(4):
        rows = pl.ds(c * step, step)
        kv_copies.append(pltpu.make_async_copy(kv_hbm.at[rows], kv.at[rows], kv_sem.at[c]))

    def project(c):
        for copy in weight_copies(c):
            copy.wait()
        if c + 1 == chunks:
            for copy in kv_copies:
                copy.start()
        cols = slice(c * KC, (c + 1) * KC)
        weights = jnp.concatenate([wq[cols], wk[cols], wv[cols]], 1)
        term = jnp.dot(hid[:, cols], weights, preferred_element_type=F32)
        acc[...] = term if c == 0 else acc[...] + term

    early = chunks // 2
    for c in range(early):
        project(c)
    near_a.start()
    near_b.start()

    settle(meta_in.at[pl.ds(0, R - 1)], meta_recv)
    meta_in[me] = meta_out[me]

    slot_rows = lax.broadcasted_iota(jnp.int32, (R, 128), 0)
    lens = jnp.zeros((R, 128), jnp.int32)
    msg_row = lax.broadcasted_iota(jnp.int32, (MSG, 128), 0)
    lane = lax.broadcasted_iota(jnp.int32, (MSG, 128), 1)
    for o in range(R):
        tile = meta_in[o]
        slot = tile & (R - 1)
        slot_wide = jnp.concatenate([slot] * (R // 8), 0)
        len_wide = jnp.concatenate([lax.shift_right_logical(tile, int(math.log2(R)))] * (R // 8), 0)
        lens = jnp.where(slot_rows == slot_wide, len_wide, lens)
        target = R * msg_row + jnp.concatenate([slot] * (MSG // 8), 0)
        for c in range(0, NH * M, 128):
            width = min(128, NH * M - c)
            hit = jnp.where(target == lane + c, 1.0, 0.0).astype(BF16)
            pick[pl.ds(o * MSG, MSG), c : c + width] = hit[:, :width]
    freq_lane = lax.broadcasted_iota(jnp.int32, (8, 128), 1) % (HD // 2)
    freq = jnp.exp(freq_lane.astype(F32) * (-2.0 / HD * math.log(ROPE_BASE)))
    angle = lens.astype(F32) * jnp.concatenate([freq] * (R // 8), 0)
    cos_len, sin_len = jnp.cos(angle), jnp.sin(angle)
    sign = jnp.where(lax.broadcasted_iota(jnp.int32, (R, 128), 1) < HD // 2, -1.0, 1.0)
    cosines, sines = [], []
    for s in range(S):
        if s == 0:
            cosines.append(cos_len)
            sines.append(sin_len * sign)
            continue
        cos_s = jnp.concatenate([jnp.cos(freq * float(s))] * (R // 8), 0)
        sin_s = jnp.concatenate([jnp.sin(freq * float(s))] * (R // 8), 0)
        cosines.append(cos_len * cos_s - sin_len * sin_s)
        sines.append((sin_len * cos_s + cos_len * sin_s) * sign)
    cosine = jnp.concatenate(cosines, 0)
    sine = jnp.concatenate(sines, 0)

    for c in range(early, chunks):
        project(c)

    for h in range(NH):
        vec = acc[:, h * HD : (h + 1) * HD]
        if h <= NQ:
            vec = vec * cosine + pltpu.roll(vec, HD // 2, 1) * sine
        stack[h * M : (h + 1) * M, :] = vec.astype(BF16)
    q_out[...] = jnp.dot(pick[...], stack[...], preferred_element_type=F32).astype(BF16).reshape(R, MSG, HD)

    def q_copy(o):
        return pltpu.make_async_remote_copy(
            src_ref=q_out.at[o], dst_ref=q_in.at[me], send_sem=q_send, recv_sem=q_recv.at[me],
            device_id={"replica": o}, device_id_type=MESH,
        )

    to_all(q_copy)
    q_in[me] = q_out[me]
    wo_copy = pltpu.make_async_copy(
        wo_hbm.at[:, pl.ds(pl.multiple_of(tx * DC, 128), DC)], wf.at[rows_at(tx, 0, KR)], wo_sem
    )
    wo_copy.start()
    far_a.wait_recv()
    pass_a.start()
    far_b.wait_recv()
    pass_b.start()

    per = 128 // MSG
    group_of_lane = lax.broadcasted_iota(jnp.int32, (8, 128), 1) // MSG
    row_of_lane = lax.broadcasted_iota(jnp.int32, (8, 128), 1) % MSG
    wide_row = lax.broadcasted_iota(jnp.int32, (NQ * M, 128), 0)
    for g in range(R // per):
        slots = jnp.zeros((8, 128), jnp.int32)
        for i in range(per):
            slots = jnp.where(group_of_lane == i, meta_in[g * per + i] & (R - 1), slots)
        target = jnp.concatenate([R * row_of_lane + slots] * (NQ * M // 8), 0)
        unpick[:, g * 128 : (g + 1) * 128] = jnp.where(target == wide_row, 1.0, 0.0).astype(BF16)

    code_copy.wait()
    for copy in kv_copies:
        copy.wait()

    span = max_pages * page
    rows = GROUP * MSG
    tok = lax.broadcasted_iota(jnp.int32, (MSG, span), 1)
    f_row = lax.broadcasted_iota(jnp.int32, (rows, rows), 0)
    f_col = lax.broadcasted_iota(jnp.int32, (rows, rows), 1)
    f_key = f_col % MSG - NQ * S
    fresh_ok = (f_row // MSG == f_col // MSG) & (f_key >= 0) & (f_key <= f_row % S)
    factor = math.log2(math.e) / math.sqrt(HD)
    dims = (((1,), (1,)), ((), ()))

    def attend(g):
        first = g * GROUP
        q = q_in[pl.ds(first, GROUP)].reshape(rows, HD)
        fresh = lax.dot_general(q, q, dims, preferred_element_type=F32)
        fresh = jnp.where(fresh_ok, fresh, -jnp.inf)
        places, scores = [], []
        for u in range(GROUP):
            word = code_sm[first + u, 0]
            slot = word & (R - 1)
            length = lax.shift_right_logical(word, int(math.log2(R)))
            places.append([table_sm[p, slot] for p in range(max_pages)])
            keys = jnp.concatenate([kv[at, 0] for at in places[u]], 0)
            sc = lax.dot_general(q[u * MSG : (u + 1) * MSG], keys, dims, preferred_element_type=F32)
            scores.append(jnp.where(tok < length, sc, -jnp.inf))
        values = pltpu.roll(q.astype(F32), rows - S, 0).astype(BF16)
        for u in range(GROUP):
            mine = slice(u * MSG, (u + 1) * MSG)
            peak = jnp.maximum(
                jnp.max(scores[u], 1, keepdims=True), jnp.max(fresh[mine], 1, keepdims=True)
            )
            w_fresh = jnp.exp2((fresh[mine] - peak) * factor).astype(BF16)
            w = jnp.exp2((scores[u] - peak) * factor).astype(BF16)
            total = jnp.dot(w_fresh, values, preferred_element_type=F32)
            cached = jnp.concatenate([kv[at, 1] for at in places[u]], 0)
            total = total + jnp.dot(w, cached, preferred_element_type=F32)
            denom = jnp.sum(w.astype(F32), 1, keepdims=True) + jnp.sum(
                w_fresh.astype(F32), 1, keepdims=True
            )
            h_out[first + u] = (total / denom).astype(BF16)

    def wait_q(n):
        settle(q_in.at[n], q_recv.at[n])

    def heads_copy(n):
        return pltpu.make_async_remote_copy(
            src_ref=h_out.at[n], dst_ref=h_in.at[me], send_sem=h_send, recv_sem=h_recv,
            device_id={"replica": n}, device_id_type=MESH,
        )

    def attend_group(i, carry):
        g = mod(group - 1 - i, groups)
        for u in range(GROUP):
            n = g * GROUP + u

            @pl.when(n != me)
            def _():
                wait_q(n)

        attend(g)
        for u in range(GROUP):
            n = g * GROUP + u

            @pl.when(n != me)
            def _():
                heads_copy(n).start()

        return carry

    lax.fori_loop(0, groups // 2, attend_group, 0, unroll=2)
    near_a.wait_recv()
    near_b.wait_recv()
    for j in (0, 1):
        to_mate[j].start()
        for e in range(4):
            spread[j][e].start()
    lax.fori_loop(groups // 2, groups, attend_group, 0, unroll=2)
    h_in[me] = h_out[me]
    pass_a.wait_recv()
    pass_b.wait_recv()
    to_mate[2].start()
    for e in range(4):
        spread[2][e].start()

    settle(h_in.at[pl.ds(0, R - 1)], h_recv)
    flat = h_in[...].reshape(R * MSG, HD)
    by_head = jnp.dot(unpick[...], flat, preferred_element_type=F32).astype(BF16)
    for h in range(NQ):
        heads[tx, :, h * HD : (h + 1) * HD] = by_head[h * M : (h + 1) * M]

    def push(ref, i, other):
        copy = pltpu.make_async_remote_copy(
            src_ref=ref, dst_ref=ref, send_sem=x_send.at[i], recv_sem=x_recv.at[i],
            device_id={"tensor": other}, device_id_type=MESH,
        )
        copy.start()
        return copy

    low, high = pl.ds(0, half), pl.ds(half, half)
    g0 = push(heads.at[tx, low], 0, right)
    g1 = push(heads.at[tx, high], 1, left)
    g2 = push(heads.at[tx, high], 2, right)
    g3 = push(heads.at[tx, low], 3, left)

    def term(owner, cols):
        rows = pl.ds(pl.multiple_of(owner * KR, 16), KR)
        return jnp.dot(heads[owner], wf[rows, cols], preferred_element_type=F32)

    every = slice(0, DC)
    wo_copy.wait()
    total[...] = term(tx, every)
    for j in range(3):
        for e in range(4):
            spread[j][e].wait_recv()
        rest_to_mate[j].start()
    g0.wait_recv()
    g4 = push(heads.at[left, low], 4, right)
    g1.wait_recv()
    g5 = push(heads.at[right, high], 5, left)
    g2.wait_recv()
    to_mate[0].wait_recv()
    rest_to_mate[0].wait_recv()
    total[...] += term(left, every)
    g3.wait_recv()
    to_mate[1].wait_recv()
    rest_to_mate[1].wait_recv()
    total[...] += term(right, every)
    to_mate[2].wait_recv()
    rest_to_mate[2].wait_recv()
    g4.wait_recv()
    g5.wait_recv()

    wide = DC // SUBS

    def cols_of(owner, b):
        return pl.ds(pl.multiple_of(owner * DC + b * wide, 128), wide)

    done = [g0, g1, g2, g3, g4, g5]
    first_r, first_l, second = [], [], []
    for b in range(SUBS):
        part = slice(b * wide, (b + 1) * wide)
        mine = cols_of(tx, b)
        out_ref[:, mine] = (total[:, part] + term(opposite, part)).astype(BF16)
        i = 6 + 6 * b
        first_r.append(push(out_ref.at[low, mine], i, right))
        first_l.append(push(out_ref.at[high, mine], i + 1, left))
        second.append(push(out_ref.at[high, mine], i + 2, right))
        second.append(push(out_ref.at[low, mine], i + 3, left))
    for b in range(SUBS):
        i = 6 + 6 * b
        first_r[b].wait_recv()
        second.append(push(out_ref.at[low, cols_of(left, b)], i + 4, right))
        first_l[b].wait_recv()
        second.append(push(out_ref.at[high, cols_of(right, b)], i + 5, left))
    for copy in second:
        copy.wait_recv()
    for copy in done + first_r + first_l + second:
        copy.wait_send()
    for copy in [far_a, far_b, near_a, near_b, pass_a, pass_b] + sum(spread, []) + to_mate + rest_to_mate:
        copy.wait_send()
    some = pl.ds(0, R - 1)
    settle(meta_out.at[some], meta_send)
    settle(q_out.at[some], q_send)
    settle(h_out.at[some], h_send)


def shards(
    replicas, tensors, hidden_in, norm_gain, w_query, w_key, w_value, w_out, kv_pages, lengths, page_table, destination
):
    S, R, D = hidden_in.shape
    T = tensors
    NQ = w_query.shape[1] // HD
    NH = NQ + 2
    M = S * R
    KC = min(1024, D // 2)
    DC = D // T
    pages, _, page, _ = kv_pages.shape
    any_spec = pl.BlockSpec(memory_space=pl.ANY)
    smem = pl.BlockSpec(memory_space=pltpu.SMEM)
    dma = pltpu.SemaphoreType.DMA
    out = pl.pallas_call(
        functools.partial(kernel, (R, T, S, NQ, D, KC)),
        out_shape=pltpu.VMEM((M, D), BF16),
        in_specs=[smem, smem, smem, pl.BlockSpec(memory_space=pltpu.VMEM)] + [any_spec] * 6,
        out_specs=pl.BlockSpec(memory_space=pltpu.VMEM),
        scratch_shapes=[
            pltpu.VMEM((M, D), BF16),
            pltpu.VMEM((D, NQ * HD), BF16),
            pltpu.VMEM((D, HD), BF16),
            pltpu.VMEM((D, HD), BF16),
            pltpu.VMEM(kv_pages.shape, BF16),
            pltpu.VMEM((T * w_out.shape[0], DC), BF16),
            pltpu.VMEM((2, w_out.shape[0] // 4, DC // 2), BF16),
            pltpu.VMEM((M, NH * HD), F32),
            pltpu.VMEM((R, 128), jnp.int32),
            pltpu.SMEM((R, 128), jnp.int32),
            pltpu.VMEM((R, 8, 128), jnp.int32),
            pltpu.VMEM((R, 8, 128), jnp.int32),
            pltpu.VMEM((R * MSG, NH * M), BF16),
            pltpu.VMEM((NQ * M, R * MSG), BF16),
            pltpu.VMEM((NH * M, HD), BF16),
            pltpu.VMEM((R, MSG, HD), BF16),
            pltpu.VMEM((R, MSG, HD), BF16),
            pltpu.VMEM((R, MSG, HD), BF16),
            pltpu.VMEM((R, MSG, HD), BF16),
            pltpu.VMEM((T, M, NQ * HD), BF16),
            pltpu.VMEM((M, DC), F32),
            dma, dma((D // KC, 3)), dma((4,)), dma, dma,
            dma, dma, dma, dma((R,)), dma, dma, dma((6 + 6 * SUBS,)), dma((6 + 6 * SUBS,)), dma((24,)), dma((24,)),
        ],
        compiler_params=pltpu.CompilerParams(
            collective_id=0, has_side_effects=True, vmem_limit_bytes=58 * 1024 * 1024
        ),
        name="decode_attention",
    )(
        destination, lengths, page_table.T, norm_gain.reshape(1, D), hidden_in.reshape(M, D),
        w_query, w_key, w_value, w_out, kv_pages,
    )
    return out.reshape(S, R, D)


def solution(mesh):
    in_specs = (
        P(None, "replica", None),
        P(),
        P(None, "tensor"),
        P(None, "tensor"),
        P(None, "tensor"),
        P("tensor", None),
        P("replica", None, None, "tensor"),
        P("replica"),
        P("replica", None),
        P("replica"),
    )
    body = functools.partial(shards, mesh.shape["replica"], mesh.shape["tensor"])
    return jax.shard_map(
        body, mesh=mesh, in_specs=in_specs, out_specs=P(None, "replica", None), check_vma=False
    )
```

```python
import functools
import math

import jax
import jax.numpy as jnp
from jax import lax
from jax.experimental import pallas as pl
from jax.experimental.pallas import tpu as pltpu
from jax.sharding import PartitionSpec as P

HD = 128
GROUP = 4
MSG = 32
ROPE_BASE = 1000000.0
EPSILON = 1e-06
SUBS = 2
CHIPS_Z = 4
MESH = pl.DeviceIdType.MESH
F32 = jnp.float32
BF16 = jnp.bfloat16


def mod(value, size):
    return lax.rem(value + 2 * size, size)


def settle(ref, sem):
    pltpu.make_async_copy(ref, ref, sem).wait()


def kernel(
    sizes,
    dest_sm, len_sm, table_sm, gain_ref, hid_hbm, wq_hbm, wk_hbm, wv_hbm, wo_hbm, kv_hbm,
    out_ref,
    hid, wq, wk, wv, kv, wf, relay, acc, code, code_sm, meta_out, meta_in, pick, unpick, stack,
    q_out, q_in, h_out, h_in, heads, total,
    hid_sem, w_sem, kv_sem, wo_sem, code_sem,
    meta_send, meta_recv, q_send, q_recv, h_send, h_recv, x_send, x_recv, f_send, f_recv,
):
    R, T, S, NQ, D, KC = sizes
    M = S * R
    NH = NQ + 2
    me = lax.axis_index("replica")
    tx = lax.axis_index("tensor")
    chunks = D // KC
    group = me // GROUP
    groups = R // GROUP
    DC = D // T
    half = M // 2
    pages = kv.shape[0]
    max_pages = pages // R
    page = kv.shape[2]
    KR = wo_hbm.shape[0]
    HB, QB = KR // 2, KR // 8
    HC = DC // 2
    core = me % 2
    mate = me + 1 - 2 * core
    chip = me // 2
    z, y = chip % CHIPS_Z, chip // CHIPS_Z
    chips_y = R // (2 * CHIPS_Z)
    parity = (y + z) % 2
    opposite = mod(tx + 2, T)

    def at(yy, zz):
        return (mod(yy, chips_y) * CHIPS_Z + mod(zz, CHIPS_Z)) * 2 + core

    around = (at(y + 1, z), at(y - 1, z), at(y, z + 1), at(y, z - 1))

    def rows_at(owner, first, size):
        return pl.ds(pl.multiple_of(owner * KR + first, 16), size)

    half_cols = pl.ds(pl.multiple_of(core * HC, 128), HC)

    def own_rows(target, first, size):
        cols = pl.ds(pl.multiple_of(target * DC + core * HC, 128), HC)
        return wo_hbm.at[pl.ds(pl.multiple_of(first, 16), size), cols]

    def weight_piece(src, dst, i, other):
        return pltpu.make_async_remote_copy(
            src_ref=src, dst_ref=dst, send_sem=f_send.at[i], recv_sem=f_recv.at[i],
            device_id=other, device_id_type=MESH,
        )

    def held(owner, first, size):
        return wf.at[rows_at(owner, first, size), half_cols]

    def same_place(owner, first, size, i, other):
        return weight_piece(held(owner, first, size), held(owner, first, size), i, {"replica": other})

    right = mod(tx + 1, T)
    left = mod(tx - 1, T)
    fetched, missing = parity * HB, (1 - parity) * HB
    QH2 = HB // 2
    far_a = weight_piece(own_rows(opposite, fetched, QH2), relay.at[0], 0, {"tensor": right})
    far_b = weight_piece(own_rows(opposite, fetched + QH2, QH2), relay.at[1], 1, {"tensor": left})
    near_a = weight_piece(own_rows(right, fetched, HB), held(tx, fetched, HB), 2, {"tensor": right})
    near_b = weight_piece(own_rows(left, fetched, HB), held(tx, fetched, HB), 3, {"tensor": left})
    pass_a = weight_piece(relay.at[0], held(left, fetched, QH2), 4, {"tensor": right})
    pass_b = weight_piece(relay.at[1], held(right, fetched + QH2, QH2), 5, {"tensor": left})
    owners = (left, right, opposite)
    spread = [
        [same_place(owner, fetched + e * QB, QB, 6 + 4 * j + e, around[e]) for e in range(4)]
        for j, owner in enumerate(owners)
    ]
    to_mate = [same_place(owner, fetched, HB, 18 + j, mate) for j, owner in enumerate(owners)]
    rest_to_mate = [same_place(owner, missing, HB, 21 + j, mate) for j, owner in enumerate(owners)]

    def weight_copies(c):
        rows = pl.ds(pl.multiple_of(c * KC, KC), KC)
        return (
            pltpu.make_async_copy(wq_hbm.at[rows], wq.at[rows], w_sem.at[c, 0]),
            pltpu.make_async_copy(wk_hbm.at[rows], wk.at[rows], w_sem.at[c, 1]),
            pltpu.make_async_copy(wv_hbm.at[rows], wv.at[rows], w_sem.at[c, 2]),
        )

    hid_copy = pltpu.make_async_copy(hid_hbm, hid, hid_sem)
    hid_copy.start()
    def load(c):
        if c < chunks:
            for copy in weight_copies(c):
                copy.start()

    load(0)
    load(1)

    barrier = pltpu.get_barrier_semaphore()

    def greet(k, carry):
        pl.semaphore_signal(barrier, inc=1, device_id={"replica": mod(me + k, R)}, device_id_type=MESH)
        return carry

    lax.fori_loop(1, R, greet, 0)
    for other in (right, left):
        pl.semaphore_signal(barrier, inc=1, device_id={"tensor": other}, device_id_type=MESH)

    numbers = lax.broadcasted_iota(jnp.int32, (R, 128), 0)
    codes = jnp.zeros((R, 128), jnp.int32)
    for b in range(R):
        codes = jnp.where(numbers == dest_sm[b], len_sm[b] * R + b, codes)
    code[...] = codes
    code_copy = pltpu.make_async_copy(code, code_sm, code_sem)
    code_copy.start()
    for n in range(R):
        meta_out[n] = jnp.broadcast_to(codes[n : n + 1], (8, 128))

    pl.semaphore_wait(barrier, R - 1 + 2)
    near_a.start()
    near_b.start()

    def to_all(make):
        def send(k, carry):
            n = mod(group * GROUP + GROUP + k, R)

            @pl.when(n != me)
            def _():
                make(n).start()

            return carry

        lax.fori_loop(0, R, send, 0)

    def meta_copy(n):
        return pltpu.make_async_remote_copy(
            src_ref=meta_out.at[n], dst_ref=meta_in.at[me], send_sem=meta_send, recv_sem=meta_recv,
            device_id={"replica": n}, device_id_type=MESH,
        )

    to_all(meta_copy)

    hid_copy.wait()
    load(2)
    squares = jnp.zeros((M, 128), F32)
    for c in range(D // 128):
        wide = hid[:, c * 128 : (c + 1) * 128].astype(F32)
        squares = squares + wide * wide
    load(3)
    scale = lax.rsqrt(jnp.sum(squares, 1, keepdims=True) * (1.0 / D) + EPSILON)

    for c in range(0, D, 512):
        cols = slice(c, c + 512)
        hid[:, cols] = (hid[:, cols].astype(F32) * scale * gain_ref[:, cols]).astype(BF16)

    for c in range(4, chunks):
        load(c)
    kv_copies = []
    step = pages // 4
    for c in range(4):
        rows = pl.ds(c * step, step)
        kv_copies.append(pltpu.make_async_copy(kv_hbm.at[rows], kv.at[rows], kv_sem.at[c]))

    def project(c):
        for copy in weight_copies(c):
            copy.wait()
        if c + 1 == chunks:
            for copy in kv_copies:
                copy.start()
        cols = slice(c * KC, (c + 1) * KC)
        weights = jnp.concatenate([wq[cols], wk[cols], wv[cols]], 1)
        term = jnp.dot(hid[:, cols], weights, preferred_element_type=F32)
        acc[...] = term if c == 0 else acc[...] + term

    early = chunks // 2
    for c in range(early):
        project(c)
    far_a.start()
    far_b.start()

    settle(meta_in.at[pl.ds(0, R - 1)], meta_recv)
    meta_in[me] = meta_out[me]

    slot_rows = lax.broadcasted_iota(jnp.int32, (R, 128), 0)
    lens = jnp.zeros((R, 128), jnp.int32)
    msg_row = lax.broadcasted_iota(jnp.int32, (MSG, 128), 0)
    lane = lax.broadcasted_iota(jnp.int32, (MSG, 128), 1)
    for o in range(R):
        tile = meta_in[o]
        slot = tile & (R - 1)
        slot_wide = jnp.concatenate([slot] * (R // 8), 0)
        len_wide = jnp.concatenate([lax.shift_right_logical(tile, int(math.log2(R)))] * (R // 8), 0)
        lens = jnp.where(slot_rows == slot_wide, len_wide, lens)
        target = R * msg_row + jnp.concatenate([slot] * (MSG // 8), 0)
        for c in range(0, NH * M, 128):
            width = min(128, NH * M - c)
            hit = jnp.where(target == lane + c, 1.0, 0.0).astype(BF16)
            pick[pl.ds(o * MSG, MSG), c : c + width] = hit[:, :width]
    freq_lane = lax.broadcasted_iota(jnp.int32, (8, 128), 1) % (HD // 2)
    freq = jnp.exp(freq_lane.astype(F32) * (-2.0 / HD * math.log(ROPE_BASE)))
    angle = lens.astype(F32) * jnp.concatenate([freq] * (R // 8), 0)
    cos_len, sin_len = jnp.cos(angle), jnp.sin(angle)
    sign = jnp.where(lax.broadcasted_iota(jnp.int32, (R, 128), 1) < HD // 2, -1.0, 1.0)
    cosines, sines = [], []
    for s in range(S):
        if s == 0:
            cosines.append(cos_len)
            sines.append(sin_len * sign)
            continue
        cos_s = jnp.concatenate([jnp.cos(freq * float(s))] * (R // 8), 0)
        sin_s = jnp.concatenate([jnp.sin(freq * float(s))] * (R // 8), 0)
        cosines.append(cos_len * cos_s - sin_len * sin_s)
        sines.append((sin_len * cos_s + cos_len * sin_s) * sign)
    cosine = jnp.concatenate(cosines, 0)
    sine = jnp.concatenate(sines, 0)

    for c in range(early, chunks):
        project(c)

    for h in range(NH):
        vec = acc[:, h * HD : (h + 1) * HD]
        if h <= NQ:
            vec = vec * cosine + pltpu.roll(vec, HD // 2, 1) * sine
        stack[h * M : (h + 1) * M, :] = vec.astype(BF16)
    q_out[...] = jnp.dot(pick[...], stack[...], preferred_element_type=F32).astype(BF16).reshape(R, MSG, HD)

    def q_copy(o):
        return pltpu.make_async_remote_copy(
            src_ref=q_out.at[o], dst_ref=q_in.at[me], send_sem=q_send, recv_sem=q_recv.at[me],
            device_id={"replica": o}, device_id_type=MESH,
        )

    to_all(q_copy)
    q_in[me] = q_out[me]
    wo_copy = pltpu.make_async_copy(
        wo_hbm.at[:, pl.ds(pl.multiple_of(tx * DC, 128), DC)], wf.at[rows_at(tx, 0, KR)], wo_sem
    )
    wo_copy.start()
    near_a.wait_recv()
    near_b.wait_recv()
    for j in (0, 1):
        to_mate[j].start()
        for e in range(4):
            spread[j][e].start()

    per = 128 // MSG
    group_of_lane = lax.broadcasted_iota(jnp.int32, (8, 128), 1) // MSG
    row_of_lane = lax.broadcasted_iota(jnp.int32, (8, 128), 1) % MSG
    wide_row = lax.broadcasted_iota(jnp.int32, (NQ * M, 128), 0)
    for g in range(R // per):
        slots = jnp.zeros((8, 128), jnp.int32)
        for i in range(per):
            slots = jnp.where(group_of_lane == i, meta_in[g * per + i] & (R - 1), slots)
        target = jnp.concatenate([R * row_of_lane + slots] * (NQ * M // 8), 0)
        unpick[:, g * 128 : (g + 1) * 128] = jnp.where(target == wide_row, 1.0, 0.0).astype(BF16)

    code_copy.wait()
    for copy in kv_copies:
        copy.wait()

    span = max_pages * page
    rows = GROUP * MSG
    far_a.wait_recv()
    pass_a.start()
    far_b.wait_recv()
    pass_b.start()
    tok = lax.broadcasted_iota(jnp.int32, (MSG, span), 1)
    f_row = lax.broadcasted_iota(jnp.int32, (rows, rows), 0)
    f_col = lax.broadcasted_iota(jnp.int32, (rows, rows), 1)
    f_key = f_col % MSG - NQ * S
    fresh_ok = (f_row // MSG == f_col // MSG) & (f_key >= 0) & (f_key <= f_row % S)
    factor = math.log2(math.e) / math.sqrt(HD)
    dims = (((1,), (1,)), ((), ()))

    def attend(g):
        first = g * GROUP
        q = q_in[pl.ds(first, GROUP)].reshape(rows, HD)
        fresh = lax.dot_general(q, q, dims, preferred_element_type=F32)
        fresh = jnp.where(fresh_ok, fresh, -jnp.inf)
        places, scores = [], []
        for u in range(GROUP):
            word = code_sm[first + u, 0]
            slot = word & (R - 1)
            length = lax.shift_right_logical(word, int(math.log2(R)))
            places.append([table_sm[p, slot] for p in range(max_pages)])
            keys = jnp.concatenate([kv[at, 0] for at in places[u]], 0)
            sc = lax.dot_general(q[u * MSG : (u + 1) * MSG], keys, dims, preferred_element_type=F32)
            scores.append(jnp.where(tok < length, sc, -jnp.inf))
        values = pltpu.roll(q.astype(F32), rows - S, 0).astype(BF16)
        for u in range(GROUP):
            mine = slice(u * MSG, (u + 1) * MSG)
            peak = jnp.maximum(
                jnp.max(scores[u], 1, keepdims=True), jnp.max(fresh[mine], 1, keepdims=True)
            )
            w_fresh = jnp.exp2((fresh[mine] - peak) * factor).astype(BF16)
            w = jnp.exp2((scores[u] - peak) * factor).astype(BF16)
            total = jnp.dot(w_fresh, values, preferred_element_type=F32)
            cached = jnp.concatenate([kv[at, 1] for at in places[u]], 0)
            total = total + jnp.dot(w, cached, preferred_element_type=F32)
            denom = jnp.sum(w.astype(F32), 1, keepdims=True) + jnp.sum(
                w_fresh.astype(F32), 1, keepdims=True
            )
            h_out[first + u] = (total / denom).astype(BF16)

    def wait_q(n):
        settle(q_in.at[n], q_recv.at[n])

    def heads_copy(n):
        return pltpu.make_async_remote_copy(
            src_ref=h_out.at[n], dst_ref=h_in.at[me], send_sem=h_send, recv_sem=h_recv,
            device_id={"replica": n}, device_id_type=MESH,
        )

    def attend_group(i, carry):
        g = mod(group - 1 - i, groups)
        for u in range(GROUP):
            n = g * GROUP + u

            @pl.when(n != me)
            def _():
                wait_q(n)

        attend(g)
        for u in range(GROUP):
            n = g * GROUP + u

            @pl.when(n != me)
            def _():
                heads_copy(n).start()

        return carry

    lax.fori_loop(0, groups // 2, attend_group, 0, unroll=2)
    for j in (0, 1):
        for e in range(4):
            spread[j][e].wait_recv()
        rest_to_mate[j].start()
    lax.fori_loop(groups // 2, groups, attend_group, 0, unroll=2)
    h_in[me] = h_out[me]
    pass_a.wait_recv()
    pass_b.wait_recv()
    to_mate[2].start()

    settle(h_in.at[pl.ds(0, R - 1)], h_recv)
    flat = h_in[...].reshape(R * MSG, HD)
    by_head = jnp.dot(unpick[...], flat, preferred_element_type=F32).astype(BF16)
    for h in range(NQ):
        heads[tx, :, h * HD : (h + 1) * HD] = by_head[h * M : (h + 1) * M]

    def push(ref, i, other):
        copy = pltpu.make_async_remote_copy(
            src_ref=ref, dst_ref=ref, send_sem=x_send.at[i], recv_sem=x_recv.at[i],
            device_id={"tensor": other}, device_id_type=MESH,
        )
        copy.start()
        return copy

    low, high = pl.ds(0, half), pl.ds(half, half)
    g0 = push(heads.at[tx, low], 0, right)
    g1 = push(heads.at[tx, high], 1, left)
    g2 = push(heads.at[tx, high], 2, right)
    g3 = push(heads.at[tx, low], 3, left)
    for e in range(4):
        spread[2][e].start()

    def term(owner, cols):
        rows = pl.ds(pl.multiple_of(owner * KR, 16), KR)
        return jnp.dot(heads[owner], wf[rows, cols], preferred_element_type=F32)

    every = slice(0, DC)
    wo_copy.wait()
    total[...] = term(tx, every)
    for e in range(4):
        spread[2][e].wait_recv()
    rest_to_mate[2].start()
    g0.wait_recv()
    g4 = push(heads.at[left, low], 4, right)
    g1.wait_recv()
    g5 = push(heads.at[right, high], 5, left)
    g2.wait_recv()
    to_mate[0].wait_recv()
    rest_to_mate[0].wait_recv()
    total[...] += term(left, every)
    g3.wait_recv()
    to_mate[1].wait_recv()
    rest_to_mate[1].wait_recv()
    total[...] += term(right, every)
    to_mate[2].wait_recv()
    rest_to_mate[2].wait_recv()
    g4.wait_recv()
    g5.wait_recv()

    wide = DC // SUBS

    def cols_of(owner, b):
        return pl.ds(pl.multiple_of(owner * DC + b * wide, 128), wide)

    done = [g0, g1, g2, g3, g4, g5]
    first_r, first_l, second = [], [], []
    for b in range(SUBS):
        part = slice(b * wide, (b + 1) * wide)
        mine = cols_of(tx, b)
        out_ref[:, mine] = (total[:, part] + term(opposite, part)).astype(BF16)
        i = 6 + 6 * b
        first_r.append(push(out_ref.at[low, mine], i, right))
        first_l.append(push(out_ref.at[high, mine], i + 1, left))
        second.append(push(out_ref.at[high, mine], i + 2, right))
        second.append(push(out_ref.at[low, mine], i + 3, left))
    for b in range(SUBS):
        i = 6 + 6 * b
        first_r[b].wait_recv()
        second.append(push(out_ref.at[low, cols_of(left, b)], i + 4, right))
        first_l[b].wait_recv()
        second.append(push(out_ref.at[high, cols_of(right, b)], i + 5, left))
    for copy in second:
        copy.wait_recv()
    for copy in done + first_r + first_l + second:
        copy.wait_send()
    for copy in [far_a, far_b, near_a, near_b, pass_a, pass_b] + sum(spread, []) + to_mate + rest_to_mate:
        copy.wait_send()
    some = pl.ds(0, R - 1)
    settle(meta_out.at[some], meta_send)
    settle(q_out.at[some], q_send)
    settle(h_out.at[some], h_send)


def shards(
    replicas, tensors, hidden_in, norm_gain, w_query, w_key, w_value, w_out, kv_pages, lengths, page_table, destination
):
    S, R, D = hidden_in.shape
    T = tensors
    NQ = w_query.shape[1] // HD
    NH = NQ + 2
    M = S * R
    KC = min(1024, D // 2)
    DC = D // T
    pages, _, page, _ = kv_pages.shape
    any_spec = pl.BlockSpec(memory_space=pl.ANY)
    smem = pl.BlockSpec(memory_space=pltpu.SMEM)
    dma = pltpu.SemaphoreType.DMA
    out = pl.pallas_call(
        functools.partial(kernel, (R, T, S, NQ, D, KC)),
        out_shape=pltpu.VMEM((M, D), BF16),
        in_specs=[smem, smem, smem, pl.BlockSpec(memory_space=pltpu.VMEM)] + [any_spec] * 6,
        out_specs=pl.BlockSpec(memory_space=pltpu.VMEM),
        scratch_shapes=[
            pltpu.VMEM((M, D), BF16),
            pltpu.VMEM((D, NQ * HD), BF16),
            pltpu.VMEM((D, HD), BF16),
            pltpu.VMEM((D, HD), BF16),
            pltpu.VMEM(kv_pages.shape, BF16),
            pltpu.VMEM((T * w_out.shape[0], DC), BF16),
            pltpu.VMEM((2, w_out.shape[0] // 4, DC // 2), BF16),
            pltpu.VMEM((M, NH * HD), F32),
            pltpu.VMEM((R, 128), jnp.int32),
            pltpu.SMEM((R, 128), jnp.int32),
            pltpu.VMEM((R, 8, 128), jnp.int32),
            pltpu.VMEM((R, 8, 128), jnp.int32),
            pltpu.VMEM((R * MSG, NH * M), BF16),
            pltpu.VMEM((NQ * M, R * MSG), BF16),
            pltpu.VMEM((NH * M, HD), BF16),
            pltpu.VMEM((R, MSG, HD), BF16),
            pltpu.VMEM((R, MSG, HD), BF16),
            pltpu.VMEM((R, MSG, HD), BF16),
            pltpu.VMEM((R, MSG, HD), BF16),
            pltpu.VMEM((T, M, NQ * HD), BF16),
            pltpu.VMEM((M, DC), F32),
            dma, dma((D // KC, 3)), dma((4,)), dma, dma,
            dma, dma, dma, dma((R,)), dma, dma, dma((6 + 6 * SUBS,)), dma((6 + 6 * SUBS,)), dma((24,)), dma((24,)),
        ],
        compiler_params=pltpu.CompilerParams(
            collective_id=0, has_side_effects=True, vmem_limit_bytes=58 * 1024 * 1024
        ),
        name="decode_attention",
    )(
        destination, lengths, page_table.T, norm_gain.reshape(1, D), hidden_in.reshape(M, D),
        w_query, w_key, w_value, w_out, kv_pages,
    )
    return out.reshape(S, R, D)


def solution(mesh):
    in_specs = (
        P(None, "replica", None),
        P(),
        P(None, "tensor"),
        P(None, "tensor"),
        P(None, "tensor"),
        P("tensor", None),
        P("replica", None, None, "tensor"),
        P("replica"),
        P("replica", None),
        P("replica"),
    )
    body = functools.partial(shards, mesh.shape["replica"], mesh.shape["tensor"])
    return jax.shard_map(
        body, mesh=mesh, in_specs=in_specs, out_specs=P(None, "replica", None), check_vma=False
    )
```

```python
import functools
import math

import jax
import jax.numpy as jnp
from jax import lax
from jax.experimental import pallas as pl
from jax.experimental.pallas import tpu as pltpu
from jax.sharding import PartitionSpec as P

HD = 128
GROUP = 4
MSG = 32
ROPE_BASE = 1000000.0
EPSILON = 1e-06
SUBS = 2
CHIPS_Z = 4
MESH = pl.DeviceIdType.MESH
F32 = jnp.float32
BF16 = jnp.bfloat16


def mod(value, size):
    return lax.rem(value + 2 * size, size)


def settle(ref, sem):
    pltpu.make_async_copy(ref, ref, sem).wait()


def kernel(
    sizes,
    dest_sm, len_sm, table_sm, gain_ref, hid_hbm, wq_hbm, wk_hbm, wv_hbm, wo_hbm, kv_hbm,
    out_ref,
    hid, wq, wk, wv, kv, wf, relay, acc, code, code_sm, meta_out, meta_in, unpick, by_head, stack,
    q_out, q_in, h_out, h_in, heads, total,
    hid_sem, w_sem, kv_sem, wo_sem, code_sem,
    meta_send, meta_recv, q_send, q_recv, h_send, h_recv, x_send, x_recv, f_send, f_recv,
):
    R, T, S, NQ, D, KC = sizes
    M = S * R
    NH = NQ + 2
    me = lax.axis_index("replica")
    tx = lax.axis_index("tensor")
    chunks = D // KC
    group = me // GROUP
    groups = R // GROUP
    DC = D // T
    half = M // 2
    pages = kv.shape[0]
    max_pages = pages // R
    page = kv.shape[2]
    KR = wo_hbm.shape[0]
    HB, QB = KR // 2, KR // 8
    HC = DC // 2
    core = me % 2
    mate = me + 1 - 2 * core
    chip = me // 2
    z, y = chip % CHIPS_Z, chip // CHIPS_Z
    chips_y = R // (2 * CHIPS_Z)
    parity = (y + z) % 2
    opposite = mod(tx + 2, T)

    def at(yy, zz):
        return (mod(yy, chips_y) * CHIPS_Z + mod(zz, CHIPS_Z)) * 2 + core

    around = (at(y + 1, z), at(y - 1, z), at(y, z + 1), at(y, z - 1))

    def rows_at(owner, first, size):
        return pl.ds(pl.multiple_of(owner * KR + first, 16), size)

    half_cols = pl.ds(pl.multiple_of(core * HC, 128), HC)

    def own_rows(target, first, size):
        cols = pl.ds(pl.multiple_of(target * DC + core * HC, 128), HC)
        return wo_hbm.at[pl.ds(pl.multiple_of(first, 16), size), cols]

    def weight_piece(src, dst, i, other):
        return pltpu.make_async_remote_copy(
            src_ref=src, dst_ref=dst, send_sem=f_send.at[i], recv_sem=f_recv.at[i],
            device_id=other, device_id_type=MESH,
        )

    def held(owner, first, size):
        return wf.at[rows_at(owner, first, size), half_cols]

    def same_place(owner, first, size, i, other):
        return weight_piece(held(owner, first, size), held(owner, first, size), i, {"replica": other})

    right = mod(tx + 1, T)
    left = mod(tx - 1, T)
    fetched, missing = parity * HB, (1 - parity) * HB
    QH2 = HB // 2
    far_a = weight_piece(own_rows(opposite, fetched, QH2), relay.at[0], 0, {"tensor": right})
    far_b = weight_piece(own_rows(opposite, fetched + QH2, QH2), relay.at[1], 1, {"tensor": left})
    near_a, near_b = (
        [
            weight_piece(
                own_rows(target, fetched + p * QH2, QH2), held(tx, fetched + p * QH2, QH2), 2 + 2 * p + i,
                {"tensor": target},
            )
            for p in range(2)
        ]
        for i, target in enumerate((right, left))
    )
    pass_a = weight_piece(relay.at[0], held(left, fetched, QH2), 24, {"tensor": right})
    pass_b = weight_piece(relay.at[1], held(right, fetched + QH2, QH2), 25, {"tensor": left})
    owners = (left, right, opposite)
    spread = [
        [same_place(owner, fetched + e * QB, QB, 6 + 4 * j + e, around[e]) for e in range(4)]
        for j, owner in enumerate(owners)
    ]
    to_mate = [same_place(owner, fetched, HB, 18 + j, mate) for j, owner in enumerate(owners)]
    rest_to_mate = [same_place(owner, missing, HB, 21 + j, mate) for j, owner in enumerate(owners)]

    def weight_copies(c):
        rows = pl.ds(pl.multiple_of(c * KC, KC), KC)
        return (
            pltpu.make_async_copy(wq_hbm.at[rows], wq.at[rows], w_sem.at[c, 0]),
            pltpu.make_async_copy(wk_hbm.at[rows], wk.at[rows], w_sem.at[c, 1]),
            pltpu.make_async_copy(wv_hbm.at[rows], wv.at[rows], w_sem.at[c, 2]),
        )

    hid_copy = pltpu.make_async_copy(hid_hbm, hid, hid_sem)
    hid_copy.start()
    def load(c):
        if c < chunks:
            for copy in weight_copies(c):
                copy.start()

    load(0)

    barrier = pltpu.get_barrier_semaphore()

    def far_first(k):
        return R // 2 + (1 - 2 * (k % 2)) * ((k + 1) // 2)

    def greet(k, carry):
        n = mod(me + far_first(k), R)
        pl.semaphore_signal(barrier, inc=1, device_id={"replica": n}, device_id_type=MESH)
        return carry

    lax.fori_loop(0, R - 1, greet, 0)
    for other in (right, left):
        pl.semaphore_signal(barrier, inc=1, device_id={"tensor": other}, device_id_type=MESH)

    load(1)

    numbers = lax.broadcasted_iota(jnp.int32, (R, 128), 0)
    codes = jnp.zeros((R, 128), jnp.int32)
    for b in range(R):
        codes = jnp.where(numbers == dest_sm[b], len_sm[b] * R + b, codes)
    code[...] = codes
    code_copy = pltpu.make_async_copy(code, code_sm, code_sem)
    code_copy.start()
    for n in range(R):
        meta_out[n] = jnp.broadcast_to(codes[n : n + 1], (8, 128))

    pl.semaphore_wait(barrier, R - 1 + 2)

    def to_all(make):
        def send(k, carry):
            n = mod(group * GROUP + GROUP + k, R)

            @pl.when(n != me)
            def _():
                make(n).start()

            return carry

        lax.fori_loop(0, R, send, 0)

    def meta_copy(n):
        return pltpu.make_async_remote_copy(
            src_ref=meta_out.at[n], dst_ref=meta_in.at[me], send_sem=meta_send, recv_sem=meta_recv,
            device_id={"replica": n}, device_id_type=MESH,
        )

    def send_meta(k, carry):
        meta_copy(mod(me + far_first(k), R)).start()
        return carry

    lax.fori_loop(0, R - 1, send_meta, 0)
    far_a.start()
    far_b.start()

    hid_copy.wait()
    load(2)
    squares = jnp.zeros((M, 128), F32)
    for c in range(D // 128):
        wide = hid[:, c * 128 : (c + 1) * 128].astype(F32)
        squares = squares + wide * wide
    load(3)
    scale = lax.rsqrt(jnp.sum(squares, 1, keepdims=True) * (1.0 / D) + EPSILON)

    for c in range(0, D, 512):
        cols = slice(c, c + 512)
        hid[:, cols] = (hid[:, cols].astype(F32) * scale * gain_ref[:, cols]).astype(BF16)

    for c in range(4, chunks):
        load(c)
    kv_copies = []
    step = pages // 4
    for c in range(4):
        rows = pl.ds(c * step, step)
        kv_copies.append(pltpu.make_async_copy(kv_hbm.at[rows], kv.at[rows], kv_sem.at[c]))

    def project(c):
        for copy in weight_copies(c):
            copy.wait()
        if c + 1 == chunks:
            for copy in kv_copies:
                copy.start()
        cols = slice(c * KC, (c + 1) * KC)
        weights = jnp.concatenate([wq[cols], wk[cols], wv[cols]], 1)
        term = jnp.dot(hid[:, cols], weights, preferred_element_type=F32)
        acc[...] = term if c == 0 else acc[...] + term

    for c in range(chunks):
        project(c)
        if c == chunks // 2:
            near_a[0].start()
            near_b[0].start()

    def share_near(p):
        near_a[p].wait_recv()
        near_b[p].wait_recv()
        for j in (0, 1):
            for e in (2 * p, 2 * p + 1):
                spread[j][e].start()

    near_a[1].start()
    near_b[1].start()
    settle(meta_in.at[pl.ds(0, R - 1)], meta_recv)
    meta_in[me] = meta_out[me]

    slot_rows = lax.broadcasted_iota(jnp.int32, (R, 128), 0)
    lens = jnp.zeros((R, 128), jnp.int32)
    for o in range(R):
        tile = meta_in[o]
        slot_wide = jnp.concatenate([tile & (R - 1)] * (R // 8), 0)
        len_wide = jnp.concatenate([lax.shift_right_logical(tile, int(math.log2(R)))] * (R // 8), 0)
        lens = jnp.where(slot_rows == slot_wide, len_wide, lens)

    freq_lane = lax.broadcasted_iota(jnp.int32, (8, 128), 1) % (HD // 2)
    freq = jnp.exp(freq_lane.astype(F32) * (-2.0 / HD * math.log(ROPE_BASE)))
    angle = lens.astype(F32) * jnp.concatenate([freq] * (R // 8), 0)
    cos_len, sin_len = jnp.cos(angle), jnp.sin(angle)
    sign = jnp.where(lax.broadcasted_iota(jnp.int32, (R, 128), 1) < HD // 2, -1.0, 1.0)
    cosines, sines = [], []
    for s in range(S):
        if s == 0:
            cosines.append(cos_len)
            sines.append(sin_len * sign)
            continue
        cos_s = jnp.concatenate([jnp.cos(freq * float(s))] * (R // 8), 0)
        sin_s = jnp.concatenate([jnp.sin(freq * float(s))] * (R // 8), 0)
        cosines.append(cos_len * cos_s - sin_len * sin_s)
        sines.append((sin_len * cos_s + cos_len * sin_s) * sign)
    cosine = jnp.concatenate(cosines, 0)
    sine = jnp.concatenate(sines, 0)


    for h in range(NH):
        vec = acc[:, h * HD : (h + 1) * HD]
        if h <= NQ:
            vec = vec * cosine + pltpu.roll(vec, HD // 2, 1) * sine
        stack[h * M : (h + 1) * M, :] = vec.astype(BF16)

    def q_copy(o):
        return pltpu.make_async_remote_copy(
            src_ref=q_out.at[o], dst_ref=q_in.at[me], send_sem=q_send, recv_sem=q_recv.at[me],
            device_id={"replica": o}, device_id_type=MESH,
        )

    msg_row = lax.broadcasted_iota(jnp.int32, (MSG, 128), 0)
    lane = lax.broadcasted_iota(jnp.int32, (MSG, 128), 1)

    def send_group(i, carry):
        first = mod(group + 1 + i, groups) * GROUP
        blocks = []
        for u in range(GROUP):
            slot = meta_in[first + u] & (R - 1)
            target = R * msg_row + jnp.concatenate([slot] * (MSG // 8), 0)
            parts = []
            for c in range(0, NH * M, 128):
                hit = jnp.where(target == lane + c, 1.0, 0.0).astype(BF16)
                parts.append(hit[:, : min(128, NH * M - c)])
            blocks.append(jnp.concatenate(parts, 1))
        pick = jnp.concatenate(blocks, 0)
        rows = jnp.dot(pick, stack[...], preferred_element_type=F32)
        q_out[pl.ds(first, GROUP)] = rows.astype(BF16).reshape(GROUP, MSG, HD)
        for u in range(GROUP):

            @pl.when(first + u != me)
            def _():
                q_copy(first + u).start()

        return carry

    lax.fori_loop(0, groups, send_group, 0, unroll=2)
    q_in[me] = q_out[me]
    wo_copy = pltpu.make_async_copy(
        wo_hbm.at[:, pl.ds(pl.multiple_of(tx * DC, 128), DC)], wf.at[rows_at(tx, 0, KR)], wo_sem
    )
    wo_copy.start()
    per = 128 // MSG
    group_of_lane = lax.broadcasted_iota(jnp.int32, (8, 128), 1) // MSG
    row_of_lane = lax.broadcasted_iota(jnp.int32, (8, 128), 1) % MSG
    wide_row = lax.broadcasted_iota(jnp.int32, (NQ * M, 128), 0)
    for g in range(R // per):
        slots = jnp.zeros((8, 128), jnp.int32)
        for i in range(per):
            slots = jnp.where(group_of_lane == i, meta_in[g * per + i] & (R - 1), slots)
        target = jnp.concatenate([R * row_of_lane + slots] * (NQ * M // 8), 0)
        unpick[:, g * 128 : (g + 1) * 128] = jnp.where(target == wide_row, 1.0, 0.0).astype(BF16)

    far_a.wait_recv()
    pass_a.start()
    far_b.wait_recv()
    pass_b.start()
    code_copy.wait()
    for copy in kv_copies:
        copy.wait()

    span = max_pages * page
    rows = GROUP * MSG
    tok = lax.broadcasted_iota(jnp.int32, (MSG, span), 1)
    f_row = lax.broadcasted_iota(jnp.int32, (rows, rows), 0)
    f_col = lax.broadcasted_iota(jnp.int32, (rows, rows), 1)
    f_key = f_col % MSG - NQ * S
    fresh_ok = (f_row // MSG == f_col // MSG) & (f_key >= 0) & (f_key <= f_row % S)
    factor = math.log2(math.e) / math.sqrt(HD)
    dims = (((1,), (1,)), ((), ()))

    def attend(g):
        first = g * GROUP
        q = q_in[pl.ds(first, GROUP)].reshape(rows, HD)
        fresh = lax.dot_general(q, q, dims, preferred_element_type=F32)
        fresh = jnp.where(fresh_ok, fresh, -jnp.inf)
        places, scores = [], []
        for u in range(GROUP):
            word = code_sm[first + u, 0]
            slot = word & (R - 1)
            length = lax.shift_right_logical(word, int(math.log2(R)))
            places.append([table_sm[p, slot] for p in range(max_pages)])
            keys = jnp.concatenate([kv[at, 0] for at in places[u]], 0)
            sc = lax.dot_general(q[u * MSG : (u + 1) * MSG], keys, dims, preferred_element_type=F32)
            scores.append(jnp.where(tok < length, sc, -jnp.inf))
        values = pltpu.roll(q.astype(F32), rows - S, 0).astype(BF16)
        for u in range(GROUP):
            mine = slice(u * MSG, (u + 1) * MSG)
            peak = jnp.maximum(
                jnp.max(scores[u], 1, keepdims=True), jnp.max(fresh[mine], 1, keepdims=True)
            )
            w_fresh = jnp.exp2((fresh[mine] - peak) * factor).astype(BF16)
            w = jnp.exp2((scores[u] - peak) * factor).astype(BF16)
            total = jnp.dot(w_fresh, values, preferred_element_type=F32)
            cached = jnp.concatenate([kv[at, 1] for at in places[u]], 0)
            total = total + jnp.dot(w, cached, preferred_element_type=F32)
            denom = jnp.sum(w.astype(F32), 1, keepdims=True) + jnp.sum(
                w_fresh.astype(F32), 1, keepdims=True
            )
            h_out[first + u] = (total / denom).astype(BF16)

    def wait_q(n):
        settle(q_in.at[n], q_recv.at[n])

    def heads_copy(n):
        return pltpu.make_async_remote_copy(
            src_ref=h_out.at[n], dst_ref=h_in.at[me], send_sem=h_send, recv_sem=h_recv.at[me],
            device_id={"replica": n}, device_id_type=MESH,
        )

    def attend_group(i, carry):
        g = mod(group - 1 - i, groups)
        for u in range(GROUP):
            n = g * GROUP + u

            @pl.when(n != me)
            def _():
                wait_q(n)

        attend(g)
        for u in range(GROUP):
            n = g * GROUP + u

            @pl.when(n != me)
            def _():
                heads_copy(n).start()

        return carry

    lax.fori_loop(0, groups, attend_group, 0, unroll=2)
    h_in[me] = h_out[me]
    share_near(0)
    share_near(1)
    to_mate[0].start()
    to_mate[1].start()
    def collect(i, carry):
        g = mod(group + 1 + i, groups)
        for u in range(GROUP):
            n = g * GROUP + u

            @pl.when(n != me)
            def _():
                settle(h_in.at[n], h_recv.at[n])

        flat = h_in[pl.ds(g * GROUP, GROUP)].reshape(GROUP * MSG, HD)
        cols = pl.ds(pl.multiple_of(g * 128, 128), 128)
        rows = jnp.dot(unpick[:, cols], flat, preferred_element_type=F32)
        by_head[...] += rows
        return carry

    by_head[...] = jnp.zeros_like(by_head)
    lax.fori_loop(0, groups, collect, 0)
    for h in range(NQ):
        heads[tx, :, h * HD : (h + 1) * HD] = by_head[h * M : (h + 1) * M].astype(BF16)

    def push(ref, i, other):
        copy = pltpu.make_async_remote_copy(
            src_ref=ref, dst_ref=ref, send_sem=x_send.at[i], recv_sem=x_recv.at[i],
            device_id={"tensor": other}, device_id_type=MESH,
        )
        copy.start()
        return copy

    low, high = pl.ds(0, half), pl.ds(half, half)
    g0 = push(heads.at[tx, low], 0, right)
    g1 = push(heads.at[tx, high], 1, left)
    g2 = push(heads.at[tx, high], 2, right)
    g3 = push(heads.at[tx, low], 3, left)
    pass_a.wait_recv()
    pass_b.wait_recv()
    to_mate[2].start()
    for e in range(4):
        spread[2][e].start()

    def term(owner, cols):
        rows = pl.ds(pl.multiple_of(owner * KR, 16), KR)
        return jnp.dot(heads[owner], wf[rows, cols], preferred_element_type=F32)

    every = slice(0, DC)
    wo_copy.wait()
    total[...] = term(tx, every)
    for j in (0, 1):
        for e in range(4):
            spread[j][e].wait_recv()
        rest_to_mate[j].start()
    for e in range(4):
        spread[2][e].wait_recv()
    rest_to_mate[2].start()
    g0.wait_recv()
    g4 = push(heads.at[left, low], 4, right)
    g1.wait_recv()
    g5 = push(heads.at[right, high], 5, left)
    g2.wait_recv()
    to_mate[0].wait_recv()
    rest_to_mate[0].wait_recv()
    total[...] += term(left, every)
    g3.wait_recv()
    to_mate[1].wait_recv()
    rest_to_mate[1].wait_recv()
    total[...] += term(right, every)
    to_mate[2].wait_recv()
    rest_to_mate[2].wait_recv()
    g4.wait_recv()
    g5.wait_recv()

    wide = DC // SUBS

    def cols_of(owner, b):
        return pl.ds(pl.multiple_of(owner * DC + b * wide, 128), wide)

    done = [g0, g1, g2, g3, g4, g5]
    first_r, first_l, second = [], [], []
    for b in range(SUBS):
        part = slice(b * wide, (b + 1) * wide)
        mine = cols_of(tx, b)
        out_ref[:, mine] = (total[:, part] + term(opposite, part)).astype(BF16)
        i = 6 + 6 * b
        first_r.append(push(out_ref.at[low, mine], i, right))
        first_l.append(push(out_ref.at[high, mine], i + 1, left))
        second.append(push(out_ref.at[high, mine], i + 2, right))
        second.append(push(out_ref.at[low, mine], i + 3, left))
    for b in range(SUBS):
        i = 6 + 6 * b
        first_r[b].wait_recv()
        second.append(push(out_ref.at[low, cols_of(left, b)], i + 4, right))
        first_l[b].wait_recv()
        second.append(push(out_ref.at[high, cols_of(right, b)], i + 5, left))
    for copy in second:
        copy.wait_recv()
    for copy in done + first_r + first_l + second:
        copy.wait_send()
    for copy in [far_a, far_b, pass_a, pass_b] + near_a + near_b + sum(spread, []) + to_mate + rest_to_mate:
        copy.wait_send()
    some = pl.ds(0, R - 1)
    settle(meta_out.at[some], meta_send)
    settle(q_out.at[some], q_send)
    settle(h_out.at[some], h_send)


def shards(
    replicas, tensors, hidden_in, norm_gain, w_query, w_key, w_value, w_out, kv_pages, lengths, page_table, destination
):
    S, R, D = hidden_in.shape
    T = tensors
    NQ = w_query.shape[1] // HD
    NH = NQ + 2
    M = S * R
    KC = min(1024, D // 2)
    DC = D // T
    pages, _, page, _ = kv_pages.shape
    any_spec = pl.BlockSpec(memory_space=pl.ANY)
    smem = pl.BlockSpec(memory_space=pltpu.SMEM)
    dma = pltpu.SemaphoreType.DMA
    out = pl.pallas_call(
        functools.partial(kernel, (R, T, S, NQ, D, KC)),
        out_shape=pltpu.VMEM((M, D), BF16),
        in_specs=[smem, smem, smem, pl.BlockSpec(memory_space=pltpu.VMEM)] + [any_spec] * 6,
        out_specs=pl.BlockSpec(memory_space=pltpu.VMEM),
        scratch_shapes=[
            pltpu.VMEM((M, D), BF16),
            pltpu.VMEM((D, NQ * HD), BF16),
            pltpu.VMEM((D, HD), BF16),
            pltpu.VMEM((D, HD), BF16),
            pltpu.VMEM(kv_pages.shape, BF16),
            pltpu.VMEM((T * w_out.shape[0], DC), BF16),
            pltpu.VMEM((2, w_out.shape[0] // 4, DC // 2), BF16),
            pltpu.VMEM((M, NH * HD), F32),
            pltpu.VMEM((R, 128), jnp.int32),
            pltpu.SMEM((R, 128), jnp.int32),
            pltpu.VMEM((R, 8, 128), jnp.int32),
            pltpu.VMEM((R, 8, 128), jnp.int32),
            pltpu.VMEM((NQ * M, R * MSG), BF16),
            pltpu.VMEM((NQ * M, HD), F32),
            pltpu.VMEM((NH * M, HD), BF16),
            pltpu.VMEM((R, MSG, HD), BF16),
            pltpu.VMEM((R, MSG, HD), BF16),
            pltpu.VMEM((R, MSG, HD), BF16),
            pltpu.VMEM((R, MSG, HD), BF16),
            pltpu.VMEM((T, M, NQ * HD), BF16),
            pltpu.VMEM((M, DC), F32),
            dma, dma((D // KC, 3)), dma((4,)), dma, dma,
            dma, dma, dma, dma((R,)), dma, dma((R,)), dma((6 + 6 * SUBS,)), dma((6 + 6 * SUBS,)), dma((26,)), dma((26,)),
        ],
        compiler_params=pltpu.CompilerParams(
            collective_id=0, has_side_effects=True, vmem_limit_bytes=58 * 1024 * 1024
        ),
        name="decode_attention",
    )(
        destination, lengths, page_table.T, norm_gain.reshape(1, D), hidden_in.reshape(M, D),
        w_query, w_key, w_value, w_out, kv_pages,
    )
    return out.reshape(S, R, D)


def solution(mesh):
    in_specs = (
        P(None, "replica", None),
        P(),
        P(None, "tensor"),
        P(None, "tensor"),
        P(None, "tensor"),
        P("tensor", None),
        P("replica", None, None, "tensor"),
        P("replica"),
        P("replica", None),
        P("replica"),
    )
    body = functools.partial(shards, mesh.shape["replica"], mesh.shape["tensor"])
    return jax.shard_map(
        body, mesh=mesh, in_specs=in_specs, out_specs=P(None, "replica", None), check_vma=False
    )
```

```python
import functools
import math

import jax
import jax.numpy as jnp
from jax import lax
from jax.experimental import pallas as pl
from jax.experimental.pallas import tpu as pltpu
from jax.sharding import PartitionSpec as P

HD = 128
GROUP = 4
MSG = 32
ROPE_BASE = 1000000.0
EPSILON = 1e-06
CHIPS_Z = 4
MESH = pl.DeviceIdType.MESH
F32 = jnp.float32
BF16 = jnp.bfloat16


def mod(value, size):
    return lax.rem(value + 2 * size, size)


def settle(ref, sem):
    pltpu.make_async_copy(ref, ref, sem).wait()


def kernel(
    sizes,
    dest_hbm, len_hbm, table_hbm, gain_hbm, hid_hbm, wq_hbm, wk_hbm, wv_hbm, wo_hbm, kv_hbm,
    out_ref,
    dest_sm, len_sm, table_sm, gain_ref, small_sem,
    hid, wq, wk, wv, kv, wf, relay, acc, code, code_sm, meta_out, meta_in, order, unpick, gathered, stack,
    q_out, q_in, h_out, h_in, heads, total,
    hid_sem, w_sem, kv_sem, wo_sem, code_sem,
    meta_send, meta_recv, q_send, q_recv, h_send, h_recv, x_send, x_recv, f_send, f_recv,
):
    R, T, S, NQ, D, KC = sizes
    M = S * R
    NH = NQ + 2
    me = lax.axis_index("replica")
    tx = lax.axis_index("tensor")
    chunks = D // KC
    group = me // GROUP
    groups = R // GROUP
    DC = D // T
    half = M // 2
    pages = kv.shape[0]
    max_pages = pages // R
    page = kv.shape[2]
    KR = wo_hbm.shape[0]
    HB, QB = KR // 2, KR // 8
    HC = DC // 2
    core = me % 2
    mate = me + 1 - 2 * core
    chip = me // 2
    z, y = chip % CHIPS_Z, chip // CHIPS_Z
    chips_y = R // (2 * CHIPS_Z)
    parity = (y + z) % 2
    opposite = mod(tx + 2, T)

    def at(yy, zz):
        return (mod(yy, chips_y) * CHIPS_Z + mod(zz, CHIPS_Z)) * 2 + core

    around = (at(y + 1, z), at(y - 1, z), at(y, z + 1), at(y, z - 1))

    def rows_at(owner, first, size):
        return pl.ds(pl.multiple_of(owner * KR + first, 16), size)

    half_cols = pl.ds(pl.multiple_of(core * HC, 128), HC)

    def own_rows(target, first, size):
        cols = pl.ds(pl.multiple_of(target * DC + core * HC, 128), HC)
        return wo_hbm.at[pl.ds(pl.multiple_of(first, 16), size), cols]

    def weight_piece(src, dst, i, other):
        return pltpu.make_async_remote_copy(
            src_ref=src, dst_ref=dst, send_sem=f_send.at[i], recv_sem=f_recv.at[i],
            device_id=other, device_id_type=MESH,
        )

    def held(owner, first, size):
        return wf.at[rows_at(owner, first, size), half_cols]

    def same_place(owner, first, size, i, other):
        return weight_piece(held(owner, first, size), held(owner, first, size), i, {"replica": other})

    right = mod(tx + 1, T)
    left = mod(tx - 1, T)
    fetched, missing = parity * HB, (1 - parity) * HB
    QH2 = HB // 2
    far_a = weight_piece(own_rows(opposite, fetched, QH2), relay.at[0], 0, {"tensor": right})
    far_b = weight_piece(own_rows(opposite, fetched + QH2, QH2), relay.at[1], 1, {"tensor": left})
    near_a, near_b = (
        [
            weight_piece(
                own_rows(target, fetched + p * QH2, QH2), held(tx, fetched + p * QH2, QH2), 2 + 2 * p + i,
                {"tensor": target},
            )
            for p in range(2)
        ]
        for i, target in enumerate((right, left))
    )
    pass_a = weight_piece(relay.at[0], held(left, fetched, QH2), 24, {"tensor": right})
    pass_b = weight_piece(relay.at[1], held(right, fetched + QH2, QH2), 25, {"tensor": left})
    owners = (left, right, opposite)
    spread = [
        [same_place(owner, fetched + e * QB, QB, 6 + 4 * j + e, around[e]) for e in range(4)]
        for j, owner in enumerate(owners)
    ]
    to_mate = [same_place(owner, fetched, HB, 18 + j, mate) for j, owner in enumerate(owners)]
    rest_to_mate = [
        [same_place(owner, missing + e * QB, QB, 26 + 4 * j + e, mate) for e in range(4)]
        for j, owner in enumerate(owners)
    ]

    def weight_copies(c):
        rows = pl.ds(pl.multiple_of(c * KC, KC), KC)
        return (
            pltpu.make_async_copy(wq_hbm.at[rows], wq.at[rows], w_sem.at[c, 0]),
            pltpu.make_async_copy(wk_hbm.at[rows], wk.at[rows], w_sem.at[c, 1]),
            pltpu.make_async_copy(wv_hbm.at[rows], wv.at[rows], w_sem.at[c, 2]),
        )

    small = [
        pltpu.make_async_copy(src, dst, small_sem.at[i])
        for i, (src, dst) in enumerate(
            ((dest_hbm, dest_sm), (len_hbm, len_sm), (gain_hbm, gain_ref), (table_hbm, table_sm))
        )
    ]
    for copy in small:
        copy.start()
    hid_copy = pltpu.make_async_copy(hid_hbm, hid, hid_sem)
    hid_copy.start()
    def load(c):
        if c < chunks:
            for copy in weight_copies(c):
                copy.start()

    load(0)

    barrier = pltpu.get_barrier_semaphore()

    def far_first(k):
        return R // 2 + (1 - 2 * (k % 2)) * ((k + 1) // 2)

    def greet(k, carry):
        n = mod(me + far_first(k), R)
        pl.semaphore_signal(barrier, inc=1, device_id={"replica": n}, device_id_type=MESH)
        return carry

    lax.fori_loop(0, R - 1, greet, 0)
    for other in (right, left):
        pl.semaphore_signal(barrier, inc=1, device_id={"tensor": other}, device_id_type=MESH)

    load(1)

    small[0].wait()
    small[1].wait()
    numbers = lax.broadcasted_iota(jnp.int32, (R, 128), 0)
    codes = jnp.zeros((R, 128), jnp.int32)
    for b in range(R):
        codes = jnp.where(numbers == dest_sm[b], len_sm[b] * R + b, codes)
    code[...] = codes
    code_copy = pltpu.make_async_copy(code, code_sm, code_sem)
    code_copy.start()
    for n in range(R):
        meta_out[n] = jnp.broadcast_to(codes[n : n + 1], (8, 128))

    pl.semaphore_wait(barrier, R - 1 + 2)

    def to_all(make):
        def send(k, carry):
            n = mod(group * GROUP + GROUP + k, R)

            @pl.when(n != me)
            def _():
                make(n).start()

            return carry

        lax.fori_loop(0, R, send, 0)

    def meta_copy(n):
        return pltpu.make_async_remote_copy(
            src_ref=meta_out.at[n], dst_ref=meta_in.at[me], send_sem=meta_send, recv_sem=meta_recv,
            device_id={"replica": n}, device_id_type=MESH,
        )

    def send_meta(k, carry):
        meta_copy(mod(me + far_first(k), R)).start()
        return carry

    lax.fori_loop(0, R - 1, send_meta, 0)
    far_a.start()
    far_b.start()

    hid_copy.wait()
    small[2].wait()
    load(2)
    squares = jnp.zeros((M, 128), F32)
    for c in range(D // 128):
        wide = hid[:, c * 128 : (c + 1) * 128].astype(F32)
        squares = squares + wide * wide
    load(3)
    scale = lax.rsqrt(jnp.sum(squares, 1, keepdims=True) * (1.0 / D) + EPSILON)

    for c in range(0, D, 512):
        cols = slice(c, c + 512)
        hid[:, cols] = (hid[:, cols].astype(F32) * scale * gain_ref[:, cols]).astype(BF16)

    for c in range(4, chunks):
        load(c)
    kv_copies = []
    step = pages // 4
    for c in range(4):
        rows = pl.ds(c * step, step)
        kv_copies.append(pltpu.make_async_copy(kv_hbm.at[rows], kv.at[rows], kv_sem.at[c]))

    def project(c):
        for copy in weight_copies(c):
            copy.wait()
        if c + 1 == chunks:
            for copy in kv_copies:
                copy.start()
        cols = slice(c * KC, (c + 1) * KC)
        weights = jnp.concatenate([wq[cols], wk[cols], wv[cols]], 1)
        term = jnp.dot(hid[:, cols], weights, preferred_element_type=F32)
        acc[...] = term if c == 0 else acc[...] + term

    for c in range(chunks):
        project(c)
        if c == chunks // 2:
            near_a[0].start()
            near_b[0].start()

    def share_near(p):
        near_a[p].wait_recv()
        near_b[p].wait_recv()
        for j in (0, 1):
            for e in (2 * p, 2 * p + 1):
                spread[j][e].start()

    near_a[1].start()
    near_b[1].start()
    settle(meta_in.at[pl.ds(0, R - 1)], meta_recv)
    meta_in[me] = meta_out[me]

    slot_rows = lax.broadcasted_iota(jnp.int32, (R, 128), 0)
    lens = jnp.zeros((R, 128), jnp.int32)
    for o in range(R):
        tile = meta_in[o]
        slot_wide = jnp.concatenate([tile & (R - 1)] * (R // 8), 0)
        len_wide = jnp.concatenate([lax.shift_right_logical(tile, int(math.log2(R)))] * (R // 8), 0)
        lens = jnp.where(slot_rows == slot_wide, len_wide, lens)

    freq_lane = lax.broadcasted_iota(jnp.int32, (8, 128), 1) % (HD // 2)
    freq = jnp.exp(freq_lane.astype(F32) * (-2.0 / HD * math.log(ROPE_BASE)))
    angle = lens.astype(F32) * jnp.concatenate([freq] * (R // 8), 0)
    cos_len, sin_len = jnp.cos(angle), jnp.sin(angle)
    sign = jnp.where(lax.broadcasted_iota(jnp.int32, (R, 128), 1) < HD // 2, -1.0, 1.0)
    cosines, sines = [], []
    for s in range(S):
        if s == 0:
            cosines.append(cos_len)
            sines.append(sin_len * sign)
            continue
        cos_s = jnp.concatenate([jnp.cos(freq * float(s))] * (R // 8), 0)
        sin_s = jnp.concatenate([jnp.sin(freq * float(s))] * (R // 8), 0)
        cosines.append(cos_len * cos_s - sin_len * sin_s)
        sines.append((sin_len * cos_s + cos_len * sin_s) * sign)
    cosine = jnp.concatenate(cosines, 0)
    sine = jnp.concatenate(sines, 0)


    for h in range(NH):
        vec = acc[:, h * HD : (h + 1) * HD]
        if h <= NQ:
            vec = vec * cosine + pltpu.roll(vec, HD // 2, 1) * sine
        stack[h * M : (h + 1) * M, :] = vec.astype(BF16)

    def q_copy(o):
        return pltpu.make_async_remote_copy(
            src_ref=q_out.at[o], dst_ref=q_in.at[me], send_sem=q_send, recv_sem=q_recv.at[me],
            device_id={"replica": o}, device_id_type=MESH,
        )

    msg_row = lax.broadcasted_iota(jnp.int32, (MSG, 128), 0)
    lane = lax.broadcasted_iota(jnp.int32, (MSG, 128), 1)

    def send_group(i, carry):
        first = mod(group + 1 + i, groups) * GROUP
        blocks = []
        for u in range(GROUP):
            slot = meta_in[first + u] & (R - 1)
            target = R * msg_row + jnp.concatenate([slot] * (MSG // 8), 0)
            parts = []
            for c in range(0, NH * M, 128):
                hit = jnp.where(target == lane + c, 1.0, 0.0).astype(BF16)
                parts.append(hit[:, : min(128, NH * M - c)])
            blocks.append(jnp.concatenate(parts, 1))
        pick = jnp.concatenate(blocks, 0)
        rows = jnp.dot(pick, stack[...], preferred_element_type=F32)
        q_out[pl.ds(first, GROUP)] = rows.astype(BF16).reshape(GROUP, MSG, HD)
        for u in range(GROUP):

            @pl.when(first + u != me)
            def _():
                q_copy(first + u).start()

        return carry

    lax.fori_loop(0, groups, send_group, 0, unroll=2)
    q_in[me] = q_out[me]
    wo_copy = pltpu.make_async_copy(
        wo_hbm.at[:, pl.ds(pl.multiple_of(tx * DC, 128), DC)], wf.at[rows_at(tx, 0, KR)], wo_sem
    )
    wo_copy.start()
    GS = GROUP * S
    order_row = lax.broadcasted_iota(jnp.int32, (NQ * GS, GROUP * MSG), 0)
    order_col = lax.broadcasted_iota(jnp.int32, (NQ * GS, GROUP * MSG), 1)
    order_at = order_row % GS // S * MSG + order_row // GS * S + order_row % S
    order[...] = jnp.where(order_at == order_col, 1.0, 0.0).astype(BF16)
    arrival = lax.broadcasted_iota(jnp.int32, (8, M), 1)
    slots = jnp.zeros((8, M), jnp.int32)
    for k in range(R):
        slot = meta_in[mod(group * GROUP + GROUP + k, R)][:, :M] & (R - 1)
        slots = jnp.where(arrival // S == k, slot, slots)
    slots = slots + R * (arrival % S)
    wide_slots = jnp.concatenate([slots] * (M // 8), 0)
    wide_rows = lax.broadcasted_iota(jnp.int32, (M, M), 0)
    unpick[...] = jnp.where(wide_slots == wide_rows, 1.0, 0.0).astype(BF16)
    far_a.wait_recv()
    pass_a.start()
    far_b.wait_recv()
    pass_b.start()
    code_copy.wait()
    small[3].wait()
    for copy in kv_copies:
        copy.wait()

    span = max_pages * page
    rows = GROUP * MSG
    tok = lax.broadcasted_iota(jnp.int32, (MSG, span), 1)
    f_row = lax.broadcasted_iota(jnp.int32, (rows, rows), 0)
    f_col = lax.broadcasted_iota(jnp.int32, (rows, rows), 1)
    f_key = f_col % MSG - NQ * S
    fresh_ok = (f_row // MSG == f_col // MSG) & (f_key >= 0) & (f_key <= f_row % S)
    factor = math.log2(math.e) / math.sqrt(HD)
    dims = (((1,), (1,)), ((), ()))

    def attend(g):
        first = g * GROUP
        q = q_in[pl.ds(first, GROUP)].reshape(rows, HD)
        fresh = lax.dot_general(q, q, dims, preferred_element_type=F32)
        fresh = jnp.where(fresh_ok, fresh, -jnp.inf)
        places, scores = [], []
        for u in range(GROUP):
            word = code_sm[first + u, 0]
            slot = word & (R - 1)
            length = lax.shift_right_logical(word, int(math.log2(R)))
            places.append([table_sm[p, slot] for p in range(max_pages)])
            keys = jnp.concatenate([kv[at, 0] for at in places[u]], 0)
            sc = lax.dot_general(q[u * MSG : (u + 1) * MSG], keys, dims, preferred_element_type=F32)
            scores.append(jnp.where(tok < length, sc, -jnp.inf))
        values = pltpu.roll(q.astype(F32), rows - S, 0).astype(BF16)
        for u in range(GROUP):
            mine = slice(u * MSG, (u + 1) * MSG)
            peak = jnp.maximum(
                jnp.max(scores[u], 1, keepdims=True), jnp.max(fresh[mine], 1, keepdims=True)
            )
            w_fresh = jnp.exp2((fresh[mine] - peak) * factor).astype(BF16)
            w = jnp.exp2((scores[u] - peak) * factor).astype(BF16)
            total = jnp.dot(w_fresh, values, preferred_element_type=F32)
            cached = jnp.concatenate([kv[at, 1] for at in places[u]], 0)
            total = total + jnp.dot(w, cached, preferred_element_type=F32)
            denom = jnp.sum(w.astype(F32), 1, keepdims=True) + jnp.sum(
                w_fresh.astype(F32), 1, keepdims=True
            )
            h_out[first + u] = (total / denom).astype(BF16)

    def wait_q(n):
        settle(q_in.at[n], q_recv.at[n])

    def heads_copy(n):
        return pltpu.make_async_remote_copy(
            src_ref=h_out.at[n], dst_ref=h_in.at[me], send_sem=h_send, recv_sem=h_recv.at[me],
            device_id={"replica": n}, device_id_type=MESH,
        )

    def attend_group(i, carry):
        g = mod(group - 1 - i, groups)
        for u in range(GROUP):
            n = g * GROUP + u

            @pl.when(n != me)
            def _():
                wait_q(n)

        attend(g)
        for u in range(GROUP):
            n = g * GROUP + u

            @pl.when(n != me)
            def _():
                heads_copy(n).start()

        return carry

    lax.fori_loop(0, groups, attend_group, 0, unroll=2)
    h_in[me] = h_out[me]
    share_near(0)
    share_near(1)
    to_mate[0].start()
    to_mate[1].start()
    def push(ref, i, other):
        copy = pltpu.make_async_remote_copy(
            src_ref=ref, dst_ref=ref, send_sem=x_send.at[i], recv_sem=x_recv.at[i],
            device_id={"tensor": other}, device_id_type=MESH,
        )
        copy.start()
        pushed.append(copy)
        return copy

    pushed = []
    halves = range(2)
    rows_of = [slice(v * half, (v + 1) * half) for v in halves]
    span_of = [pl.ds(v * half, half) for v in halves]
    to_right = [pl.ds(v * half, half // 2) for v in halves]
    to_left = [pl.ds(v * half + half // 2, half // 2) for v in halves]

    def collect(v):
        for i in range(v * groups // 2, (v + 1) * groups // 2):
            g = mod(group + 1 + i, groups)
            for u in range(GROUP):
                n = g * GROUP + u

                @pl.when(n != me)
                def _():
                    settle(h_in.at[n], h_recv.at[n])

            flat = h_in[pl.ds(g * GROUP, GROUP)].reshape(GROUP * MSG, HD)
            rows = jnp.dot(order[...], flat, preferred_element_type=F32).astype(BF16)
            for h in range(NQ):
                heads[tx, i * GS : (i + 1) * GS, h * HD : (h + 1) * HD] = rows[h * GS : (h + 1) * GS]

    heads_r, heads_l, heads_far = [], [], []
    for v in halves:
        collect(v)
        heads_r.append(push(heads.at[tx, span_of[v]], 4 * v, right))
        heads_l.append(push(heads.at[tx, span_of[v]], 4 * v + 1, left))
        if v == 0:
            pass_a.wait_recv()
            pass_b.wait_recv()
            to_mate[2].start()
            for e in range(4):
                spread[2][e].start()

    def pass_heads(v):
        heads_r[v].wait_recv()
        heads_far.append(push(heads.at[left, to_right[v]], 4 * v + 2, right))
        heads_l[v].wait_recv()
        heads_far.append(push(heads.at[right, to_left[v]], 4 * v + 3, left))

    def term(owner, rows):
        block = wf[pl.ds(pl.multiple_of(owner * KR, 16), KR), :]
        return jnp.dot(heads[owner, rows], block, preferred_element_type=F32)

    pass_heads(0)
    for e in range(4):
        for j in (0, 1):
            spread[j][e].wait_recv()
            rest_to_mate[j][e].start()
    wo_copy.wait()
    total[...] = term(tx, slice(0, M))
    for e in range(4):
        spread[2][e].wait_recv()
        rest_to_mate[2][e].start()
    for j in (0, 1):
        to_mate[j].wait_recv()
        for e in range(4):
            rest_to_mate[j][e].wait_recv()
    total[rows_of[0]] += term(left, rows_of[0]) + term(right, rows_of[0])
    pass_heads(1)
    to_mate[2].wait_recv()
    for e in range(4):
        rest_to_mate[2][e].wait_recv()

    def cols_of(owner):
        return pl.ds(pl.multiple_of(owner * DC, 128), DC)

    outs_r, outs_l, outs_far = [], [], []
    for v in halves:
        if v == 1:
            total[rows_of[1]] += term(left, rows_of[1]) + term(right, rows_of[1])
        heads_far[2 * v].wait_recv()
        heads_far[2 * v + 1].wait_recv()
        gathered[rows_of[v], cols_of(tx)] = (total[rows_of[v]] + term(opposite, rows_of[v])).astype(BF16)
        mine = gathered.at[span_of[v], cols_of(tx)]
        outs_r.append(push(mine, 8 + 4 * v, right))
        outs_l.append(push(mine, 9 + 4 * v, left))

    def place(owner):
        rows = jnp.dot(unpick[...], gathered[:, cols_of(owner)], preferred_element_type=F32)
        out_ref[:, cols_of(owner)] = rows.astype(BF16)

    for v in halves:
        outs_r[v].wait_recv()
        outs_far.append(push(gathered.at[to_right[v], cols_of(left)], 10 + 4 * v, right))
        outs_l[v].wait_recv()
        outs_far.append(push(gathered.at[to_left[v], cols_of(right)], 11 + 4 * v, left))
        if v == 0:
            place(tx)
    place(left)
    place(right)
    for copy in outs_far:
        copy.wait_recv()
    place(opposite)
    for copy in pushed:
        copy.wait_send()
    for copy in [far_a, far_b, pass_a, pass_b] + near_a + near_b + sum(spread + rest_to_mate, []) + to_mate:
        copy.wait_send()
    some = pl.ds(0, R - 1)
    settle(meta_out.at[some], meta_send)
    settle(q_out.at[some], q_send)
    settle(h_out.at[some], h_send)


def shards(
    replicas, tensors, hidden_in, norm_gain, w_query, w_key, w_value, w_out, kv_pages, lengths, page_table, destination
):
    S, R, D = hidden_in.shape
    T = tensors
    NQ = w_query.shape[1] // HD
    NH = NQ + 2
    M = S * R
    KC = min(1024, D // 2)
    DC = D // T
    pages, _, page, _ = kv_pages.shape
    any_spec = pl.BlockSpec(memory_space=pl.ANY)
    smem = pl.BlockSpec(memory_space=pltpu.SMEM)
    dma = pltpu.SemaphoreType.DMA
    out = pl.pallas_call(
        functools.partial(kernel, (R, T, S, NQ, D, KC)),
        out_shape=pltpu.VMEM((M, D), BF16),
        in_specs=[any_spec, any_spec, any_spec] + [any_spec] * 7,
        out_specs=pl.BlockSpec(memory_space=pltpu.VMEM),
        scratch_shapes=[
            pltpu.SMEM((R,), jnp.int32),
            pltpu.SMEM((R,), jnp.int32),
            pltpu.SMEM((pages // R, R), jnp.int32),
            pltpu.VMEM((1, D), F32),
            dma((4,)),
            pltpu.VMEM((M, D), BF16),
            pltpu.VMEM((D, NQ * HD), BF16),
            pltpu.VMEM((D, HD), BF16),
            pltpu.VMEM((D, HD), BF16),
            pltpu.VMEM(kv_pages.shape, BF16),
            pltpu.VMEM((T * w_out.shape[0], DC), BF16),
            pltpu.VMEM((2, w_out.shape[0] // 4, DC // 2), BF16),
            pltpu.VMEM((M, NH * HD), F32),
            pltpu.VMEM((R, 128), jnp.int32),
            pltpu.SMEM((R, 128), jnp.int32),
            pltpu.VMEM((R, 8, 128), jnp.int32),
            pltpu.VMEM((R, 8, 128), jnp.int32),
            pltpu.VMEM((NQ * GROUP * S, GROUP * MSG), BF16),
            pltpu.VMEM((M, M), BF16),
            pltpu.VMEM((M, D), BF16),
            pltpu.VMEM((NH * M, HD), BF16),
            pltpu.VMEM((R, MSG, HD), BF16),
            pltpu.VMEM((R, MSG, HD), BF16),
            pltpu.VMEM((R, MSG, HD), BF16),
            pltpu.VMEM((R, MSG, HD), BF16),
            pltpu.VMEM((T, M, NQ * HD), BF16),
            pltpu.VMEM((M, DC), F32),
            dma, dma((D // KC, 3)), dma((4,)), dma, dma,
            dma, dma, dma, dma((R,)), dma, dma((R,)), dma((16,)), dma((16,)), dma((38,)), dma((38,)),
        ],
        compiler_params=pltpu.CompilerParams(
            collective_id=0, has_side_effects=True, vmem_limit_bytes=58 * 1024 * 1024
        ),
        name="decode_attention",
    )(
        destination, lengths, page_table.T, norm_gain.reshape(1, D), hidden_in.reshape(M, D),
        w_query, w_key, w_value, w_out, kv_pages,
    )
    return out.reshape(S, R, D)


def solution(mesh):
    in_specs = (
        P(None, "replica", None),
        P(),
        P(None, "tensor"),
        P(None, "tensor"),
        P(None, "tensor"),
        P("tensor", None),
        P("replica", None, None, "tensor"),
        P("replica"),
        P("replica", None),
        P("replica"),
    )
    body = functools.partial(shards, mesh.shape["replica"], mesh.shape["tensor"])
    return jax.shard_map(
        body, mesh=mesh, in_specs=in_specs, out_specs=P(None, "replica", None), check_vma=False
    )
```

```python
import functools
import math

import jax
import jax.numpy as jnp
from jax import lax
from jax.experimental import pallas as pl
from jax.experimental.pallas import tpu as pltpu
from jax.sharding import PartitionSpec as P

HD = 128
GROUP = 4
MSG = 32
ROPE_BASE = 1000000.0
EPSILON = 1e-06
SUBS = 2
CHIPS_Z = 4
MESH = pl.DeviceIdType.MESH
F32 = jnp.float32
BF16 = jnp.bfloat16


def mod(value, size):
    return lax.rem(value + 2 * size, size)


def settle(ref, sem):
    pltpu.make_async_copy(ref, ref, sem).wait()


def kernel(
    sizes,
    dest_hbm, len_hbm, table_hbm, gain_hbm, hid_hbm, wq_hbm, wk_hbm, wv_hbm, wo_hbm, kv_hbm,
    out_ref,
    dest_sm, len_sm, table_sm, gain_ref, small_sem,
    hid, wq, wk, wv, kv, wf, relay, acc, code, code_sm, meta_out, meta_in, unpick, by_head, stack,
    q_out, q_in, h_out, h_in, heads, total,
    hid_sem, w_sem, kv_sem, wo_sem, code_sem,
    meta_send, meta_recv, q_send, q_recv, h_send, h_recv, x_send, x_recv, f_send, f_recv,
):
    R, T, S, NQ, D, KC = sizes
    M = S * R
    NH = NQ + 2
    me = lax.axis_index("replica")
    tx = lax.axis_index("tensor")
    chunks = D // KC
    group = me // GROUP
    groups = R // GROUP
    DC = D // T
    half = M // 2
    pages = kv.shape[0]
    max_pages = pages // R
    page = kv.shape[2]
    KR = wo_hbm.shape[0]
    HB, QB = KR // 2, KR // 8
    HC = DC // 2
    core = me % 2
    mate = me + 1 - 2 * core
    chip = me // 2
    z, y = chip % CHIPS_Z, chip // CHIPS_Z
    chips_y = R // (2 * CHIPS_Z)
    parity = (y + z) % 2
    opposite = mod(tx + 2, T)

    def at(yy, zz):
        return (mod(yy, chips_y) * CHIPS_Z + mod(zz, CHIPS_Z)) * 2 + core

    around = (at(y + 1, z), at(y - 1, z), at(y, z + 1), at(y, z - 1))

    def rows_at(owner, first, size):
        return pl.ds(pl.multiple_of(owner * KR + first, 16), size)

    half_cols = pl.ds(pl.multiple_of(core * HC, 128), HC)

    def own_rows(target, first, size):
        cols = pl.ds(pl.multiple_of(target * DC + core * HC, 128), HC)
        return wo_hbm.at[pl.ds(pl.multiple_of(first, 16), size), cols]

    def weight_piece(src, dst, i, other):
        return pltpu.make_async_remote_copy(
            src_ref=src, dst_ref=dst, send_sem=f_send.at[i], recv_sem=f_recv.at[i],
            device_id=other, device_id_type=MESH,
        )

    def held(owner, first, size):
        return wf.at[rows_at(owner, first, size), half_cols]

    def same_place(owner, first, size, i, other):
        return weight_piece(held(owner, first, size), held(owner, first, size), i, {"replica": other})

    right = mod(tx + 1, T)
    left = mod(tx - 1, T)
    fetched, missing = parity * HB, (1 - parity) * HB
    QH2 = HB // 2
    far_a = weight_piece(own_rows(opposite, fetched, QH2), relay.at[0], 0, {"tensor": right})
    far_b = weight_piece(own_rows(opposite, fetched + QH2, QH2), relay.at[1], 1, {"tensor": left})
    near_a, near_b = (
        [
            weight_piece(
                own_rows(target, fetched + p * QH2, QH2), held(tx, fetched + p * QH2, QH2), 2 + 2 * p + i,
                {"tensor": target},
            )
            for p in range(2)
        ]
        for i, target in enumerate((right, left))
    )
    pass_a = weight_piece(relay.at[0], held(left, fetched, QH2), 24, {"tensor": right})
    pass_b = weight_piece(relay.at[1], held(right, fetched + QH2, QH2), 25, {"tensor": left})
    owners = (left, right, opposite)
    spread = [
        [same_place(owner, fetched + e * QB, QB, 6 + 4 * j + e, around[e]) for e in range(4)]
        for j, owner in enumerate(owners)
    ]
    to_mate = [same_place(owner, fetched, HB, 18 + j, mate) for j, owner in enumerate(owners)]
    rest_to_mate = [same_place(owner, missing, HB, 21 + j, mate) for j, owner in enumerate(owners)]

    def weight_copies(c):
        rows = pl.ds(pl.multiple_of(c * KC, KC), KC)
        return (
            pltpu.make_async_copy(wq_hbm.at[rows], wq.at[rows], w_sem.at[c, 0]),
            pltpu.make_async_copy(wk_hbm.at[rows], wk.at[rows], w_sem.at[c, 1]),
            pltpu.make_async_copy(wv_hbm.at[rows], wv.at[rows], w_sem.at[c, 2]),
        )

    small = [
        pltpu.make_async_copy(src, dst, small_sem.at[i])
        for i, (src, dst) in enumerate(
            ((dest_hbm, dest_sm), (len_hbm, len_sm), (gain_hbm, gain_ref), (table_hbm, table_sm))
        )
    ]
    for copy in small:
        copy.start()
    hid_copy = pltpu.make_async_copy(hid_hbm, hid, hid_sem)
    hid_copy.start()
    def load(c):
        if c < chunks:
            for copy in weight_copies(c):
                copy.start()

    barrier = pltpu.get_barrier_semaphore()

    def far_first(k):
        return R // 2 + (1 - 2 * (k % 2)) * ((k + 1) // 2)

    def greet(k, carry):
        n = mod(me + far_first(k), R)
        pl.semaphore_signal(barrier, inc=1, device_id={"replica": n}, device_id_type=MESH)
        return carry

    lax.fori_loop(0, R - 1, greet, 0, unroll=True)
    for other in (right, left):
        pl.semaphore_signal(barrier, inc=1, device_id={"tensor": other}, device_id_type=MESH)

    load(0)
    load(1)

    small[0].wait()
    small[1].wait()
    numbers = lax.broadcasted_iota(jnp.int32, (R, 128), 0)
    codes = jnp.zeros((R, 128), jnp.int32)
    for b in range(R):
        codes = jnp.where(numbers == dest_sm[b], len_sm[b] * R + b, codes)
    code[...] = codes
    code_copy = pltpu.make_async_copy(code, code_sm, code_sem)
    code_copy.start()
    for n in range(R):
        meta_out[n] = jnp.broadcast_to(codes[n : n + 1], (8, 128))

    pl.semaphore_wait(barrier, R - 1 + 2)

    def to_all(make):
        def send(k, carry):
            n = mod(group * GROUP + GROUP + k, R)

            @pl.when(n != me)
            def _():
                make(n).start()

            return carry

        lax.fori_loop(0, R, send, 0)

    def meta_copy(n):
        return pltpu.make_async_remote_copy(
            src_ref=meta_out.at[n], dst_ref=meta_in.at[me], send_sem=meta_send, recv_sem=meta_recv,
            device_id={"replica": n}, device_id_type=MESH,
        )

    def send_meta(k, carry):
        meta_copy(mod(me + far_first(k), R)).start()
        return carry

    lax.fori_loop(0, R - 1, send_meta, 0, unroll=True)
    far_a.start()
    far_b.start()

    hid_copy.wait()
    small[2].wait()
    load(2)
    squares = jnp.zeros((M, 128), F32)
    for c in range(D // 128):
        wide = hid[:, c * 128 : (c + 1) * 128].astype(F32)
        squares = squares + wide * wide
    load(3)
    scale = lax.rsqrt(jnp.sum(squares, 1, keepdims=True) * (1.0 / D) + EPSILON)

    for c in range(0, D, 512):
        cols = slice(c, c + 512)
        hid[:, cols] = (hid[:, cols].astype(F32) * scale * gain_ref[:, cols]).astype(BF16)

    for c in range(4, chunks):
        load(c)
    kv_copies = []
    step = pages // 4
    for c in range(4):
        rows = pl.ds(c * step, step)
        kv_copies.append(pltpu.make_async_copy(kv_hbm.at[rows], kv.at[rows], kv_sem.at[c]))

    def project(c):
        for copy in weight_copies(c):
            copy.wait()
        if c + 1 == chunks:
            for copy in kv_copies:
                copy.start()
        cols = slice(c * KC, (c + 1) * KC)
        weights = jnp.concatenate([wq[cols], wk[cols], wv[cols]], 1)
        term = jnp.dot(hid[:, cols], weights, preferred_element_type=F32)
        acc[...] = term if c == 0 else acc[...] + term

    for c in range(chunks):
        project(c)
        if c == chunks // 2:
            near_a[0].start()
            near_b[0].start()

    def share_near(p):
        near_a[p].wait_recv()
        near_b[p].wait_recv()
        for j in (0, 1):
            for e in (2 * p, 2 * p + 1):
                spread[j][e].start()

    near_a[1].start()
    near_b[1].start()
    settle(meta_in.at[pl.ds(0, R - 1)], meta_recv)
    meta_in[me] = meta_out[me]

    slot_rows = lax.broadcasted_iota(jnp.int32, (R, 128), 0)
    lens = jnp.zeros((R, 128), jnp.int32)
    for o in range(R):
        tile = meta_in[o]
        slot_wide = jnp.concatenate([tile & (R - 1)] * (R // 8), 0)
        len_wide = jnp.concatenate([lax.shift_right_logical(tile, int(math.log2(R)))] * (R // 8), 0)
        lens = jnp.where(slot_rows == slot_wide, len_wide, lens)

    freq_lane = lax.broadcasted_iota(jnp.int32, (8, 128), 1) % (HD // 2)
    freq = jnp.exp(freq_lane.astype(F32) * (-2.0 / HD * math.log(ROPE_BASE)))
    angle = lens.astype(F32) * jnp.concatenate([freq] * (R // 8), 0)
    cos_len, sin_len = jnp.cos(angle), jnp.sin(angle)
    sign = jnp.where(lax.broadcasted_iota(jnp.int32, (R, 128), 1) < HD // 2, -1.0, 1.0)
    cosines, sines = [], []
    for s in range(S):
        if s == 0:
            cosines.append(cos_len)
            sines.append(sin_len * sign)
            continue
        cos_s = jnp.concatenate([jnp.cos(freq * float(s))] * (R // 8), 0)
        sin_s = jnp.concatenate([jnp.sin(freq * float(s))] * (R // 8), 0)
        cosines.append(cos_len * cos_s - sin_len * sin_s)
        sines.append((sin_len * cos_s + cos_len * sin_s) * sign)
    cosine = jnp.concatenate(cosines, 0)
    sine = jnp.concatenate(sines, 0)


    for h in range(NH):
        vec = acc[:, h * HD : (h + 1) * HD]
        if h <= NQ:
            vec = vec * cosine + pltpu.roll(vec, HD // 2, 1) * sine
        stack[h * M : (h + 1) * M, :] = vec.astype(BF16)

    def q_copy(o):
        return pltpu.make_async_remote_copy(
            src_ref=q_out.at[o], dst_ref=q_in.at[me], send_sem=q_send, recv_sem=q_recv.at[me],
            device_id={"replica": o}, device_id_type=MESH,
        )

    msg_row = lax.broadcasted_iota(jnp.int32, (MSG, 128), 0)
    lane = lax.broadcasted_iota(jnp.int32, (MSG, 128), 1)

    def send_group(i, carry):
        first = mod(group + 1 + i, groups) * GROUP
        blocks = []
        for u in range(GROUP):
            slot = meta_in[first + u] & (R - 1)
            target = R * msg_row + jnp.concatenate([slot] * (MSG // 8), 0)
            parts = []
            for c in range(0, NH * M, 128):
                hit = jnp.where(target == lane + c, 1.0, 0.0).astype(BF16)
                parts.append(hit[:, : min(128, NH * M - c)])
            blocks.append(jnp.concatenate(parts, 1))
        pick = jnp.concatenate(blocks, 0)
        rows = jnp.dot(pick, stack[...], preferred_element_type=F32)
        q_out[pl.ds(first, GROUP)] = rows.astype(BF16).reshape(GROUP, MSG, HD)
        for u in range(GROUP):

            @pl.when(first + u != me)
            def _():
                q_copy(first + u).start()

        return carry

    lax.fori_loop(0, groups, send_group, 0, unroll=2)
    q_in[me] = q_out[me]
    wo_copy = pltpu.make_async_copy(
        wo_hbm.at[:, pl.ds(pl.multiple_of(tx * DC, 128), DC)], wf.at[rows_at(tx, 0, KR)], wo_sem
    )
    wo_copy.start()
    per = 128 // MSG
    group_of_lane = lax.broadcasted_iota(jnp.int32, (8, 128), 1) // MSG
    row_of_lane = lax.broadcasted_iota(jnp.int32, (8, 128), 1) % MSG
    wide_row = lax.broadcasted_iota(jnp.int32, (NQ * M, 128), 0)
    for g in range(R // per):
        slots = jnp.zeros((8, 128), jnp.int32)
        for i in range(per):
            slots = jnp.where(group_of_lane == i, meta_in[g * per + i] & (R - 1), slots)
        target = jnp.concatenate([R * row_of_lane + slots] * (NQ * M // 8), 0)
        unpick[:, g * 128 : (g + 1) * 128] = jnp.where(target == wide_row, 1.0, 0.0).astype(BF16)

    far_a.wait_recv()
    pass_a.start()
    far_b.wait_recv()
    pass_b.start()
    code_copy.wait()
    small[3].wait()
    for copy in kv_copies:
        copy.wait()

    span = max_pages * page
    rows = GROUP * MSG
    tok = lax.broadcasted_iota(jnp.int32, (MSG, span), 1)
    f_row = lax.broadcasted_iota(jnp.int32, (rows, rows), 0)
    f_col = lax.broadcasted_iota(jnp.int32, (rows, rows), 1)
    f_key = f_col % MSG - NQ * S
    fresh_ok = (f_row // MSG == f_col // MSG) & (f_key >= 0) & (f_key <= f_row % S)
    factor = math.log2(math.e) / math.sqrt(HD)
    dims = (((1,), (1,)), ((), ()))

    def attend(g):
        first = g * GROUP
        q = q_in[pl.ds(first, GROUP)].reshape(rows, HD)
        fresh = lax.dot_general(q, q, dims, preferred_element_type=F32)
        fresh = jnp.where(fresh_ok, fresh, -jnp.inf)
        places, scores = [], []
        for u in range(GROUP):
            word = code_sm[first + u, 0]
            slot = word & (R - 1)
            length = lax.shift_right_logical(word, int(math.log2(R)))
            places.append([table_sm[p, slot] for p in range(max_pages)])
            keys = jnp.concatenate([kv[at, 0] for at in places[u]], 0)
            sc = lax.dot_general(q[u * MSG : (u + 1) * MSG], keys, dims, preferred_element_type=F32)
            scores.append(jnp.where(tok < length, sc, -jnp.inf))
        values = pltpu.roll(q.astype(F32), rows - S, 0).astype(BF16)
        for u in range(GROUP):
            mine = slice(u * MSG, (u + 1) * MSG)
            peak = jnp.maximum(
                jnp.max(scores[u], 1, keepdims=True), jnp.max(fresh[mine], 1, keepdims=True)
            )
            w_fresh = jnp.exp2((fresh[mine] - peak) * factor).astype(BF16)
            w = jnp.exp2((scores[u] - peak) * factor).astype(BF16)
            total = jnp.dot(w_fresh, values, preferred_element_type=F32)
            cached = jnp.concatenate([kv[at, 1] for at in places[u]], 0)
            total = total + jnp.dot(w, cached, preferred_element_type=F32)
            denom = jnp.sum(w.astype(F32), 1, keepdims=True) + jnp.sum(
                w_fresh.astype(F32), 1, keepdims=True
            )
            h_out[first + u] = (total / denom).astype(BF16)

    def wait_q(n):
        settle(q_in.at[n], q_recv.at[n])

    def heads_copy(n):
        return pltpu.make_async_remote_copy(
            src_ref=h_out.at[n], dst_ref=h_in.at[me], send_sem=h_send, recv_sem=h_recv.at[me],
            device_id={"replica": n}, device_id_type=MESH,
        )

    def attend_group(i, carry):
        g = mod(group - 1 - i, groups)
        for u in range(GROUP):
            n = g * GROUP + u

            @pl.when(n != me)
            def _():
                wait_q(n)

        attend(g)
        for u in range(GROUP):
            n = g * GROUP + u

            @pl.when(n != me)
            def _():
                heads_copy(n).start()

        return carry

    lax.fori_loop(0, groups, attend_group, 0, unroll=4)
    h_in[me] = h_out[me]
    share_near(0)
    share_near(1)
    to_mate[0].start()
    to_mate[1].start()
    def collect(i, carry):
        g = mod(group + 1 + i, groups)
        for u in range(GROUP):
            n = g * GROUP + u

            @pl.when(n != me)
            def _():
                settle(h_in.at[n], h_recv.at[n])

        flat = h_in[pl.ds(g * GROUP, GROUP)].reshape(GROUP * MSG, HD)
        cols = pl.ds(pl.multiple_of(g * 128, 128), 128)
        rows = jnp.dot(unpick[:, cols], flat, preferred_element_type=F32)
        by_head[...] += rows
        return carry

    by_head[...] = jnp.zeros_like(by_head)
    lax.fori_loop(0, groups, collect, 0)
    for h in range(NQ):
        heads[tx, :, h * HD : (h + 1) * HD] = by_head[h * M : (h + 1) * M].astype(BF16)

    def push(ref, i, other):
        copy = pltpu.make_async_remote_copy(
            src_ref=ref, dst_ref=ref, send_sem=x_send.at[i], recv_sem=x_recv.at[i],
            device_id={"tensor": other}, device_id_type=MESH,
        )
        copy.start()
        return copy

    low, high = pl.ds(0, half), pl.ds(half, half)
    g0 = push(heads.at[tx, low], 0, right)
    g1 = push(heads.at[tx, high], 1, left)
    g2 = push(heads.at[tx, high], 2, right)
    g3 = push(heads.at[tx, low], 3, left)
    pass_a.wait_recv()
    pass_b.wait_recv()
    to_mate[2].start()
    for e in range(4):
        spread[2][e].start()

    def term(owner, cols):
        rows = pl.ds(pl.multiple_of(owner * KR, 16), KR)
        return jnp.dot(heads[owner], wf[rows, cols], preferred_element_type=F32)

    every = slice(0, DC)
    wo_copy.wait()
    total[...] = term(tx, every)
    for j in (0, 1):
        for e in range(4):
            spread[j][e].wait_recv()
        rest_to_mate[j].start()
    for e in range(4):
        spread[2][e].wait_recv()
    rest_to_mate[2].start()
    g0.wait_recv()
    g4 = push(heads.at[left, low], 4, right)
    g1.wait_recv()
    g5 = push(heads.at[right, high], 5, left)
    g2.wait_recv()
    to_mate[0].wait_recv()
    rest_to_mate[0].wait_recv()
    total[...] += term(left, every)
    g3.wait_recv()
    to_mate[1].wait_recv()
    rest_to_mate[1].wait_recv()
    total[...] += term(right, every)
    to_mate[2].wait_recv()
    rest_to_mate[2].wait_recv()
    g4.wait_recv()
    g5.wait_recv()

    wide = DC // SUBS

    def cols_of(owner, b):
        return pl.ds(pl.multiple_of(owner * DC + b * wide, 128), wide)

    done = [g0, g1, g2, g3, g4, g5]
    first_r, first_l, second = [], [], []
    for b in range(SUBS):
        part = slice(b * wide, (b + 1) * wide)
        mine = cols_of(tx, b)
        out_ref[:, mine] = (total[:, part] + term(opposite, part)).astype(BF16)
        i = 6 + 6 * b
        first_r.append(push(out_ref.at[low, mine], i, right))
        first_l.append(push(out_ref.at[high, mine], i + 1, left))
        second.append(push(out_ref.at[high, mine], i + 2, right))
        second.append(push(out_ref.at[low, mine], i + 3, left))
    for b in range(SUBS):
        i = 6 + 6 * b
        first_r[b].wait_recv()
        second.append(push(out_ref.at[low, cols_of(left, b)], i + 4, right))
        first_l[b].wait_recv()
        second.append(push(out_ref.at[high, cols_of(right, b)], i + 5, left))
    for copy in second:
        copy.wait_recv()
    for copy in done + first_r + first_l + second:
        copy.wait_send()
    for copy in [far_a, far_b, pass_a, pass_b] + near_a + near_b + sum(spread, []) + to_mate + rest_to_mate:
        copy.wait_send()
    some = pl.ds(0, R - 1)
    settle(meta_out.at[some], meta_send)
    settle(q_out.at[some], q_send)
    settle(h_out.at[some], h_send)


def shards(
    replicas, tensors, hidden_in, norm_gain, w_query, w_key, w_value, w_out, kv_pages, lengths, page_table, destination
):
    S, R, D = hidden_in.shape
    T = tensors
    NQ = w_query.shape[1] // HD
    NH = NQ + 2
    M = S * R
    KC = min(1024, D // 2)
    DC = D // T
    pages, _, page, _ = kv_pages.shape
    any_spec = pl.BlockSpec(memory_space=pl.ANY)
    smem = pl.BlockSpec(memory_space=pltpu.SMEM)
    dma = pltpu.SemaphoreType.DMA
    out = pl.pallas_call(
        functools.partial(kernel, (R, T, S, NQ, D, KC)),
        out_shape=pltpu.VMEM((M, D), BF16),
        in_specs=[any_spec, any_spec, any_spec] + [any_spec] * 7,
        out_specs=pl.BlockSpec(memory_space=pltpu.VMEM),
        scratch_shapes=[
            pltpu.SMEM((R,), jnp.int32),
            pltpu.SMEM((R,), jnp.int32),
            pltpu.SMEM((pages // R, R), jnp.int32),
            pltpu.VMEM((1, D), F32),
            dma((4,)),
            pltpu.VMEM((M, D), BF16),
            pltpu.VMEM((D, NQ * HD), BF16),
            pltpu.VMEM((D, HD), BF16),
            pltpu.VMEM((D, HD), BF16),
            pltpu.VMEM(kv_pages.shape, BF16),
            pltpu.VMEM((T * w_out.shape[0], DC), BF16),
            pltpu.VMEM((2, w_out.shape[0] // 4, DC // 2), BF16),
            pltpu.VMEM((M, NH * HD), F32),
            pltpu.VMEM((R, 128), jnp.int32),
            pltpu.SMEM((R, 128), jnp.int32),
            pltpu.VMEM((R, 8, 128), jnp.int32),
            pltpu.VMEM((R, 8, 128), jnp.int32),
            pltpu.VMEM((NQ * M, R * MSG), BF16),
            pltpu.VMEM((NQ * M, HD), F32),
            pltpu.VMEM((NH * M, HD), BF16),
            pltpu.VMEM((R, MSG, HD), BF16),
            pltpu.VMEM((R, MSG, HD), BF16),
            pltpu.VMEM((R, MSG, HD), BF16),
            pltpu.VMEM((R, MSG, HD), BF16),
            pltpu.VMEM((T, M, NQ * HD), BF16),
            pltpu.VMEM((M, DC), F32),
            dma, dma((D // KC, 3)), dma((4,)), dma, dma,
            dma, dma, dma, dma((R,)), dma, dma((R,)), dma((6 + 6 * SUBS,)), dma((6 + 6 * SUBS,)), dma((26,)), dma((26,)),
        ],
        compiler_params=pltpu.CompilerParams(
            collective_id=0, has_side_effects=True, vmem_limit_bytes=58 * 1024 * 1024
        ),
        name="decode_attention",
    )(
        destination, lengths, page_table.T, norm_gain.reshape(1, D), hidden_in.reshape(M, D),
        w_query, w_key, w_value, w_out, kv_pages,
    )
    return out.reshape(S, R, D)


def solution(mesh):
    in_specs = (
        P(None, "replica", None),
        P(),
        P(None, "tensor"),
        P(None, "tensor"),
        P(None, "tensor"),
        P("tensor", None),
        P("replica", None, None, "tensor"),
        P("replica"),
        P("replica", None),
        P("replica"),
    )
    body = functools.partial(shards, mesh.shape["replica"], mesh.shape["tensor"])
    return jax.shard_map(
        body, mesh=mesh, in_specs=in_specs, out_specs=P(None, "replica", None), check_vma=False
    )
```

```python
import functools
import math

import jax
import jax.numpy as jnp
from jax import lax
from jax.experimental import pallas as pl
from jax.experimental.pallas import tpu as pltpu
from jax.sharding import PartitionSpec as P

HD = 128
GROUP = 4
MSG = 32
ROPE_BASE = 1000000.0
EPSILON = 1e-06
SUBS = 2
CHIPS_Z = 4
MESH = pl.DeviceIdType.MESH
F32 = jnp.float32
BF16 = jnp.bfloat16


def mod(value, size):
    return lax.rem(value + 2 * size, size)


def settle(ref, sem):
    pltpu.make_async_copy(ref, ref, sem).wait()


def kernel(
    sizes,
    dest_hbm, len_hbm, table_hbm, gain_hbm, hid_hbm, wq_hbm, wk_hbm, wv_hbm, wo_hbm, kv_hbm,
    out_ref,
    dest_sm, len_sm, table_sm, gain_ref, small_sem,
    hid, wq, wk, wv, kv, wf, relay, acc, code, code_sm, meta_out, meta_in, unpick, by_head, stack,
    q_out, q_in, h_out, h_in, heads, total,
    hid_sem, w_sem, kv_sem, wo_sem, code_sem,
    meta_send, meta_recv, q_send, q_recv, h_send, h_recv, x_send, x_recv, f_send, f_recv,
):
    R, T, S, NQ, D, KC = sizes
    M = S * R
    NH = NQ + 2
    me = lax.axis_index("replica")
    tx = lax.axis_index("tensor")
    chunks = D // KC
    group = me // GROUP
    groups = R // GROUP
    DC = D // T
    half = M // 2
    pages = kv.shape[0]
    max_pages = pages // R
    page = kv.shape[2]
    KR = wo_hbm.shape[0]
    HB, QB = KR // 2, KR // 8
    HC = DC // 2
    core = me % 2
    mate = me + 1 - 2 * core
    chip = me // 2
    z, y = chip % CHIPS_Z, chip // CHIPS_Z
    chips_y = R // (2 * CHIPS_Z)
    parity = (y + z) % 2
    opposite = mod(tx + 2, T)

    def at(yy, zz):
        return (mod(yy, chips_y) * CHIPS_Z + mod(zz, CHIPS_Z)) * 2 + core

    around = (at(y + 1, z), at(y - 1, z), at(y, z + 1), at(y, z - 1))

    def rows_at(owner, first, size):
        return pl.ds(pl.multiple_of(owner * KR + first, 16), size)

    half_cols = pl.ds(pl.multiple_of(core * HC, 128), HC)

    def own_rows(target, first, size):
        cols = pl.ds(pl.multiple_of(target * DC + core * HC, 128), HC)
        return wo_hbm.at[pl.ds(pl.multiple_of(first, 16), size), cols]

    def weight_piece(src, dst, i, other):
        return pltpu.make_async_remote_copy(
            src_ref=src, dst_ref=dst, send_sem=f_send.at[i], recv_sem=f_recv.at[i],
            device_id=other, device_id_type=MESH,
        )

    def held(owner, first, size):
        return wf.at[rows_at(owner, first, size), half_cols]

    def same_place(owner, first, size, i, other):
        return weight_piece(held(owner, first, size), held(owner, first, size), i, {"replica": other})

    right = mod(tx + 1, T)
    left = mod(tx - 1, T)
    fetched, missing = parity * HB, (1 - parity) * HB
    QH2 = HB // 2
    far_a = weight_piece(own_rows(opposite, fetched, QH2), relay.at[0], 0, {"tensor": right})
    far_b = weight_piece(own_rows(opposite, fetched + QH2, QH2), relay.at[1], 1, {"tensor": left})
    near_a, near_b = (
        [
            weight_piece(
                own_rows(target, fetched + p * QH2, QH2), held(tx, fetched + p * QH2, QH2), 2 + 2 * p + i,
                {"tensor": target},
            )
            for p in range(2)
        ]
        for i, target in enumerate((right, left))
    )
    pass_a = weight_piece(relay.at[0], held(left, fetched, QH2), 24, {"tensor": right})
    pass_b = weight_piece(relay.at[1], held(right, fetched + QH2, QH2), 25, {"tensor": left})
    owners = (left, right, opposite)
    spread = [
        [same_place(owner, fetched + e * QB, QB, 6 + 4 * j + e, around[e]) for e in range(4)]
        for j, owner in enumerate(owners)
    ]
    to_mate = [same_place(owner, fetched, HB, 18 + j, mate) for j, owner in enumerate(owners)]
    rest_to_mate = [same_place(owner, missing, HB, 21 + j, mate) for j, owner in enumerate(owners)]

    def weight_copies(c):
        rows = pl.ds(pl.multiple_of(c * KC, KC), KC)
        return (
            pltpu.make_async_copy(wq_hbm.at[rows], wq.at[rows], w_sem.at[c, 0]),
            pltpu.make_async_copy(wk_hbm.at[rows], wk.at[rows], w_sem.at[c, 1]),
            pltpu.make_async_copy(wv_hbm.at[rows], wv.at[rows], w_sem.at[c, 2]),
        )

    small = [
        pltpu.make_async_copy(src, dst, small_sem.at[i])
        for i, (src, dst) in enumerate(
            ((dest_hbm, dest_sm), (len_hbm, len_sm), (gain_hbm, gain_ref), (table_hbm, table_sm))
        )
    ]
    for copy in small:
        copy.start()
    hid_copy = pltpu.make_async_copy(hid_hbm, hid, hid_sem)
    hid_copy.start()
    def load(c):
        if c < chunks:
            for copy in weight_copies(c):
                copy.start()

    barrier = pltpu.get_barrier_semaphore()

    def far_first(k):
        return R // 2 + (1 - 2 * (k % 2)) * ((k + 1) // 2)

    def greet(k, carry):
        n = mod(me + far_first(k), R)
        pl.semaphore_signal(barrier, inc=1, device_id={"replica": n}, device_id_type=MESH)
        return carry

    lax.fori_loop(0, R - 1, greet, 0, unroll=True)
    for other in (right, left):
        pl.semaphore_signal(barrier, inc=1, device_id={"tensor": other}, device_id_type=MESH)

    load(0)
    load(1)

    small[0].wait()
    small[1].wait()
    numbers = lax.broadcasted_iota(jnp.int32, (R, 128), 0)
    codes = jnp.zeros((R, 128), jnp.int32)
    for b in range(R):
        codes = jnp.where(numbers == dest_sm[b], len_sm[b] * R + b, codes)
    code[...] = codes
    code_copy = pltpu.make_async_copy(code, code_sm, code_sem)
    code_copy.start()
    for n in range(R):
        meta_out[n] = jnp.broadcast_to(codes[n : n + 1], (8, 128))

    pl.semaphore_wait(barrier, R - 1 + 2)

    def to_all(make):
        def send(k, carry):
            n = mod(group * GROUP + GROUP + k, R)

            @pl.when(n != me)
            def _():
                make(n).start()

            return carry

        lax.fori_loop(0, R, send, 0)

    def meta_copy(n):
        return pltpu.make_async_remote_copy(
            src_ref=meta_out.at[n], dst_ref=meta_in.at[me], send_sem=meta_send, recv_sem=meta_recv,
            device_id={"replica": n}, device_id_type=MESH,
        )

    def send_meta(k, carry):
        meta_copy(mod(me + far_first(k), R)).start()
        return carry

    lax.fori_loop(0, R - 1, send_meta, 0, unroll=True)
    far_a.start()
    far_b.start()

    hid_copy.wait()
    small[2].wait()
    load(2)
    squares = jnp.zeros((M, 128), F32)
    for c in range(D // 128):
        wide = hid[:, c * 128 : (c + 1) * 128].astype(F32)
        squares = squares + wide * wide
    load(3)
    scale = lax.rsqrt(jnp.sum(squares, 1, keepdims=True) * (1.0 / D) + EPSILON)

    for c in range(0, D, 512):
        cols = slice(c, c + 512)
        hid[:, cols] = (hid[:, cols].astype(F32) * scale * gain_ref[:, cols]).astype(BF16)

    for c in range(4, chunks):
        load(c)
    kv_copies = []
    step = pages // 4
    for c in range(4):
        rows = pl.ds(c * step, step)
        kv_copies.append(pltpu.make_async_copy(kv_hbm.at[rows], kv.at[rows], kv_sem.at[c]))

    def project(c):
        for copy in weight_copies(c):
            copy.wait()
        if c + 1 == chunks:
            for copy in kv_copies:
                copy.start()
        cols = slice(c * KC, (c + 1) * KC)
        weights = jnp.concatenate([wq[cols], wk[cols], wv[cols]], 1)
        term = jnp.dot(hid[:, cols], weights, preferred_element_type=F32)
        acc[...] = term if c == 0 else acc[...] + term

    for c in range(chunks):
        project(c)
        if c == chunks // 2:
            near_a[0].start()
            near_b[0].start()

    def share_near(p):
        near_a[p].wait_recv()
        near_b[p].wait_recv()
        for j in (0, 1):
            for e in (2 * p, 2 * p + 1):
                spread[j][e].start()

    near_a[1].start()
    near_b[1].start()
    settle(meta_in.at[pl.ds(0, R - 1)], meta_recv)
    meta_in[me] = meta_out[me]

    slot_rows = lax.broadcasted_iota(jnp.int32, (R, 128), 0)
    lens = jnp.zeros((R, 128), jnp.int32)
    for o in range(R):
        tile = meta_in[o]
        slot_wide = jnp.concatenate([tile & (R - 1)] * (R // 8), 0)
        len_wide = jnp.concatenate([lax.shift_right_logical(tile, int(math.log2(R)))] * (R // 8), 0)
        lens = jnp.where(slot_rows == slot_wide, len_wide, lens)

    freq_lane = lax.broadcasted_iota(jnp.int32, (8, 128), 1) % (HD // 2)
    freq = jnp.exp(freq_lane.astype(F32) * (-2.0 / HD * math.log(ROPE_BASE)))
    angle = lens.astype(F32) * jnp.concatenate([freq] * (R // 8), 0)
    cos_len, sin_len = jnp.cos(angle), jnp.sin(angle)
    sign = jnp.where(lax.broadcasted_iota(jnp.int32, (R, 128), 1) < HD // 2, -1.0, 1.0)
    cosines, sines = [], []
    for s in range(S):
        if s == 0:
            cosines.append(cos_len)
            sines.append(sin_len * sign)
            continue
        cos_s = jnp.concatenate([jnp.cos(freq * float(s))] * (R // 8), 0)
        sin_s = jnp.concatenate([jnp.sin(freq * float(s))] * (R // 8), 0)
        cosines.append(cos_len * cos_s - sin_len * sin_s)
        sines.append((sin_len * cos_s + cos_len * sin_s) * sign)
    cosine = jnp.concatenate(cosines, 0)
    sine = jnp.concatenate(sines, 0)


    for h in range(NH):
        vec = acc[:, h * HD : (h + 1) * HD]
        if h <= NQ:
            vec = vec * cosine + pltpu.roll(vec, HD // 2, 1) * sine
        stack[h * M : (h + 1) * M, :] = vec.astype(BF16)

    def q_copy(o):
        return pltpu.make_async_remote_copy(
            src_ref=q_out.at[o], dst_ref=q_in.at[me], send_sem=q_send, recv_sem=q_recv.at[me],
            device_id={"replica": o}, device_id_type=MESH,
        )

    msg_row = lax.broadcasted_iota(jnp.int32, (MSG, 128), 0)
    lane = lax.broadcasted_iota(jnp.int32, (MSG, 128), 1)

    def send_group(i, carry):
        first = mod(group + 1 + i, groups) * GROUP
        blocks = []
        for u in range(GROUP):
            slot = meta_in[first + u] & (R - 1)
            target = R * msg_row + jnp.concatenate([slot] * (MSG // 8), 0)
            parts = []
            for c in range(0, NH * M, 128):
                hit = jnp.where(target == lane + c, 1.0, 0.0).astype(BF16)
                parts.append(hit[:, : min(128, NH * M - c)])
            blocks.append(jnp.concatenate(parts, 1))
        pick = jnp.concatenate(blocks, 0)
        rows = jnp.dot(pick, stack[...], preferred_element_type=F32)
        q_out[pl.ds(first, GROUP)] = rows.astype(BF16).reshape(GROUP, MSG, HD)
        for u in range(GROUP):

            @pl.when(first + u != me)
            def _():
                q_copy(first + u).start()

        return carry

    lax.fori_loop(0, groups, send_group, 0, unroll=2)
    q_in[me] = q_out[me]
    wo_copy = pltpu.make_async_copy(
        wo_hbm.at[:, pl.ds(pl.multiple_of(tx * DC, 128), DC)], wf.at[rows_at(tx, 0, KR)], wo_sem
    )
    wo_copy.start()
    per = 128 // MSG
    group_of_lane = lax.broadcasted_iota(jnp.int32, (8, 128), 1) // MSG
    row_of_lane = lax.broadcasted_iota(jnp.int32, (8, 128), 1) % MSG
    wide_row = lax.broadcasted_iota(jnp.int32, (NQ * M, 128), 0)
    for g in range(R // per):
        slots = jnp.zeros((8, 128), jnp.int32)
        for i in range(per):
            slots = jnp.where(group_of_lane == i, meta_in[g * per + i] & (R - 1), slots)
        target = jnp.concatenate([R * row_of_lane + slots] * (NQ * M // 8), 0)
        unpick[:, g * 128 : (g + 1) * 128] = jnp.where(target == wide_row, 1.0, 0.0).astype(BF16)

    far_a.wait_recv()
    pass_a.start()
    far_b.wait_recv()
    pass_b.start()
    code_copy.wait()
    small[3].wait()
    for copy in kv_copies:
        copy.wait()

    span = max_pages * page
    rows = GROUP * MSG
    tok = lax.broadcasted_iota(jnp.int32, (MSG, span), 1)
    f_row = lax.broadcasted_iota(jnp.int32, (rows, rows), 0)
    f_col = lax.broadcasted_iota(jnp.int32, (rows, rows), 1)
    f_key = f_col % MSG - NQ * S
    fresh_ok = (f_row // MSG == f_col // MSG) & (f_key >= 0) & (f_key <= f_row % S)
    factor = math.log2(math.e) / math.sqrt(HD)
    dims = (((1,), (1,)), ((), ()))

    def attend(g):
        first = g * GROUP
        q = q_in[pl.ds(first, GROUP)].reshape(rows, HD)
        fresh = lax.dot_general(q, q, dims, preferred_element_type=F32)
        fresh = jnp.where(fresh_ok, fresh, -jnp.inf)
        places, scores = [], []
        for u in range(GROUP):
            word = code_sm[first + u, 0]
            slot = word & (R - 1)
            length = lax.shift_right_logical(word, int(math.log2(R)))
            places.append([table_sm[p, slot] for p in range(max_pages)])
            keys = jnp.concatenate([kv[at, 0] for at in places[u]], 0)
            sc = lax.dot_general(q[u * MSG : (u + 1) * MSG], keys, dims, preferred_element_type=F32)
            scores.append(jnp.where(tok < length, sc, -jnp.inf))
        values = pltpu.roll(q.astype(F32), rows - S, 0).astype(BF16)
        for u in range(GROUP):
            mine = slice(u * MSG, (u + 1) * MSG)
            peak = jnp.maximum(
                jnp.max(scores[u], 1, keepdims=True), jnp.max(fresh[mine], 1, keepdims=True)
            )
            w_fresh = jnp.exp2((fresh[mine] - peak) * factor).astype(BF16)
            w = jnp.exp2((scores[u] - peak) * factor).astype(BF16)
            total = jnp.dot(w_fresh, values, preferred_element_type=F32)
            cached = jnp.concatenate([kv[at, 1] for at in places[u]], 0)
            total = total + jnp.dot(w, cached, preferred_element_type=F32)
            denom = jnp.sum(w.astype(F32), 1, keepdims=True) + jnp.sum(
                w_fresh.astype(F32), 1, keepdims=True
            )
            h_out[first + u] = (total / denom).astype(BF16)

    def wait_q(n):
        settle(q_in.at[n], q_recv.at[n])

    def heads_copy(n):
        return pltpu.make_async_remote_copy(
            src_ref=h_out.at[n], dst_ref=h_in.at[me], send_sem=h_send, recv_sem=h_recv.at[me],
            device_id={"replica": n}, device_id_type=MESH,
        )

    def attend_group(i, carry):
        g = mod(group - 1 - i, groups)
        for u in range(GROUP):
            n = g * GROUP + u

            @pl.when(n != me)
            def _():
                wait_q(n)

        attend(g)
        for u in range(GROUP):
            n = g * GROUP + u

            @pl.when(n != me)
            def _():
                heads_copy(n).start()

        return carry

    lax.fori_loop(0, groups, attend_group, 0, unroll=4)
    h_in[me] = h_out[me]
    share_near(0)
    share_near(1)
    to_mate[0].start()
    to_mate[1].start()
    def collect(i, carry):
        g = mod(group + 1 + i, groups)
        for u in range(GROUP):
            n = g * GROUP + u

            @pl.when(n != me)
            def _():
                settle(h_in.at[n], h_recv.at[n])

        flat = h_in[pl.ds(g * GROUP, GROUP)].reshape(GROUP * MSG, HD)
        cols = pl.ds(pl.multiple_of(g * 128, 128), 128)
        rows = jnp.dot(unpick[:, cols], flat, preferred_element_type=F32)
        by_head[...] += rows
        return carry

    by_head[...] = jnp.zeros_like(by_head)
    lax.fori_loop(0, groups, collect, 0)
    for h in range(NQ):
        heads[tx, :, h * HD : (h + 1) * HD] = by_head[h * M : (h + 1) * M].astype(BF16)

    def push(ref, i, other):
        copy = pltpu.make_async_remote_copy(
            src_ref=ref, dst_ref=ref, send_sem=x_send.at[i], recv_sem=x_recv.at[i],
            device_id={"tensor": other}, device_id_type=MESH,
        )
        copy.start()
        return copy

    low, high = pl.ds(0, half), pl.ds(half, half)
    g0 = push(heads.at[tx, low], 0, right)
    g1 = push(heads.at[tx, high], 1, left)
    g2 = push(heads.at[tx, high], 2, right)
    g3 = push(heads.at[tx, low], 3, left)
    pass_a.wait_recv()
    pass_b.wait_recv()
    to_mate[2].start()
    for e in range(4):
        spread[2][e].start()

    def term(owner, cols):
        rows = pl.ds(pl.multiple_of(owner * KR, 16), KR)
        return jnp.dot(heads[owner], wf[rows, cols], preferred_element_type=F32)

    every = slice(0, DC)
    for j in (0, 1):
        for e in range(4):
            spread[j][e].wait_recv()
        rest_to_mate[j].start()
    wo_copy.wait()
    total[...] = term(tx, every)
    g0.wait_recv()
    g4 = push(heads.at[left, low], 4, right)
    g1.wait_recv()
    g5 = push(heads.at[right, high], 5, left)
    for e in range(4):
        spread[2][e].wait_recv()
    rest_to_mate[2].start()
    g2.wait_recv()
    to_mate[0].wait_recv()
    rest_to_mate[0].wait_recv()
    total[...] += term(left, every)
    g3.wait_recv()
    to_mate[1].wait_recv()
    rest_to_mate[1].wait_recv()
    total[...] += term(right, every)
    to_mate[2].wait_recv()
    rest_to_mate[2].wait_recv()
    g4.wait_recv()
    g5.wait_recv()

    wide = DC // SUBS

    def cols_of(owner, b):
        return pl.ds(pl.multiple_of(owner * DC + b * wide, 128), wide)

    done = [g0, g1, g2, g3, g4, g5]
    first_r, first_l, second = [], [], []
    for b in range(SUBS):
        part = slice(b * wide, (b + 1) * wide)
        mine = cols_of(tx, b)
        out_ref[:, mine] = (total[:, part] + term(opposite, part)).astype(BF16)
        i = 6 + 6 * b
        first_r.append(push(out_ref.at[low, mine], i, right))
        first_l.append(push(out_ref.at[high, mine], i + 1, left))
        second.append(push(out_ref.at[high, mine], i + 2, right))
        second.append(push(out_ref.at[low, mine], i + 3, left))
    for b in range(SUBS):
        i = 6 + 6 * b
        first_r[b].wait_recv()
        second.append(push(out_ref.at[low, cols_of(left, b)], i + 4, right))
        first_l[b].wait_recv()
        second.append(push(out_ref.at[high, cols_of(right, b)], i + 5, left))
    for copy in second:
        copy.wait_recv()
    for copy in done + first_r + first_l + second:
        copy.wait_send()
    for copy in [far_a, far_b, pass_a, pass_b] + near_a + near_b + sum(spread, []) + to_mate + rest_to_mate:
        copy.wait_send()
    some = pl.ds(0, R - 1)
    settle(meta_out.at[some], meta_send)
    settle(q_out.at[some], q_send)
    settle(h_out.at[some], h_send)


def shards(
    replicas, tensors, hidden_in, norm_gain, w_query, w_key, w_value, w_out, kv_pages, lengths, page_table, destination
):
    S, R, D = hidden_in.shape
    T = tensors
    NQ = w_query.shape[1] // HD
    NH = NQ + 2
    M = S * R
    KC = min(1024, D // 2)
    DC = D // T
    pages, _, page, _ = kv_pages.shape
    any_spec = pl.BlockSpec(memory_space=pl.ANY)
    smem = pl.BlockSpec(memory_space=pltpu.SMEM)
    dma = pltpu.SemaphoreType.DMA
    out = pl.pallas_call(
        functools.partial(kernel, (R, T, S, NQ, D, KC)),
        out_shape=pltpu.VMEM((M, D), BF16),
        in_specs=[any_spec, any_spec, any_spec] + [any_spec] * 7,
        out_specs=pl.BlockSpec(memory_space=pltpu.VMEM),
        scratch_shapes=[
            pltpu.SMEM((R,), jnp.int32),
            pltpu.SMEM((R,), jnp.int32),
            pltpu.SMEM((pages // R, R), jnp.int32),
            pltpu.VMEM((1, D), F32),
            dma((4,)),
            pltpu.VMEM((M, D), BF16),
            pltpu.VMEM((D, NQ * HD), BF16),
            pltpu.VMEM((D, HD), BF16),
            pltpu.VMEM((D, HD), BF16),
            pltpu.VMEM(kv_pages.shape, BF16),
            pltpu.VMEM((T * w_out.shape[0], DC), BF16),
            pltpu.VMEM((2, w_out.shape[0] // 4, DC // 2), BF16),
            pltpu.VMEM((M, NH * HD), F32),
            pltpu.VMEM((R, 128), jnp.int32),
            pltpu.SMEM((R, 128), jnp.int32),
            pltpu.VMEM((R, 8, 128), jnp.int32),
            pltpu.VMEM((R, 8, 128), jnp.int32),
            pltpu.VMEM((NQ * M, R * MSG), BF16),
            pltpu.VMEM((NQ * M, HD), F32),
            pltpu.VMEM((NH * M, HD), BF16),
            pltpu.VMEM((R, MSG, HD), BF16),
            pltpu.VMEM((R, MSG, HD), BF16),
            pltpu.VMEM((R, MSG, HD), BF16),
            pltpu.VMEM((R, MSG, HD), BF16),
            pltpu.VMEM((T, M, NQ * HD), BF16),
            pltpu.VMEM((M, DC), F32),
            dma, dma((D // KC, 3)), dma((4,)), dma, dma,
            dma, dma, dma, dma((R,)), dma, dma((R,)), dma((6 + 6 * SUBS,)), dma((6 + 6 * SUBS,)), dma((26,)), dma((26,)),
        ],
        compiler_params=pltpu.CompilerParams(
            collective_id=0, has_side_effects=True, vmem_limit_bytes=58 * 1024 * 1024
        ),
        name="decode_attention",
    )(
        destination, lengths, page_table.T, norm_gain.reshape(1, D), hidden_in.reshape(M, D),
        w_query, w_key, w_value, w_out, kv_pages,
    )
    return out.reshape(S, R, D)


def solution(mesh):
    in_specs = (
        P(None, "replica", None),
        P(),
        P(None, "tensor"),
        P(None, "tensor"),
        P(None, "tensor"),
        P("tensor", None),
        P("replica", None, None, "tensor"),
        P("replica"),
        P("replica", None),
        P("replica"),
    )
    body = functools.partial(shards, mesh.shape["replica"], mesh.shape["tensor"])
    return jax.shard_map(
        body, mesh=mesh, in_specs=in_specs, out_specs=P(None, "replica", None), check_vma=False
    )
```

```python
import functools
import math

import jax
import jax.numpy as jnp
from jax import lax
from jax.experimental import pallas as pl
from jax.experimental.pallas import tpu as pltpu
from jax.sharding import PartitionSpec as P

HD = 128
GROUP = 4
MSG = 32
ROPE_BASE = 1000000.0
EPSILON = 1e-06
SUBS = 2
CHIPS_Z = 4
MESH = pl.DeviceIdType.MESH
F32 = jnp.float32
BF16 = jnp.bfloat16


def mod(value, size):
    return lax.rem(value + 2 * size, size)


def settle(ref, sem):
    pltpu.make_async_copy(ref, ref, sem).wait()


def kernel(
    sizes,
    dest_hbm, len_hbm, table_hbm, gain_hbm, hid_hbm, wq_hbm, wk_hbm, wv_hbm, wo_hbm, kv_hbm,
    out_ref,
    dest_sm, len_sm, table_sm, gain_ref, small_sem,
    hid, wq, wk, wv, kv, wf, relay, acc, code, code_sm, meta_out, meta_in, unpick, by_head, stack,
    q_out, q_in, h_out, h_in, heads, total,
    hid_sem, w_sem, kv_sem, wo_sem, code_sem,
    meta_send, meta_recv, q_send, q_recv, h_send, h_recv, x_send, x_recv, f_send, f_recv,
):
    R, T, S, NQ, D, KC = sizes
    M = S * R
    NH = NQ + 2
    me = lax.axis_index("replica")
    tx = lax.axis_index("tensor")
    chunks = D // KC
    group = me // GROUP
    groups = R // GROUP
    DC = D // T
    half = M // 2
    pages = kv.shape[0]
    max_pages = pages // R
    page = kv.shape[2]
    KR = wo_hbm.shape[0]
    HB, QB = KR // 2, KR // 8
    HC = DC // 2
    core = me % 2
    mate = me + 1 - 2 * core
    chip = me // 2
    z, y = chip % CHIPS_Z, chip // CHIPS_Z
    chips_y = R // (2 * CHIPS_Z)
    parity = (y + z) % 2
    opposite = mod(tx + 2, T)

    def at(yy, zz):
        return (mod(yy, chips_y) * CHIPS_Z + mod(zz, CHIPS_Z)) * 2 + core

    around = (at(y + 1, z), at(y - 1, z), at(y, z + 1), at(y, z - 1))

    def rows_at(owner, first, size):
        return pl.ds(pl.multiple_of(owner * KR + first, 16), size)

    half_cols = pl.ds(pl.multiple_of(core * HC, 128), HC)

    def own_rows(target, first, size):
        cols = pl.ds(pl.multiple_of(target * DC + core * HC, 128), HC)
        return wo_hbm.at[pl.ds(pl.multiple_of(first, 16), size), cols]

    def weight_piece(src, dst, i, other):
        return pltpu.make_async_remote_copy(
            src_ref=src, dst_ref=dst, send_sem=f_send.at[i], recv_sem=f_recv.at[i],
            device_id=other, device_id_type=MESH,
        )

    def held(owner, first, size):
        return wf.at[rows_at(owner, first, size), half_cols]

    def same_place(owner, first, size, i, other):
        return weight_piece(held(owner, first, size), held(owner, first, size), i, {"replica": other})

    right = mod(tx + 1, T)
    left = mod(tx - 1, T)
    fetched, missing = parity * HB, (1 - parity) * HB
    QH2 = HB // 2
    far_a = weight_piece(own_rows(opposite, fetched, QH2), relay.at[0], 0, {"tensor": right})
    far_b = weight_piece(own_rows(opposite, fetched + QH2, QH2), relay.at[1], 1, {"tensor": left})
    near_a, near_b = (
        [
            weight_piece(
                own_rows(target, fetched + p * QH2, QH2), held(tx, fetched + p * QH2, QH2), 2 + 2 * p + i,
                {"tensor": target},
            )
            for p in range(2)
        ]
        for i, target in enumerate((right, left))
    )
    pass_a = weight_piece(relay.at[0], held(left, fetched, QH2), 24, {"tensor": right})
    pass_b = weight_piece(relay.at[1], held(right, fetched + QH2, QH2), 25, {"tensor": left})
    owners = (left, right, opposite)
    spread = [
        [same_place(owner, fetched + e * QB, QB, 6 + 4 * j + e, around[e]) for e in range(4)]
        for j, owner in enumerate(owners)
    ]
    to_mate = [same_place(owner, fetched, HB, 18 + j, mate) for j, owner in enumerate(owners)]
    rest_to_mate = [same_place(owner, missing, HB, 21 + j, mate) for j, owner in enumerate(owners)]

    def weight_copies(c):
        rows = pl.ds(pl.multiple_of(c * KC, KC), KC)
        return (
            pltpu.make_async_copy(wq_hbm.at[rows], wq.at[rows], w_sem.at[c, 0]),
            pltpu.make_async_copy(wk_hbm.at[rows], wk.at[rows], w_sem.at[c, 1]),
            pltpu.make_async_copy(wv_hbm.at[rows], wv.at[rows], w_sem.at[c, 2]),
        )

    small = [
        pltpu.make_async_copy(src, dst, small_sem.at[i])
        for i, (src, dst) in enumerate(
            ((dest_hbm, dest_sm), (len_hbm, len_sm), (gain_hbm, gain_ref), (table_hbm, table_sm))
        )
    ]
    for copy in small:
        copy.start()
    hid_copy = pltpu.make_async_copy(hid_hbm, hid, hid_sem)
    hid_copy.start()
    def load(c):
        if c < chunks:
            for copy in weight_copies(c):
                copy.start()

    barrier = pltpu.get_barrier_semaphore()

    def far_first(k):
        return R // 2 + (1 - 2 * (k % 2)) * ((k + 1) // 2)

    def greet(k, carry):
        n = mod(me + far_first(k), R)
        pl.semaphore_signal(barrier, inc=1, device_id={"replica": n}, device_id_type=MESH)
        return carry

    lax.fori_loop(0, R - 1, greet, 0, unroll=True)
    for other in (right, left):
        pl.semaphore_signal(barrier, inc=1, device_id={"tensor": other}, device_id_type=MESH)

    load(0)
    load(1)

    small[0].wait()
    small[1].wait()
    numbers = lax.broadcasted_iota(jnp.int32, (R, 128), 0)
    codes = jnp.zeros((R, 128), jnp.int32)
    for b in range(R):
        codes = jnp.where(numbers == dest_sm[b], len_sm[b] * R + b, codes)
    code[...] = codes
    code_copy = pltpu.make_async_copy(code, code_sm, code_sem)
    code_copy.start()
    for n in range(R):
        meta_out[n] = jnp.broadcast_to(codes[n : n + 1], (8, 128))

    pl.semaphore_wait(barrier, R - 1 + 2)

    def to_all(make):
        def send(k, carry):
            n = mod(group * GROUP + GROUP + k, R)

            @pl.when(n != me)
            def _():
                make(n).start()

            return carry

        lax.fori_loop(0, R, send, 0)

    def meta_copy(n):
        return pltpu.make_async_remote_copy(
            src_ref=meta_out.at[n], dst_ref=meta_in.at[me], send_sem=meta_send, recv_sem=meta_recv,
            device_id={"replica": n}, device_id_type=MESH,
        )

    def send_meta(k, carry):
        meta_copy(mod(me + far_first(k), R)).start()
        return carry

    lax.fori_loop(0, R - 1, send_meta, 0, unroll=True)
    far_a.start()
    far_b.start()

    hid_copy.wait()
    small[2].wait()
    load(2)
    squares = jnp.zeros((M, 128), F32)
    for c in range(D // 128):
        wide = hid[:, c * 128 : (c + 1) * 128].astype(F32)
        squares = squares + wide * wide
    load(3)
    scale = lax.rsqrt(jnp.sum(squares, 1, keepdims=True) * (1.0 / D) + EPSILON)

    for c in range(0, D, 512):
        cols = slice(c, c + 512)
        hid[:, cols] = (hid[:, cols].astype(F32) * scale * gain_ref[:, cols]).astype(BF16)

    for c in range(4, chunks):
        load(c)
    kv_copies = []
    step = pages // 4
    for c in range(4):
        rows = pl.ds(c * step, step)
        kv_copies.append(pltpu.make_async_copy(kv_hbm.at[rows], kv.at[rows], kv_sem.at[c]))

    def project(c):
        for copy in weight_copies(c):
            copy.wait()
        if c + 1 == chunks:
            for copy in kv_copies:
                copy.start()
        cols = slice(c * KC, (c + 1) * KC)
        weights = jnp.concatenate([wq[cols], wk[cols], wv[cols]], 1)
        term = jnp.dot(hid[:, cols], weights, preferred_element_type=F32)
        acc[...] = term if c == 0 else acc[...] + term

    for c in range(chunks):
        project(c)
        if c == chunks // 2:
            near_a[0].start()
            near_b[0].start()

    def share_near(p):
        near_a[p].wait_recv()
        near_b[p].wait_recv()
        for j in (0, 1):
            for e in (2 * p, 2 * p + 1):
                spread[j][e].start()

    near_a[1].start()
    near_b[1].start()
    settle(meta_in.at[pl.ds(0, R - 1)], meta_recv)
    meta_in[me] = meta_out[me]

    slot_rows = lax.broadcasted_iota(jnp.int32, (R, 128), 0)
    lens = jnp.zeros((R, 128), jnp.int32)
    for o in range(R):
        tile = meta_in[o]
        slot_wide = jnp.concatenate([tile & (R - 1)] * (R // 8), 0)
        len_wide = jnp.concatenate([lax.shift_right_logical(tile, int(math.log2(R)))] * (R // 8), 0)
        lens = jnp.where(slot_rows == slot_wide, len_wide, lens)

    freq_lane = lax.broadcasted_iota(jnp.int32, (8, 128), 1) % (HD // 2)
    freq = jnp.exp(freq_lane.astype(F32) * (-2.0 / HD * math.log(ROPE_BASE)))
    angle = lens.astype(F32) * jnp.concatenate([freq] * (R // 8), 0)
    cos_len, sin_len = jnp.cos(angle), jnp.sin(angle)
    sign = jnp.where(lax.broadcasted_iota(jnp.int32, (R, 128), 1) < HD // 2, -1.0, 1.0)
    cosines, sines = [], []
    for s in range(S):
        if s == 0:
            cosines.append(cos_len)
            sines.append(sin_len * sign)
            continue
        cos_s = jnp.concatenate([jnp.cos(freq * float(s))] * (R // 8), 0)
        sin_s = jnp.concatenate([jnp.sin(freq * float(s))] * (R // 8), 0)
        cosines.append(cos_len * cos_s - sin_len * sin_s)
        sines.append((sin_len * cos_s + cos_len * sin_s) * sign)
    cosine = jnp.concatenate(cosines, 0)
    sine = jnp.concatenate(sines, 0)


    for h in range(NH):
        vec = acc[:, h * HD : (h + 1) * HD]
        if h <= NQ:
            vec = vec * cosine + pltpu.roll(vec, HD // 2, 1) * sine
        stack[h * M : (h + 1) * M, :] = vec.astype(BF16)

    def q_copy(o):
        return pltpu.make_async_remote_copy(
            src_ref=q_out.at[o], dst_ref=q_in.at[me], send_sem=q_send, recv_sem=q_recv.at[me],
            device_id={"replica": o}, device_id_type=MESH,
        )

    msg_row = lax.broadcasted_iota(jnp.int32, (MSG, 128), 0)
    lane = lax.broadcasted_iota(jnp.int32, (MSG, 128), 1)

    def send_group(i, carry):
        first = mod(group + 1 + i, groups) * GROUP
        blocks = []
        for u in range(GROUP):
            slot = meta_in[first + u] & (R - 1)
            target = R * msg_row + jnp.concatenate([slot] * (MSG // 8), 0)
            parts = []
            for c in range(0, NH * M, 128):
                hit = jnp.where(target == lane + c, 1.0, 0.0).astype(BF16)
                parts.append(hit[:, : min(128, NH * M - c)])
            blocks.append(jnp.concatenate(parts, 1))
        pick = jnp.concatenate(blocks, 0)
        rows = jnp.dot(pick, stack[...], preferred_element_type=F32)
        q_out[pl.ds(first, GROUP)] = rows.astype(BF16).reshape(GROUP, MSG, HD)
        for u in range(GROUP):

            @pl.when(first + u != me)
            def _():
                q_copy(first + u).start()

        return carry

    lax.fori_loop(0, groups, send_group, 0, unroll=2)
    q_in[me] = q_out[me]
    wo_copy = pltpu.make_async_copy(
        wo_hbm.at[:, pl.ds(pl.multiple_of(tx * DC, 128), DC)], wf.at[rows_at(tx, 0, KR)], wo_sem
    )
    wo_copy.start()
    per = 128 // MSG
    group_of_lane = lax.broadcasted_iota(jnp.int32, (8, 128), 1) // MSG
    row_of_lane = lax.broadcasted_iota(jnp.int32, (8, 128), 1) % MSG
    wide_row = lax.broadcasted_iota(jnp.int32, (NQ * M, 128), 0)
    for g in range(R // per):
        slots = jnp.zeros((8, 128), jnp.int32)
        for i in range(per):
            slots = jnp.where(group_of_lane == i, meta_in[g * per + i] & (R - 1), slots)
        target = jnp.concatenate([R * row_of_lane + slots] * (NQ * M // 8), 0)
        unpick[:, g * 128 : (g + 1) * 128] = jnp.where(target == wide_row, 1.0, 0.0).astype(BF16)

    far_a.wait_recv()
    pass_a.start()
    far_b.wait_recv()
    pass_b.start()
    code_copy.wait()
    small[3].wait()
    for copy in kv_copies:
        copy.wait()

    span = max_pages * page
    rows = GROUP * MSG
    tok = lax.broadcasted_iota(jnp.int32, (MSG, span), 1)
    f_row = lax.broadcasted_iota(jnp.int32, (rows, rows), 0)
    f_col = lax.broadcasted_iota(jnp.int32, (rows, rows), 1)
    f_key = f_col % MSG - NQ * S
    fresh_ok = (f_row // MSG == f_col // MSG) & (f_key >= 0) & (f_key <= f_row % S)
    factor = math.log2(math.e) / math.sqrt(HD)
    dims = (((1,), (1,)), ((), ()))

    def attend(g):
        first = g * GROUP
        q = q_in[pl.ds(first, GROUP)].reshape(rows, HD)
        fresh = lax.dot_general(q, q, dims, preferred_element_type=F32)
        fresh = jnp.where(fresh_ok, fresh, -jnp.inf)
        places, scores = [], []
        for u in range(GROUP):
            word = code_sm[first + u, 0]
            slot = word & (R - 1)
            length = lax.shift_right_logical(word, int(math.log2(R)))
            places.append([table_sm[p, slot] for p in range(max_pages)])
            keys = jnp.concatenate([kv[at, 0] for at in places[u]], 0)
            sc = lax.dot_general(q[u * MSG : (u + 1) * MSG], keys, dims, preferred_element_type=F32)
            scores.append(jnp.where(tok < length, sc, -jnp.inf))
        values = pltpu.roll(q.astype(F32), rows - S, 0).astype(BF16)
        for u in range(GROUP):
            mine = slice(u * MSG, (u + 1) * MSG)
            peak = jnp.maximum(
                jnp.max(scores[u], 1, keepdims=True), jnp.max(fresh[mine], 1, keepdims=True)
            )
            w_fresh = jnp.exp2((fresh[mine] - peak) * factor).astype(BF16)
            w = jnp.exp2((scores[u] - peak) * factor).astype(BF16)
            total = jnp.dot(w_fresh, values, preferred_element_type=F32)
            cached = jnp.concatenate([kv[at, 1] for at in places[u]], 0)
            total = total + jnp.dot(w, cached, preferred_element_type=F32)
            denom = jnp.sum(w.astype(F32), 1, keepdims=True) + jnp.sum(
                w_fresh.astype(F32), 1, keepdims=True
            )
            h_out[first + u] = (total / denom).astype(BF16)

    def wait_q(n):
        settle(q_in.at[n], q_recv.at[n])

    def heads_copy(n):
        return pltpu.make_async_remote_copy(
            src_ref=h_out.at[n], dst_ref=h_in.at[me], send_sem=h_send, recv_sem=h_recv.at[me],
            device_id={"replica": n}, device_id_type=MESH,
        )

    def attend_group(i, carry):
        g = mod(group - 1 - i, groups)
        for u in range(GROUP):
            n = g * GROUP + u

            @pl.when(n != me)
            def _():
                wait_q(n)

        attend(g)
        for u in range(GROUP):
            n = g * GROUP + u

            @pl.when(n != me)
            def _():
                heads_copy(n).start()

        return carry

    lax.fori_loop(0, groups, attend_group, 0, unroll=4)
    h_in[me] = h_out[me]
    share_near(0)
    share_near(1)
    to_mate[0].start()
    to_mate[1].start()
    def collect(i, carry):
        g = mod(group + 1 + i, groups)
        for u in range(GROUP):
            n = g * GROUP + u

            @pl.when(n != me)
            def _():
                settle(h_in.at[n], h_recv.at[n])

        flat = h_in[pl.ds(g * GROUP, GROUP)].reshape(GROUP * MSG, HD)
        cols = pl.ds(pl.multiple_of(g * 128, 128), 128)
        rows = jnp.dot(unpick[:, cols], flat, preferred_element_type=F32)
        by_head[...] += rows
        return carry

    by_head[...] = jnp.zeros_like(by_head)
    lax.fori_loop(0, groups, collect, 0)
    for h in range(NQ):
        heads[tx, :, h * HD : (h + 1) * HD] = by_head[h * M : (h + 1) * M].astype(BF16)

    def push(ref, i, other):
        copy = pltpu.make_async_remote_copy(
            src_ref=ref, dst_ref=ref, send_sem=x_send.at[i], recv_sem=x_recv.at[i],
            device_id={"tensor": other}, device_id_type=MESH,
        )
        copy.start()
        return copy

    low, high = pl.ds(0, half), pl.ds(half, half)
    g0 = push(heads.at[tx, low], 0, right)
    g1 = push(heads.at[tx, high], 1, left)
    g2 = push(heads.at[tx, high], 2, right)
    g3 = push(heads.at[tx, low], 3, left)
    pass_a.wait_recv()
    pass_b.wait_recv()
    to_mate[2].start()
    for e in range(4):
        spread[2][e].start()

    def term(owner, cols):
        rows = pl.ds(pl.multiple_of(owner * KR, 16), KR)
        return jnp.dot(heads[owner], wf[rows, cols], preferred_element_type=F32)

    every = slice(0, DC)
    for j in (0, 1):
        for e in range(4):
            spread[j][e].wait_recv()
        rest_to_mate[j].start()
    wo_copy.wait()
    total[...] = term(tx, every)
    g0.wait_recv()
    g4 = push(heads.at[left, low], 4, right)
    g1.wait_recv()
    g5 = push(heads.at[right, high], 5, left)
    for e in range(4):
        spread[2][e].wait_recv()
    rest_to_mate[2].start()
    g2.wait_recv()
    to_mate[0].wait_recv()
    rest_to_mate[0].wait_recv()
    total[...] += term(left, every)
    g3.wait_recv()
    to_mate[1].wait_recv()
    rest_to_mate[1].wait_recv()
    total[...] += term(right, every)
    g4.wait_recv()
    g5.wait_recv()

    wide = DC // SUBS

    def cols_of(owner, b):
        own = core if b == 0 else 1 - core
        return pl.ds(pl.multiple_of(owner * DC + own * wide, 128), wide)

    done = [g0, g1, g2, g3, g4, g5]
    first_r, first_l, second = [], [], []
    for b in range(SUBS):
        part = cols_of(0, b)
        if b == 1:
            to_mate[2].wait_recv()
            rest_to_mate[2].wait_recv()
        mine = cols_of(tx, b)
        out_ref[:, mine] = (total[:, part] + term(opposite, part)).astype(BF16)
        i = 6 + 6 * b
        first_r.append(push(out_ref.at[low, mine], i, right))
        first_l.append(push(out_ref.at[high, mine], i + 1, left))
        second.append(push(out_ref.at[high, mine], i + 2, right))
        second.append(push(out_ref.at[low, mine], i + 3, left))
    for b in range(SUBS):
        i = 6 + 6 * b
        first_r[b].wait_recv()
        second.append(push(out_ref.at[low, cols_of(left, b)], i + 4, right))
        first_l[b].wait_recv()
        second.append(push(out_ref.at[high, cols_of(right, b)], i + 5, left))
    for copy in second:
        copy.wait_recv()
    for copy in done + first_r + first_l + second:
        copy.wait_send()
    for copy in [far_a, far_b, pass_a, pass_b] + near_a + near_b + sum(spread, []) + to_mate + rest_to_mate:
        copy.wait_send()
    some = pl.ds(0, R - 1)
    settle(meta_out.at[some], meta_send)
    settle(q_out.at[some], q_send)
    settle(h_out.at[some], h_send)


def shards(
    replicas, tensors, hidden_in, norm_gain, w_query, w_key, w_value, w_out, kv_pages, lengths, page_table, destination
):
    S, R, D = hidden_in.shape
    T = tensors
    NQ = w_query.shape[1] // HD
    NH = NQ + 2
    M = S * R
    KC = min(1024, D // 2)
    DC = D // T
    pages, _, page, _ = kv_pages.shape
    any_spec = pl.BlockSpec(memory_space=pl.ANY)
    smem = pl.BlockSpec(memory_space=pltpu.SMEM)
    dma = pltpu.SemaphoreType.DMA
    out = pl.pallas_call(
        functools.partial(kernel, (R, T, S, NQ, D, KC)),
        out_shape=pltpu.VMEM((M, D), BF16),
        in_specs=[any_spec, any_spec, any_spec] + [any_spec] * 7,
        out_specs=pl.BlockSpec(memory_space=pltpu.VMEM),
        scratch_shapes=[
            pltpu.SMEM((R,), jnp.int32),
            pltpu.SMEM((R,), jnp.int32),
            pltpu.SMEM((pages // R, R), jnp.int32),
            pltpu.VMEM((1, D), F32),
            dma((4,)),
            pltpu.VMEM((M, D), BF16),
            pltpu.VMEM((D, NQ * HD), BF16),
            pltpu.VMEM((D, HD), BF16),
            pltpu.VMEM((D, HD), BF16),
            pltpu.VMEM(kv_pages.shape, BF16),
            pltpu.VMEM((T * w_out.shape[0], DC), BF16),
            pltpu.VMEM((2, w_out.shape[0] // 4, DC // 2), BF16),
            pltpu.VMEM((M, NH * HD), F32),
            pltpu.VMEM((R, 128), jnp.int32),
            pltpu.SMEM((R, 128), jnp.int32),
            pltpu.VMEM((R, 8, 128), jnp.int32),
            pltpu.VMEM((R, 8, 128), jnp.int32),
            pltpu.VMEM((NQ * M, R * MSG), BF16),
            pltpu.VMEM((NQ * M, HD), F32),
            pltpu.VMEM((NH * M, HD), BF16),
            pltpu.VMEM((R, MSG, HD), BF16),
            pltpu.VMEM((R, MSG, HD), BF16),
            pltpu.VMEM((R, MSG, HD), BF16),
            pltpu.VMEM((R, MSG, HD), BF16),
            pltpu.VMEM((T, M, NQ * HD), BF16),
            pltpu.VMEM((M, DC), F32),
            dma, dma((D // KC, 3)), dma((4,)), dma, dma,
            dma, dma, dma, dma((R,)), dma, dma((R,)), dma((6 + 6 * SUBS,)), dma((6 + 6 * SUBS,)), dma((26,)), dma((26,)),
        ],
        compiler_params=pltpu.CompilerParams(
            collective_id=0, has_side_effects=True, vmem_limit_bytes=58 * 1024 * 1024
        ),
        name="decode_attention",
    )(
        destination, lengths, page_table.T, norm_gain.reshape(1, D), hidden_in.reshape(M, D),
        w_query, w_key, w_value, w_out, kv_pages,
    )
    return out.reshape(S, R, D)


def solution(mesh):
    in_specs = (
        P(None, "replica", None),
        P(),
        P(None, "tensor"),
        P(None, "tensor"),
        P(None, "tensor"),
        P("tensor", None),
        P("replica", None, None, "tensor"),
        P("replica"),
        P("replica", None),
        P("replica"),
    )
    body = functools.partial(shards, mesh.shape["replica"], mesh.shape["tensor"])
    return jax.shard_map(
        body, mesh=mesh, in_specs=in_specs, out_specs=P(None, "replica", None), check_vma=False
    )
```
